32 devices in a mesh: seq: 8 (over z, x), batch: 4 (over y, core).
Axes of the slice: x: 2, y: 2, z: 4, core: 2. Of those that a mesh axis runs over, the one named last changes fastest.
Arguments:
- tokens: float32 [4, 1024, 2048], P('batch', 'seq'), may hold values from -6 to 6
- language: int32 [4], P('batch'), may hold values from 0 to 6
- language_weight: float32 [7], replicated, may hold values from 0.5 to 2
- output_grad: float32 [4, 1024, 2048], P('batch', 'seq'), may hold values from -6 to 6
- attention_gain: bfloat16 [2048], P(('seq', 'batch')), may hold values from 0.5 to 1.5
- attention_shift: bfloat16 [2048], P(('seq', 'batch')), may hold values from -4 to 4
- joint_weight: bfloat16 [2048, 6144], P(('seq', 'batch')), may hold values from -0.1875 to 0.1875
- joint_bias: bfloat16 [6144], P(('seq', 'batch')), may hold values from -4 to 4
- output_weight: bfloat16 [2048, 2048], P(('seq', 'batch')), may hold values from -0.75 to 0.75
- feedfwd_gain: bfloat16 [2048], P(('seq', 'batch')), may hold values from 0.5 to 1.5
- feedfwd_shift: bfloat16 [2048], P(('seq', 'batch')), may hold values from -4 to 4
- gate_weight: bfloat16 [2048, 5632], P(('seq', 'batch')), may hold values from -0.125 to 0.125
- up_weight: bfloat16 [2048, 5632], P(('seq', 'batch')), may hold values from -0.125 to 0.125
- down_weight: bfloat16 [2048, 5632], P(('seq', 'batch')), may hold values from -0.15625 to 0.15625
Outputs:
- result: float32 [4, 1024, 2048], P('batch', 'seq')
- grad_tokens: float32 [4, 1024, 2048], P('batch', 'seq')
- grad_attgain: float32 [2048], P(('seq', 'batch'))
- grad_attshift: float32 [2048], P(('seq', 'batch'))
- grad_joint: float32 [2048, 6144], P(('seq', 'batch'))
- grad_jointbias: float32 [6144], P(('seq', 'batch'))
- grad_output: float32 [2048, 2048], P(('seq', 'batch'))
- grad_ffgain: float32 [2048], P(('seq', 'batch'))
- grad_ffshift: float32 [2048], P(('seq', 'batch'))
- grad_gate: float32 [2048, 5632], P(('seq', 'batch'))
- grad_up: float32 [2048, 5632], P(('seq', 'batch'))
- grad_down: float32 [2048, 5632], P(('seq', 'batch'))
The draws below stay inside these ranges and needn't reach their ends.
All inputs are finite; a program needn't handle non-finite values.
Results may differ from the reference program's by a relative error of at most 0.025.
Values may be sent and summed in bfloat16 or wider, within the bound.
No kernel may reach another device: no remote copies, remote signals or barrier semaphores. Data moves between devices by JAX's collectives and lax.ppermute only.
A program may use at most 448 MiB of HBM per device.

```python
import math
import jax
import jax.numpy as jnp
from jax import lax

D = 2048
FF = 5632
HEADS = 32
HEAD_DIM = 64
ROT_DIMS = 16
LANGS = 7
SEQ_LEN = 1024
ROWS = 4


def set_ends(values, key, least, high):
    shape = values.shape
    index_at = [jax.random.randint(jax.random.fold_in(key, axis), (), 0, shape[axis]) for axis in range(len(shape))]
    values = values.at[tuple(index_at)].set(least)
    longest = shape.index(max(shape))
    index_at[longest] = (index_at[longest] + 1) % shape[longest]
    return values.at[tuple(index_at)].set(high)


def levels(key, extent, pieces, low, largest):
    level = 1.0
    for axis_at, parts in pieces:
        steps = jax.random.uniform(jax.random.fold_in(jax.random.fold_in(key, 6), axis_at), (parts,), jnp.float32, low / len(pieces), largest / len(pieces))
        level = level * jnp.repeat(jnp.exp(steps), extent[axis_at] // parts).reshape((-1,) + (1,) * (len(extent) - 1 - axis_at))
    return level


def scatter_about(rng, dims, width, limit, split=(), kind=jnp.bfloat16):
    loudness = levels(rng, dims, split, -0.22, 0.18) if split else 1.0
    array = jax.random.normal(rng, dims, jnp.float32) * width * loudness
    return jnp.minimum(jnp.maximum(array, -limit), limit).astype(kind)


def setup_inputs(seed: int = 0) -> dict:
    key_list = jax.random.split(jax.random.key(seed), 15)
    return {
        "tokens": scatter_about(key_list[0], (ROWS, SEQ_LEN, D), 1.0, 6.0, ((0, 4), (1, 8)), jnp.float32),
        "language": set_ends(jax.random.randint(key_list[1], (ROWS,), 0, LANGS), jax.random.fold_in(key_list[1], 1), 0, LANGS - 1).astype(jnp.int32),
        "language_weight": jnp.clip(jnp.exp(jax.random.uniform(key_list[2], (LANGS,), jnp.float32, math.log(0.5), math.log(2.0))), 0.5, 2.0),
        "output_grad": scatter_about(key_list[3], (ROWS, SEQ_LEN, D), 1.0, 6.0, ((0, 4), (1, 8)), jnp.float32),
        "attention_gain": jnp.clip(1.0 + 0.1 * jax.random.normal(key_list[4], (D,), jnp.float32), 0.5, 1.5).astype(jnp.bfloat16),
        "attention_shift": scatter_about(key_list[5], (D,), 0.3, 4.0, ((0, 32),)),
        "joint_weight": scatter_about(key_list[6], (D, 3 * D), (D // 2) ** -0.5, 0.1875, ((0, 32),)),
        "joint_bias": scatter_about(key_list[7], (3 * D,), 0.3, 4.0, ((0, 32),)),
        "output_weight": scatter_about(key_list[8], (D, D), (D // 32) ** -0.5, 0.75, ((0, 32),)),
        "feedfwd_gain": jnp.clip(1.0 + 0.1 * jax.random.normal(key_list[9], (D,), jnp.float32), 0.5, 1.5).astype(jnp.bfloat16),
        "feedfwd_shift": scatter_about(key_list[10], (D,), 0.3, 4.0, ((0, 32),)),
        "gate_weight": scatter_about(key_list[11], (D, FF), D ** -0.5, 0.125, ((0, 32),)),
        "up_weight": scatter_about(key_list[12], (D, FF), D ** -0.5, 0.125, ((0, 32),)),
        "down_weight": scatter_about(key_list[13], (D, FF), (FF // 4) ** -0.5, 0.15625, ((0, 32),)),
    }


EPSILON = 1e-05
THETA_BASE = 10000.0
NEGATIVE = -1e+30

@jax.custom_vjp
def low(v):
    return lax.optimization_barrier(v.astype(jnp.bfloat16)).astype(jnp.float32)

@jax.custom_vjp
def low_back(v):
    return v

def low_keep(v):
    return (low(v), None)

def low_pass(kept, grad):
    return (grad,)

def back_keep(v):
    return (v, None)

def back_low(kept, grad):
    return (low(grad),)
low.defvjp(low_keep, low_pass)
low_back.defvjp(back_keep, back_low)

def precise_dot(left, right):
    return jnp.dot(left, right, precision=lax.Precision.HIGHEST)

def layer_norm(values, gain_values, shift_values):
    center = values - lax.optimization_barrier(jnp.mean(values, axis=-1, keepdims=True))
    spread = lax.optimization_barrier(jnp.mean(center * center, axis=-1, keepdims=True))
    return center * lax.rsqrt(spread + EPSILON) * gain_values + shift_values

def rotary_tables(positions):
    half_rot = ROT_DIMS // 2
    frequency = THETA_BASE ** (-jnp.arange(half_rot, dtype=jnp.float32) / half_rot)
    angles = positions.astype(jnp.float32)[:, None] * frequency[None, :]
    return (jnp.cos(angles)[:, None, :], jnp.sin(angles)[:, None, :])

def rotate(values, cosine_table, sine_table):
    half_rot = ROT_DIMS // 2
    first_half = values[..., :half_rot]
    second_half = values[..., half_rot:ROT_DIMS]
    remainder = values[..., ROT_DIMS:]
    return jnp.concatenate([first_half * cosine_table - second_half * sine_table, second_half * cosine_table + first_half * sine_table, remainder], axis=-1)

def attend(queries, key_rows, value_rows):
    length = queries.shape[0]
    block_rows = math.gcd(length, 512)
    number = length // block_rows
    key_positions = jnp.arange(length, dtype=jnp.int32)
    score_scale = 1.0 / math.sqrt(HEAD_DIM)

    def one_block(element):
        query_block, offset = element
        scores = jnp.einsum('qhe,khe->hqk', query_block, key_rows, precision=lax.Precision.HIGHEST) * score_scale
        scores = low_back(scores)
        query_positions = offset + jnp.arange(block_rows, dtype=jnp.int32)
        allowed = key_positions[None, :] <= query_positions[:, None]
        scores = jnp.where(allowed[None], scores, NEGATIVE)
        probabilities = low(jax.nn.softmax(scores, axis=-1))
        return jnp.einsum('hqk,khe->qhe', probabilities, value_rows, precision=lax.Precision.HIGHEST)
    reshaped = queries.reshape(number, block_rows, HEADS, HEAD_DIM)
    offsets = (block_rows * jnp.arange(number)).astype(jnp.int32)
    outcome = lax.map(jax.checkpoint(one_block), (reshaped, offsets))
    return outcome.reshape(length, HEADS, HEAD_DIM)

def forward(values, parameters):
    att_gain, att_shift, joint_w, joint_b, out_w, ff_gain, ff_shift, gate_w, up_w, down_w = parameters
    length = values.shape[0]
    first_input = low(layer_norm(values, att_gain, att_shift))
    joint_value = low_back(precise_dot(first_input, joint_w) + joint_b)
    cosine_table, sine_table = rotary_tables(jnp.arange(length, dtype=jnp.int32))
    queries = low(rotate(joint_value[:, :D].reshape(length, HEADS, HEAD_DIM), cosine_table, sine_table))
    key_rows = low(rotate(joint_value[:, D:2 * D].reshape(length, HEADS, HEAD_DIM), cosine_table, sine_table))
    value_rows = low(joint_value[:, 2 * D:].reshape(length, HEADS, HEAD_DIM))
    mixed = low(low_back(attend(queries, key_rows, value_rows).reshape(length, D)))
    middle = values + low_back(precise_dot(mixed, out_w))
    second_input = low(layer_norm(middle, ff_gain, ff_shift))
    gate_value = low_back(precise_dot(second_input, gate_w))
    up_value = low_back(precise_dot(second_input, up_w))
    hidden = low(jax.nn.silu(gate_value) * up_value)
    return middle + low_back(precise_dot(hidden, down_w.T))

def reference(tokens, language, language_weight, output_grad, attention_gain, attention_shift, joint_weight, joint_bias, output_weight, feedfwd_gain, feedfwd_shift, gate_weight, up_weight, down_weight):
    parameters = tuple((item.astype(jnp.float32) for item in (attention_gain, attention_shift, joint_weight, joint_bias, output_weight, feedfwd_gain, feedfwd_shift, gate_weight, up_weight, down_weight)))
    chosen = language[:, None] == jnp.arange(LANGS, dtype=jnp.int32)[None, :]
    row_scale = lax.optimization_barrier(jnp.sum(jnp.where(chosen, language_weight[None, :], 0.0), axis=1))
    cotangent = output_grad * row_scale[:, None, None]
    zero_grads = tuple((jnp.zeros_like(item) for item in parameters))

    def one_row(totals, element):
        token_row, grad_row = element
        outcome, pullback = jax.vjp(forward, token_row, parameters)
        grad_in, grad_params = pullback(grad_row)
        totals = tuple((left + right for left, right in zip(totals, grad_params)))
        return (totals, (outcome, grad_in))
    totals, (result, grad_tokens) = lax.scan(one_row, zero_grads, (tokens, cotangent))
    return (result, grad_tokens, totals[0], totals[1], totals[2], totals[3], totals[4], totals[5], totals[6], totals[7], totals[8], totals[9])
```

```python
import math

import numpy as np

import jax
import jax.numpy as jnp
from jax import lax
from jax.experimental import pallas as pl
from jax.experimental.pallas import tpu as pltpu
from jax.sharding import PartitionSpec as P

HEADS = 32
HEAD_DIM = 64
ROT_DIMS = 16
LANGS = 7

EPSILON = 1e-05
THETA_BASE = 10000.0
NEGATIVE = -1e30
VMEM_BYTES = 56 * 1024 * 1024

bf16 = jnp.bfloat16
f32 = jnp.float32


def swap(value, axis, number, bit):
    return lax.ppermute(value, axis, [(i, i ^ bit) for i in range(number)])


def bits_of(number):
    return [1 << i for i in range(number.bit_length() - 1)]


def tie(*values):
    return lax.optimization_barrier(values)


def after(value, *others):
    return tie(value, *others)[0]


def exchange_near(blocks, number):
    if number != 8:
        return blocks
    mine = lax.axis_index("seq") % 2
    pairs = blocks.reshape((number // 2, 2) + blocks.shape[1:])
    got = swap(lax.dynamic_slice_in_dim(pairs, 1 - mine, 1, 1), "seq", number, 1)
    return lax.dynamic_update_slice_in_dim(pairs, got, 1 - mine, 1).reshape(blocks.shape)


def exchange_far(blocks, number):
    low = 2 if number == 8 else 1
    place = lax.axis_index("seq") // low
    out = blocks.reshape((number // low, low) + blocks.shape[1:])
    parts = [
        swap(lax.dynamic_slice_in_dim(out, place ^ k, 1, 0), "seq", number, k * low)
        for k in range(1, number // low)
    ]
    for k, part in enumerate(parts):
        out = lax.dynamic_update_slice_in_dim(out, part, place ^ (k + 1), 0)
    return out.reshape(blocks.shape)


def gather_far(value, number):
    held = [(0, value)]
    for bit in reversed(bits_of(number)[1:]):
        held = held + [(k ^ bit, swap(v, "batch", number, bit)) for k, v in held]
    return held


def gather_near(held, number):
    me = lax.axis_index("batch")
    held = held + [(k ^ 1, swap(v, "batch", number, 1)) for k, v in held]
    own = held[0][1]
    out = jnp.broadcast_to(own[:, None], own.shape[:1] + (number,) + own.shape[1:])
    for k, v in held[1:]:
        out = lax.dynamic_update_slice_in_dim(out, v[:, None], me ^ k, 1)
    return out


def scatter_stage(value, number, bit):
    n, _, r, c = value.shape
    pairs = value.reshape(n, -1, 2, r, c)
    mine = (lax.axis_index("batch") // bit) % 2
    keep = lax.dynamic_index_in_dim(pairs, mine, 2, False)
    send = lax.dynamic_index_in_dim(pairs, 1 - mine, 2, False).astype(bf16)
    return keep.astype(f32) + swap(send, "batch", number, bit).astype(f32)


def scatter_near(value, number):
    return scatter_stage(value, number, 1)


def scatter_far(value, number):
    for bit in bits_of(number)[1:]:
        value = scatter_stage(value, number, bit)
    return value[:, 0].astype(bf16)


RING = (0, 2, 4, 6, 7, 5, 3, 1)


def ring_place():
    s = lax.axis_index("seq")
    return jnp.where(s % 2 == 0, s // 2, 7 - s // 2)


def ring_index(place):
    place = (place + 16) % 8
    return jnp.where(place < 4, 2 * place, 15 - 2 * place)


def ring_step(value, way):
    return lax.ppermute(value, "seq", [(RING[i], RING[(i + way) % 8]) for i in range(8)])


class Ring:
    ahead = behind = None
    taken = 0

    def tie(self, *others):
        if self.number != 8:
            return others
        self.ahead, self.behind, *others = tie(self.ahead, self.behind, *others)
        return others


class Gather(Ring):
    def __init__(self, value, number):
        self.number = number
        if number != 8:
            every = lax.all_gather(value, "seq", axis=0, tiled=False)
            self.pieces = [(i, every[i]) for i in range(number)]
            return
        self.pieces = [(lax.axis_index("seq"), value)]
        self.ahead = self.behind = value
        self.place = ring_place()

    def step(self):
        if self.number != 8:
            return
        self.taken += 1
        k = self.taken
        self.ahead = ring_step(self.ahead, 1)
        if k < 4:
            self.behind = ring_step(self.behind, -1)
            self.pieces.append((ring_index(self.place + k), self.behind))
        self.pieces.append((ring_index(self.place - k), self.ahead))


class Scatter(Ring):
    def __init__(self, block, number):
        self.number = number
        self.block = block
        self.place = ring_place()

    def step(self):
        if self.number != 8:
            return
        k = 4 - self.taken
        self.taken += 1
        part = self.block(ring_index(self.place + k))
        if self.ahead is not None:
            part = (part.astype(f32) + self.ahead.astype(f32)).astype(bf16)
        self.ahead = ring_step(part, 1)
        if k > 1:
            part = self.block(ring_index(self.place - k + 1))
            if self.behind is not None:
                part = (part.astype(f32) + self.behind.astype(f32)).astype(bf16)
            self.behind = ring_step(part, -1)

    def total(self):
        if self.number != 8:
            every = jnp.stack([self.block(i) for i in range(self.number)])
            return lax.psum_scatter(every, "seq", scatter_dimension=0, tiled=False).astype(f32)
        own = self.block(lax.axis_index("seq"))
        return own.astype(f32) + self.ahead.astype(f32) + self.behind.astype(f32)


def join(pieces, number, axis):
    at, first = pieces[0]
    size = first.shape[axis]
    shape = first.shape[:axis] + (number * size,) + first.shape[axis + 1 :]
    out = jnp.zeros(shape, first.dtype)
    for at, piece in pieces:
        out = lax.dynamic_update_slice_in_dim(out, piece, at * size, axis)
    return out


def turn_tables(length):
    half = ROT_DIMS // 2
    frequency = THETA_BASE ** (-np.arange(half, dtype=np.float32) / np.float32(half))
    angle = (np.arange(length, dtype=np.float32)[:, None] * frequency.astype(np.float32)[None]).astype(
        np.float32
    )
    cosine = np.ones((length, HEAD_DIM), np.float32)
    left = np.zeros((length, HEAD_DIM), np.float32)
    right = np.zeros((length, HEAD_DIM), np.float32)
    cosine[:, :half] = np.cos(angle)
    cosine[:, half:ROT_DIMS] = np.cos(angle)
    left[:, :half] = -np.sin(angle)
    right[:, half:ROT_DIMS] = np.sin(angle)
    return [np.concatenate([t, t], 1) for t in (cosine, left, right)]


def wide(table, columns):
    if columns < table.shape[1]:
        return table[:, :columns]
    return jnp.concatenate([table] * (columns // table.shape[1]), axis=1)


def lane_roll(value, amount):
    columns = value.shape[1]
    if columns % 128 == 0:
        return pltpu.roll(value, amount % columns, 1)
    amount = amount % columns
    return jnp.concatenate([value[:, columns - amount :], value[:, : columns - amount]], axis=1)


def turn(value, cosine, left, right):
    half = ROT_DIMS // 2
    return value * cosine + lane_roll(value, -half) * left + lane_roll(value, half) * right


def turn_back(value, cosine, left, right):
    half = ROT_DIMS // 2
    return value * cosine - lane_roll(value, -half) * left - lane_roll(value, half) * right


def head_mask(columns, head):
    lane = lax.broadcasted_iota(jnp.int32, (1, columns), 1)
    return (lane >= head * HEAD_DIM) & (lane < (head + 1) * HEAD_DIM)


def block_of(length):
    return math.gcd(length, 256)


def attend_kernel(joint_ref, cos_ref, left_ref, right_ref, low_ref, context_ref, mixed_ref, lse_ref):
    length, total = joint_ref.shape
    columns = total // 3
    heads = columns // HEAD_DIM
    block = block_of(length)
    scale = 1.0 / math.sqrt(HEAD_DIM)
    for i in range(length // block):
        rows = pl.ds(i * block, block)
        tables = [wide(t[rows, :], columns) for t in (cos_ref, left_ref, right_ref)]
        low_ref[rows, 0:columns] = (
            turn(joint_ref[rows, 0:columns], *tables).astype(bf16) * scale
        ).astype(bf16)
        low_ref[rows, columns : 2 * columns] = turn(
            joint_ref[rows, columns : 2 * columns], *tables
        ).astype(bf16)
        low_ref[rows, 2 * columns :] = joint_ref[rows, 2 * columns :].astype(bf16)
    for i in range(length // block):
        rows = pl.ds(i * block, block)
        reach = (i + 1) * block
        query = low_ref[rows, 0:columns]
        key = low_ref[0:reach, columns : 2 * columns]
        value = low_ref[0:reach, 2 * columns :]
        total_out = jnp.zeros((block, columns), f32)
        lse_all = jnp.zeros((block, 128), f32)
        lane = lax.broadcasted_iota(jnp.int32, (block, 128), 1)
        ahead = lax.broadcasted_iota(jnp.int32, (block, reach), 1) > (
            i * block + lax.broadcasted_iota(jnp.int32, (block, reach), 0)
        )
        for h in range(heads):
            mask = head_mask(columns, h)
            scores = lax.dot_general(
                jnp.where(mask, query, jnp.zeros_like(query)),
                key,
                (((1,), (1,)), ((), ())),
                preferred_element_type=f32,
            )
            scores = jnp.where(ahead, NEGATIVE, scores)
            top = jnp.max(scores, axis=1, keepdims=True)
            weight = jnp.exp(scores - top)
            denominator = jnp.sum(weight, axis=1, keepdims=True)
            probs = (weight * (1.0 / denominator)).astype(bf16)
            total_out += jnp.dot(
                probs, jnp.where(mask, value, jnp.zeros_like(value)), preferred_element_type=f32
            )
            lse_all = jnp.where(lane == h, top + jnp.log(denominator), lse_all)
        context_ref[rows, :] = total_out
        mixed_ref[rows, :] = total_out.astype(bf16)
        lse_ref[rows, :] = lse_all


def attend(joint, tables):
    length, total = joint.shape
    columns = total // 3
    return pl.pallas_call(
        attend_kernel,
        out_shape=(
            jax.ShapeDtypeStruct((length, total), bf16),
            jax.ShapeDtypeStruct((length, columns), f32),
            jax.ShapeDtypeStruct((length, columns), bf16),
            jax.ShapeDtypeStruct((length, 128), f32),
        ),
        compiler_params=pltpu.CompilerParams(vmem_limit_bytes=VMEM_BYTES),
        cost_estimate=pl.CostEstimate(
            flops=4 * length * length * columns * 2,
            bytes_accessed=16 * length * total,
            transcendentals=length * length * columns // HEAD_DIM,
        ),
        name="attend",
    )(joint, *tables)


def attend_back_kernel(
    low_ref, grad_ref, context_ref, lse_ref, cos_ref, left_ref, right_ref, out_ref, dq_ref, dk_ref, dv_ref
):
    length, total = low_ref.shape
    columns = total // 3
    heads = columns // HEAD_DIM
    block = block_of(length)
    scale = 1.0 / math.sqrt(HEAD_DIM)
    dk_ref[...] = jnp.zeros_like(dk_ref)
    dv_ref[...] = jnp.zeros_like(dv_ref)
    for i in range(length // block):
        rows = pl.ds(i * block, block)
        reach = (i + 1) * block
        query = low_ref[rows, 0:columns]
        grad = grad_ref[rows, :]
        grad_wide = grad.astype(f32)
        query_t = query.astype(f32).T.astype(bf16)
        grad_t = grad_wide.T.astype(bf16)
        product = grad_wide * context_ref[rows, :]
        key = low_ref[0:reach, columns : 2 * columns]
        value = low_ref[0:reach, 2 * columns :]
        dq = jnp.zeros((block, columns), f32)
        ahead = lax.broadcasted_iota(jnp.int32, (block, reach), 1) > (
            i * block + lax.broadcasted_iota(jnp.int32, (block, reach), 0)
        )
        for h in range(heads):
            mask = head_mask(columns, h)
            span = slice(h * HEAD_DIM, (h + 1) * HEAD_DIM)
            scores = lax.dot_general(
                jnp.where(mask, query, jnp.zeros_like(query)),
                key,
                (((1,), (1,)), ((), ())),
                preferred_element_type=f32,
            )
            scores = jnp.where(ahead, NEGATIVE, scores)
            probs = jnp.exp(scores - lse_ref[rows, h : h + 1])
            dots = lax.dot_general(
                jnp.where(mask, grad, jnp.zeros_like(grad)),
                value,
                (((1,), (1,)), ((), ())),
                preferred_element_type=f32,
            )
            balance = jnp.sum(jnp.where(mask, product, 0.0), axis=1, keepdims=True)
            score_grad = (probs * (dots - balance)).astype(bf16)
            dq += jnp.dot(
                score_grad, jnp.where(mask, key, jnp.zeros_like(key)), preferred_element_type=f32
            )
            dk_ref[span, 0:reach] += jnp.dot(query_t[span], score_grad, preferred_element_type=f32)
            dv_ref[span, 0:reach] += jnp.dot(
                grad_t[span], probs.astype(bf16), preferred_element_type=f32
            )
        dq_ref[rows, :] = dq
    for i in range(length // block):
        rows = pl.ds(i * block, block)
        tables = [wide(t[rows, :], columns) for t in (cos_ref, left_ref, right_ref)]
        out_ref[rows, 0:columns] = turn_back(dq_ref[rows, :] * scale, *tables).astype(bf16)
        out_ref[rows, columns : 2 * columns] = turn_back(dk_ref[:, rows].T, *tables).astype(bf16)
        out_ref[rows, 2 * columns :] = dv_ref[:, rows].T.astype(bf16)


def attend_back(low, grad, context, lse, tables):
    length, total = low.shape
    columns = total // 3
    return pl.pallas_call(
        attend_back_kernel,
        out_shape=jax.ShapeDtypeStruct((length, total), bf16),
        scratch_shapes=[
            pltpu.VMEM((length, columns), f32),
            pltpu.VMEM((columns, length), f32),
            pltpu.VMEM((columns, length), f32),
        ],
        compiler_params=pltpu.CompilerParams(vmem_limit_bytes=VMEM_BYTES),
        cost_estimate=pl.CostEstimate(
            flops=10 * length * length * columns * 2,
            bytes_accessed=16 * length * total,
            transcendentals=length * length * columns // HEAD_DIM,
        ),
        name="attend_back",
    )(low, grad, context, lse, *tables)


def mean_of(values):
    return jnp.mean(values, axis=-1, keepdims=True)


def unit_of(values):
    center = values - mean_of(values)
    inverse_std = lax.rsqrt(mean_of(center * center) + EPSILON)
    return center * inverse_std, inverse_std


def norm_back(incoming, unit_rows, inverse_std, gain_values):
    inner = incoming * gain_values
    return inverse_std * (inner - mean_of(inner) - unit_rows * mean_of(inner * unit_rows))


def dot(left, right, contract):
    return lax.dot_general(left, right, (contract, ((), ())), preferred_element_type=f32)


def make_body(n_seq, n_batch):
    def body(
        tokens,
        language,
        language_weight,
        output_grad,
        attention_gain,
        attention_shift,
        joint_weight,
        joint_bias,
        output_weight,
        feedfwd_gain,
        feedfwd_shift,
        gate_weight,
        up_weight,
        down_weight,
    ):
        _, local, width = tokens.shape
        rows, ff_width = gate_weight.shape
        length = local * n_seq
        columns = width // n_seq
        tiles = -(-ff_width // (128 * n_seq))
        ff_local = 128 * tiles
        seq_at = lax.axis_index("seq")
        first_row = seq_at * local
        values = tokens[0]
        tables = [jnp.asarray(t) for t in turn_tables(length)]

        center_own = values - mean_of(values)
        inverse_one = lax.rsqrt(mean_of(center_own * center_own) + EPSILON)
        unit_own = center_own * inverse_one
        ring = Gather(center_own.astype(bf16), n_seq)

        small = jnp.concatenate(
            [attention_gain, attention_shift, feedfwd_gain, feedfwd_shift, joint_bias]
        )
        extra = -(-small.shape[0] // (3 * columns))
        small = jnp.pad(small, (0, 8 * 3 * columns - small.shape[0])).reshape(8, 3 * columns)
        blocks = jnp.transpose(joint_weight.reshape(rows, 3, n_seq, columns), (2, 0, 1, 3))
        blocks = blocks.reshape(n_seq, rows, 3 * columns)
        blocks = jnp.concatenate(
            [blocks, jnp.broadcast_to(small[None], (n_seq,) + small.shape)], axis=1
        )
        ff_blocks = [
            jnp.pad(w, ((0, 0), (0, n_seq * ff_local - ff_width))).reshape(rows, tiles, n_seq, 128)
            for w in (gate_weight, up_weight, down_weight)
        ]
        ff_blocks = jnp.transpose(jnp.stack(ff_blocks, 1), (3, 0, 1, 2, 4))
        ff_blocks = ff_blocks.reshape(n_seq, rows, 3 * ff_local)

        ring.step()
        blocks = exchange_near(blocks, n_seq)
        ff_blocks = after(ff_blocks, blocks)
        ff_blocks = exchange_near(ff_blocks, n_seq)
        (blocks,) = ring.tie(blocks)
        ring.step()
        blocks = exchange_far(blocks, n_seq)
        blocks, ff_blocks = ring.tie(blocks, ff_blocks)
        ring.step()
        held = gather_far(blocks, n_batch)
        ff_blocks = exchange_far(ff_blocks, n_seq)
        (tied,) = ring.tie(held[-1][1])
        held[-1] = (held[-1][0], tied)
        ring.step()
        joint_all = gather_near(held, n_batch)
        center = join(ring.pieces, n_seq, 0)
        joint_all, center, ff_blocks = tie(joint_all, center, ff_blocks)
        ff_held = gather_far(ff_blocks, n_batch)
        small = joint_all[:, :, rows : rows + extra].reshape(n_seq, n_batch, -1)
        joint_all = joint_all[:, :, :rows].reshape(width, 3 * columns)
        piece = width // (n_seq * n_batch)

        def small_part(start, size):
            return small[:, :, start : start + size].reshape(1, -1).astype(f32)

        gain_one = small_part(0, piece)
        shift_one = small_part(piece, piece)
        gain_two = small_part(2 * piece, piece)
        shift_two = small_part(3 * piece, piece)
        bias_all = small_part(4 * piece, 3 * piece).reshape(3, n_seq, columns)
        bias = lax.dynamic_slice_in_dim(bias_all, seq_at, 1, 1).reshape(1, 3 * columns)

        output_all = lax.all_gather(output_weight, ("seq", "batch"), axis=0, tiled=True)

        def output_rows(at):
            return lax.dynamic_slice_in_dim(output_all, at * columns, columns, 0)

        chosen = language[:, None] == jnp.arange(LANGS, dtype=jnp.int32)[None, :]
        row_scale = jnp.sum(jnp.where(chosen, language_weight[None, :], 0.0), axis=1)
        cotangent = output_grad[0] * row_scale[:, None]
        down_grad = after(cotangent.astype(bf16), center)
        down_grad = lax.all_gather(down_grad, "seq", axis=0, tiled=True)

        unit_one, _ = unit_of(center.astype(f32))
        first_input = (unit_one * gain_one + shift_one).astype(bf16)
        joint = dot(first_input, joint_all, ((1,), (0,))) + bias
        low, context, mixed, lse = attend(joint, tables)

        ring = Gather(mixed, n_seq)
        ring.step()
        ring.tie()
        ring.step()
        ring.tie()
        ring.step()
        (tied,) = ring.tie(ff_held[-1][1])
        ff_held[-1] = (ff_held[-1][0], tied)
        ring.step()
        ff_all = gather_near(ff_held, n_batch)
        if n_seq == 8:
            at, last = ring.pieces[-1]
            early = join(ring.pieces[:-1] + [(at, jnp.zeros_like(last))], n_seq, 1)
            projected = dot(early, output_all, ((1,), (0,)))
            projected, last, ff_all = tie(projected, last, ff_all)
            projected = projected + dot(last, output_rows(at), ((1,), (0,)))
            mixed_all = lax.dynamic_update_slice_in_dim(early, last, at * columns, 1)
        else:
            mixed_all = join(ring.pieces, n_seq, 1)
            projected = dot(mixed_all, output_all, ((1,), (0,)))
        ff_all = ff_all.reshape(width, 3 * ff_local)
        gate_all = ff_all[:, :ff_local]
        up_all = ff_all[:, ff_local : 2 * ff_local]
        down_all = ff_all[:, 2 * ff_local :]
        middle_own = values + lax.dynamic_slice_in_dim(projected, first_row, local, 0)
        unit_two, inverse_two = unit_of(center.astype(f32) + projected)
        second_input = (unit_two * gain_two + shift_two).astype(bf16)

        gate = dot(second_input, gate_all, ((1,), (0,)))
        upper = dot(second_input, up_all, ((1,), (0,)))
        sigmoid = jax.nn.sigmoid(gate)
        activated = gate * sigmoid
        hidden = (activated * upper).astype(bf16)
        result_part = dot(hidden, down_all, ((1,), (1,))).astype(bf16)
        result_sum = lax.psum_scatter(result_part, "seq", scatter_dimension=0, tiled=True)

        def split(grad, *shape):
            return grad.astype(bf16).reshape((n_seq, n_batch, rows) + shape)

        grad_down = scatter_near(split(dot(down_grad, hidden, ((0,), (0,))), ff_local), n_batch)
        hidden_grad = dot(down_grad, down_all, ((1,), (0,)))
        hidden_grad, result_part = tie(hidden_grad, result_part)
        gate_grad = (hidden_grad * upper * sigmoid * (1.0 + gate * (1.0 - sigmoid))).astype(bf16)
        up_grad = (hidden_grad * activated).astype(bf16)
        second_part = dot(gate_grad, gate_all, ((1,), (1,))) + dot(up_grad, up_all, ((1,), (1,)))
        second_part, grad_down = tie(second_part, grad_down)
        grad_down = scatter_far(grad_down, n_batch)

        scaled = second_part * (gain_two * inverse_two)
        scaled_low = scaled.astype(bf16)
        sums = jnp.stack([jnp.mean(scaled, axis=-1), jnp.mean(scaled * unit_two, axis=-1)])
        sums = sums.astype(bf16).reshape(-1, columns)
        if n_seq == 8:

            def through_block(at):
                part = dot(scaled_low, output_rows(at), ((1,), (1,))).astype(bf16)
                return jnp.concatenate([part, sums], axis=0)

        else:
            through = dot(scaled_low, output_all, ((1,), (1,))).astype(bf16)

            def through_block(at):
                return jnp.concatenate([through[:, at * columns : (at + 1) * columns], sums], axis=0)

        heads_weight = output_rows(seq_at)
        ring = Scatter(through_block, n_seq)
        ring.step()
        grad_both = [split(dot(second_input, g, ((0,), (0,))), ff_local) for g in (gate_grad, up_grad)]
        grad_both = jnp.concatenate(grad_both, axis=3)
        grad_down, grad_both = ring.tie(grad_down, grad_both)
        ring.step()
        grad_both = scatter_near(grad_both, n_batch)
        grad_down = exchange_near(grad_down, n_seq)
        grad_both, grad_down = ring.tie(grad_both, grad_down)
        ring.step()
        grad_both = scatter_far(grad_both, n_batch)
        from_cot = dot(down_grad, heads_weight, ((1,), (1,)))
        from_unit = dot(unit_two.astype(bf16), heads_weight, ((1,), (1,)))
        from_cot, from_unit, result_sum = ring.tie(from_cot, from_unit, result_sum)
        ring.step()
        grad_output = dot(mixed_all, scaled_low, ((0,), (0,))).astype(bf16)
        (grad_output,) = ring.tie(grad_output)
        through = ring.total()
        through, grad_both, grad_down = tie(through, grad_both, grad_down)
        grad_both = exchange_near(grad_both, n_seq)
        grad_down = exchange_far(grad_down, n_seq)
        result = middle_own + result_sum.astype(f32)
        weight_sums = jnp.sum(heads_weight.astype(f32), axis=1)[None, :]
        means = through[length:].reshape(2, length)
        mean_one, mean_two = means[0][:, None], means[1][:, None]
        context_grad = (
            through[:length] + from_cot - mean_one * weight_sums - mean_two * from_unit
        ).astype(bf16)
        joint_grad = attend_back(low, context_grad, context, lse, tables)

        rest = down_grad.astype(f32) - mean_one - unit_two * mean_two
        rest = dot(mixed, rest.astype(bf16), ((0,), (0,)))
        rest = rest + lax.dynamic_slice_in_dim(grad_output, seq_at * columns, columns, 0)
        grad_output = lax.dynamic_update_slice_in_dim(
            grad_output, rest.astype(bf16), seq_at * columns, 0
        )
        joint_grad, grad_both, grad_down, grad_output = tie(
            joint_grad, grad_both, grad_down, grad_output
        )
        grad_joint = dot(first_input, joint_grad, ((0,), (0,)))
        first_part = dot(joint_grad, joint_all, ((1,), (1,)))

        bias_part = jnp.sum(joint_grad.astype(f32), axis=0).reshape(3, 1, columns)
        bias_part = lax.dynamic_update_slice_in_dim(
            jnp.zeros((3, n_seq, columns), f32), bias_part, seq_at, 1
        )
        vectors = [
            jnp.sum(first_part * unit_one, axis=0),
            jnp.sum(first_part, axis=0),
            jnp.sum(second_part * unit_two, axis=0),
            jnp.sum(second_part, axis=0),
            bias_part,
        ]
        vectors = jnp.concatenate([v.reshape(n_seq, n_batch, -1) for v in vectors], axis=2)
        vectors = jnp.pad(vectors, ((0, 0), (0, 0), (0, 8 * 3 * columns - vectors.shape[2])))
        vectors = vectors.reshape(n_seq, n_batch, 8, 3 * columns).astype(bf16)
        grad_joint = jnp.concatenate([split(grad_joint, 3 * columns), vectors], axis=2)
        grad_joint = scatter_near(grad_joint, n_batch)

        inner = first_part * (gain_one * lax.rsqrt(mean_of(center.astype(f32) ** 2) + EPSILON))
        first_sums = jnp.stack([jnp.mean(inner, axis=-1), jnp.mean(inner * unit_one, axis=-1)])
        both = (scaled + inner).astype(bf16)
        both, grad_joint = tie(both, grad_joint)

        def both_block(at):
            part = lax.dynamic_slice_in_dim(both, at * local, local, 0)
            below = lax.dynamic_slice_in_dim(first_sums, at * local, local, 1)
            below = jnp.pad(below.reshape(-1), (0, 8 * width - 2 * local)).reshape(8, width)
            return jnp.concatenate([part, below.astype(bf16)], axis=0)

        ring = Scatter(both_block, n_seq)
        ring.step()
        grad_joint = scatter_far(grad_joint, n_batch)
        grad_output = scatter_near(split(grad_output, width), n_batch)
        grad_joint, grad_output = ring.tie(grad_joint, grad_output)
        ring.step()
        grad_joint = exchange_near(grad_joint, n_seq)
        grad_output = scatter_far(grad_output, n_batch)
        (grad_joint,) = ring.tie(grad_joint)
        ring.step()
        grad_joint = exchange_far(grad_joint, n_seq)
        grad_joint, grad_both, grad_output = ring.tie(grad_joint, grad_both, grad_output)
        ring.step()
        grad_both = exchange_far(grad_both, n_seq)
        grad_output = lax.psum_scatter(
            grad_output, "seq", scatter_dimension=0, tiled=False
        ).astype(f32)
        both_own = ring.total()
        first_sums = both_own[local].reshape(-1)[: 2 * local].reshape(2, local)

        def own(array):
            return lax.dynamic_slice_in_dim(array, first_row, local, 0)

        token_grad = (
            cotangent
            - own(mean_one)
            - own(unit_two) * own(mean_two)
            + both_own[:local]
            - first_sums[0][:, None]
            - unit_own * first_sums[1][:, None]
        )

        def unsplit(grad):
            grad = grad.reshape(n_seq, rows, tiles, 128).astype(f32)
            return jnp.transpose(grad, (1, 2, 0, 3)).reshape(rows, n_seq * ff_local)[:, :ff_width]

        grad_gate = unsplit(grad_both[:, :, :ff_local])
        grad_up = unsplit(grad_both[:, :, ff_local:])
        grad_down = unsplit(grad_down)
        grad_joint = grad_joint.astype(f32)
        vectors = jnp.sum(grad_joint[:, rows : rows + extra], axis=0).reshape(-1)
        grad_joint = grad_joint[:, :rows].reshape(n_seq, rows, 3, columns)
        grad_joint = jnp.transpose(grad_joint, (1, 2, 0, 3)).reshape(rows, 3 * width)
        return (
            result[None],
            token_grad[None],
            vectors[:piece],
            vectors[piece : 2 * piece],
            grad_joint,
            vectors[4 * piece : 7 * piece],
            grad_output,
            vectors[2 * piece : 3 * piece],
            vectors[3 * piece : 4 * piece],
            grad_gate,
            grad_up,
            grad_down,
        )

    return body


def solution(mesh):
    rows = P(("seq", "batch"))
    matrix = P(("seq", "batch"), None)
    data = P("batch", "seq", None)
    return jax.shard_map(
        make_body(mesh.shape["seq"], mesh.shape["batch"]),
        mesh=mesh,
        in_specs=(
            data,
            P("batch"),
            P(),
            data,
            rows,
            rows,
            matrix,
            rows,
            matrix,
            rows,
            rows,
            matrix,
            matrix,
            matrix,
        ),
        out_specs=(data, data, rows, rows, matrix, rows, matrix, rows, rows, matrix, matrix, matrix),
        check_vma=False,
    )
```

```python
import math

import numpy as np

import jax
import jax.numpy as jnp
from jax import lax
from jax.experimental import pallas as pl
from jax.experimental.pallas import tpu as pltpu
from jax.sharding import PartitionSpec as P

HEADS = 32
HEAD_DIM = 64
ROT_DIMS = 16
LANGS = 7

EPSILON = 1e-05
THETA_BASE = 10000.0
NEGATIVE = -1e30
VMEM_BYTES = 56 * 1024 * 1024

bf16 = jnp.bfloat16
f32 = jnp.float32


def swap(value, axis, number, bit):
    return lax.ppermute(value, axis, [(i, i ^ bit) for i in range(number)])


def bits_of(number):
    return [1 << i for i in range(number.bit_length() - 1)]


def tie(*values):
    return lax.optimization_barrier(values)


def after(value, *others):
    return tie(value, *others)[0]


def exchange_begin(blocks, number, bit):
    mine = (lax.axis_index("seq") // bit) % 2
    pairs = blocks.reshape((number // (2 * bit), 2, bit) + blocks.shape[1:])
    return pairs, swap(lax.dynamic_slice_in_dim(pairs, 1 - mine, 1, 1), "seq", number, bit)


def exchange_end(state, number, bit):
    pairs, got = state
    mine = (lax.axis_index("seq") // bit) % 2
    out = lax.dynamic_update_slice_in_dim(pairs, got, 1 - mine, 1)
    return out.reshape((number,) + pairs.shape[3:])


def exchange(blocks, number, bit):
    return exchange_end(exchange_begin(blocks, number, bit), number, bit)


def exchange_far(blocks, number):
    if number != 8:
        for bit in bits_of(number)[1:]:
            blocks = exchange(blocks, number, bit)
        return blocks
    place = lax.axis_index("seq") // 2
    out = blocks.reshape((4, 2) + blocks.shape[1:])
    parts = [
        swap(lax.dynamic_slice_in_dim(out, place ^ k, 1, 0), "seq", number, k * 2)
        for k in range(1, 4)
    ]
    for k, part in enumerate(parts):
        out = lax.dynamic_update_slice_in_dim(out, part, place ^ (k + 1), 0)
    return out.reshape(blocks.shape)


def rest_of_exchange(blocks, number):
    for bit in bits_of(number)[3:]:
        blocks = exchange(blocks, number, bit)
    return blocks


def gather_far(value, number):
    held = [(0, value)]
    for bit in reversed(bits_of(number)[1:]):
        held = held + [(k ^ bit, swap(v, "batch", number, bit)) for k, v in held]
    return held


def gather_near(held, number):
    held = dict(held + [(k ^ 1, swap(v, "batch", number, 1)) for k, v in held])
    return [held[k] for k in range(number)]


def scatter_stage(value, number, bit):
    n, _, r, c = value.shape
    pairs = value.reshape(n, -1, 2, r, c)
    mine = (lax.axis_index("batch") // bit) % 2
    keep = lax.dynamic_index_in_dim(pairs, mine, 2, False)
    send = lax.dynamic_index_in_dim(pairs, 1 - mine, 2, False).astype(bf16)
    return (keep.astype(f32) + swap(send, "batch", number, bit).astype(f32)).astype(bf16)


def scatter_near(value, number):
    return scatter_stage(value, number, 1)


def scatter_far(value, number):
    for bit in bits_of(number)[1:]:
        value = scatter_stage(value, number, bit)
    return value[:, 0]


RING = (0, 2, 4, 6, 7, 5, 3, 1)


def ring_place():
    s = lax.axis_index("seq")
    return jnp.where(s % 2 == 0, s // 2, 7 - s // 2)


def ring_index(place):
    place = (place + 16) % 8
    return jnp.where(place < 4, 2 * place, 15 - 2 * place)


ARRIVAL = (0, 1, -1, 2, -2, 3, -3, -4)


def arrival(number):
    if number != 8:
        return list(range(number))
    return [ring_index(ring_place() + step) for step in ARRIVAL]


def ring_step(value, way):
    return lax.ppermute(value, "seq", [(RING[i], RING[(i + way) % 8]) for i in range(8)])


class Ring:
    ahead = behind = None
    taken = 0

    def tie(self, *others):
        if self.number != 8:
            return others
        self.ahead, self.behind, *others = tie(self.ahead, self.behind, *others)
        return others


class Gather(Ring):
    def __init__(self, value, number):
        self.number = number
        if number != 8:
            every = lax.all_gather(value, "seq", axis=0, tiled=False)
            self.pieces = [(i, every[i]) for i in range(number)]
            return
        self.pieces = [(lax.axis_index("seq"), value)]
        self.ahead = self.behind = value
        self.place = ring_place()

    def step(self):
        if self.number != 8:
            return
        self.taken += 1
        k = self.taken
        self.ahead = ring_step(self.ahead, 1)
        if k < 4:
            self.behind = ring_step(self.behind, -1)
            self.pieces.append((ring_index(self.place + k), self.behind))
        self.pieces.append((ring_index(self.place - k), self.ahead))


class Scatter(Ring):
    def __init__(self, block, number):
        self.number = number
        self.block = block
        self.place = ring_place()

    def step(self):
        if self.number != 8:
            return
        k = 4 - self.taken
        self.taken += 1
        part = self.block(ring_index(self.place + k))
        if self.ahead is not None:
            part = (part.astype(f32) + self.ahead.astype(f32)).astype(bf16)
        self.ahead = ring_step(part, 1)
        if k > 1:
            part = self.block(ring_index(self.place - k + 1))
            if self.behind is not None:
                part = (part.astype(f32) + self.behind.astype(f32)).astype(bf16)
            self.behind = ring_step(part, -1)

    def total(self):
        if self.number != 8:
            every = jnp.stack([self.block(i) for i in range(self.number)])
            return lax.psum_scatter(every, "seq", scatter_dimension=0, tiled=False).astype(f32)
        own = self.block(lax.axis_index("seq"))
        return own.astype(f32) + self.ahead.astype(f32) + self.behind.astype(f32)


def join(pieces, number, axis):
    at, first = pieces[0]
    size = first.shape[axis]
    shape = first.shape[:axis] + (number * size,) + first.shape[axis + 1 :]
    out = jnp.zeros(shape, first.dtype)
    for at, piece in pieces:
        out = lax.dynamic_update_slice_in_dim(out, piece, at * size, axis)
    return out


def turn_tables(length):
    half = ROT_DIMS // 2
    frequency = THETA_BASE ** (-np.arange(half, dtype=np.float32) / np.float32(half))
    angle = (np.arange(length, dtype=np.float32)[:, None] * frequency.astype(np.float32)[None]).astype(
        np.float32
    )
    cosine = np.ones((length, HEAD_DIM), np.float32)
    left = np.zeros((length, HEAD_DIM), np.float32)
    right = np.zeros((length, HEAD_DIM), np.float32)
    cosine[:, :half] = np.cos(angle)
    cosine[:, half:ROT_DIMS] = np.cos(angle)
    left[:, :half] = -np.sin(angle)
    right[:, half:ROT_DIMS] = np.sin(angle)
    return [np.concatenate([t, t], 1) for t in (cosine, left, right)]


def wide(table, columns):
    if columns < table.shape[1]:
        return table[:, :columns]
    return jnp.concatenate([table] * (columns // table.shape[1]), axis=1)


def lane_roll(value, amount):
    columns = value.shape[1]
    if columns % 128 == 0:
        return pltpu.roll(value, amount % columns, 1)
    amount = amount % columns
    return jnp.concatenate([value[:, columns - amount :], value[:, : columns - amount]], axis=1)


def turn(value, cosine, left, right):
    half = ROT_DIMS // 2
    return value * cosine + lane_roll(value, -half) * left + lane_roll(value, half) * right


def turn_back(value, cosine, left, right):
    half = ROT_DIMS // 2
    return value * cosine - lane_roll(value, -half) * left - lane_roll(value, half) * right


def head_mask(columns, head):
    lane = lax.broadcasted_iota(jnp.int32, (1, columns), 1)
    return (lane >= head * HEAD_DIM) & (lane < (head + 1) * HEAD_DIM)


def block_of(length):
    return math.gcd(length, 256)


def attend_kernel(low_ref, context_ref, mixed_ref, lse_ref):
    length, total = low_ref.shape
    columns = total // 3
    heads = columns // HEAD_DIM
    block = block_of(length)
    for i in range(length // block):
        rows = pl.ds(i * block, block)
        reach = (i + 1) * block
        query = low_ref[rows, 0:columns]
        key = low_ref[0:reach, columns : 2 * columns]
        value = low_ref[0:reach, 2 * columns :]
        total_out = jnp.zeros((block, columns), f32)
        lse_all = jnp.zeros((block, 128), f32)
        lane = lax.broadcasted_iota(jnp.int32, (block, 128), 1)
        ahead = lax.broadcasted_iota(jnp.int32, (block, reach), 1) > (
            i * block + lax.broadcasted_iota(jnp.int32, (block, reach), 0)
        )
        for h in range(heads):
            mask = head_mask(columns, h)
            scores = lax.dot_general(
                jnp.where(mask, query, jnp.zeros_like(query)),
                key,
                (((1,), (1,)), ((), ())),
                preferred_element_type=f32,
            )
            scores = jnp.where(ahead, NEGATIVE, scores)
            top = jnp.max(scores, axis=1, keepdims=True)
            weight = jnp.exp(scores - top)
            denominator = jnp.sum(weight, axis=1, keepdims=True)
            probs = (weight * (1.0 / denominator)).astype(bf16)
            total_out += jnp.dot(
                probs, jnp.where(mask, value, jnp.zeros_like(value)), preferred_element_type=f32
            )
            lse_all = jnp.where(lane == h, top + jnp.log(denominator), lse_all)
        context_ref[rows, :] = total_out
        mixed_ref[rows, :] = total_out.astype(bf16)
        lse_ref[rows, :] = lse_all


def attend(low):
    length, total = low.shape
    columns = total // 3
    return pl.pallas_call(
        attend_kernel,
        out_shape=(
            jax.ShapeDtypeStruct((length, columns), f32),
            jax.ShapeDtypeStruct((length, columns), bf16),
            jax.ShapeDtypeStruct((length, 128), f32),
        ),
        compiler_params=pltpu.CompilerParams(vmem_limit_bytes=VMEM_BYTES),
        cost_estimate=pl.CostEstimate(
            flops=4 * length * length * columns * 2,
            bytes_accessed=16 * length * total,
            transcendentals=length * length * columns // HEAD_DIM,
        ),
        name="attend",
    )(low)


def attend_back_kernel(
    low_ref, grad_ref, context_ref, lse_ref, cos_ref, left_ref, right_ref, out_ref, dq_ref, dk_ref, dv_ref
):
    length, total = low_ref.shape
    columns = total // 3
    heads = columns // HEAD_DIM
    block = block_of(length)
    scale = 1.0 / math.sqrt(HEAD_DIM)
    dk_ref[...] = jnp.zeros_like(dk_ref)
    dv_ref[...] = jnp.zeros_like(dv_ref)
    for i in range(length // block):
        rows = pl.ds(i * block, block)
        reach = (i + 1) * block
        query = low_ref[rows, 0:columns]
        grad = grad_ref[rows, :]
        grad_wide = grad.astype(f32)
        query_t = query.astype(f32).T.astype(bf16)
        grad_t = grad_wide.T.astype(bf16)
        product = grad_wide * context_ref[rows, :]
        key = low_ref[0:reach, columns : 2 * columns]
        value = low_ref[0:reach, 2 * columns :]
        dq = jnp.zeros((block, columns), f32)
        ahead = lax.broadcasted_iota(jnp.int32, (block, reach), 1) > (
            i * block + lax.broadcasted_iota(jnp.int32, (block, reach), 0)
        )
        for h in range(heads):
            mask = head_mask(columns, h)
            span = slice(h * HEAD_DIM, (h + 1) * HEAD_DIM)
            scores = lax.dot_general(
                jnp.where(mask, query, jnp.zeros_like(query)),
                key,
                (((1,), (1,)), ((), ())),
                preferred_element_type=f32,
            )
            scores = jnp.where(ahead, NEGATIVE, scores)
            probs = jnp.exp(scores - lse_ref[rows, h : h + 1])
            dots = lax.dot_general(
                jnp.where(mask, grad, jnp.zeros_like(grad)),
                value,
                (((1,), (1,)), ((), ())),
                preferred_element_type=f32,
            )
            balance = jnp.sum(jnp.where(mask, product, 0.0), axis=1, keepdims=True)
            score_grad = (probs * (dots - balance)).astype(bf16)
            dq += jnp.dot(
                score_grad, jnp.where(mask, key, jnp.zeros_like(key)), preferred_element_type=f32
            )
            dk_ref[span, 0:reach] += jnp.dot(query_t[span], score_grad, preferred_element_type=f32)
            dv_ref[span, 0:reach] += jnp.dot(
                grad_t[span], probs.astype(bf16), preferred_element_type=f32
            )
        dq_ref[rows, :] = dq
    for i in range(length // block):
        rows = pl.ds(i * block, block)
        tables = [wide(t[rows, :], columns) for t in (cos_ref, left_ref, right_ref)]
        out_ref[rows, 0:columns] = turn_back(dq_ref[rows, :] * scale, *tables).astype(bf16)
        out_ref[rows, columns : 2 * columns] = turn_back(dk_ref[:, rows].T, *tables).astype(bf16)
        out_ref[rows, 2 * columns :] = dv_ref[:, rows].T.astype(bf16)


def attend_back(low, grad, context, lse, tables):
    length, total = low.shape
    columns = total // 3
    return pl.pallas_call(
        attend_back_kernel,
        out_shape=jax.ShapeDtypeStruct((length, total), bf16),
        scratch_shapes=[
            pltpu.VMEM((length, columns), f32),
            pltpu.VMEM((columns, length), f32),
            pltpu.VMEM((columns, length), f32),
        ],
        compiler_params=pltpu.CompilerParams(vmem_limit_bytes=VMEM_BYTES),
        cost_estimate=pl.CostEstimate(
            flops=10 * length * length * columns * 2,
            bytes_accessed=16 * length * total,
            transcendentals=length * length * columns // HEAD_DIM,
        ),
        name="attend_back",
    )(low, grad, context, lse, *tables)


def mean_of(values):
    return jnp.mean(values, axis=-1, keepdims=True)


def unit_of(values):
    center = values - mean_of(values)
    inverse_std = lax.rsqrt(mean_of(center * center) + EPSILON)
    return center * inverse_std, inverse_std


def norm_back(incoming, unit_rows, inverse_std, gain_values):
    inner = incoming * gain_values
    return inverse_std * (inner - mean_of(inner) - unit_rows * mean_of(inner * unit_rows))


def dot(left, right, contract):
    return lax.dot_general(left, right, (contract, ((), ())), preferred_element_type=f32)


def block_spec(block, columns):
    return pl.BlockSpec((block, columns), lambda i: (i, 0))


def whole_spec(rows, columns):
    return pl.BlockSpec((rows, columns), lambda i: (0, 0))


def once_spec(rows, columns):
    return pl.BlockSpec((rows, columns), lambda i: (0, 0), pipeline_mode=pl.Buffered(1))


def any_specs(number):
    return [pl.BlockSpec(memory_space=pl.ANY)] * number


def run_copies(copies, sems):
    copies = [pltpu.make_async_copy(*pair, sems.at[i]) for i, pair in enumerate(copies)]
    for copy in copies:
        copy.start()
    for copy in copies:
        copy.wait()


def weight_copies(piece_refs, weight_ref):
    me = lax.axis_index("batch")
    rows = weight_ref.shape[2]
    return [
        (ref.at[:, pl.ds(0, rows), :], weight_ref.at[:, me ^ k])
        for k, ref in enumerate(piece_refs)
    ]


def load_pieces(piece_refs, weight_ref, sems):
    @pl.when(pl.program_id(0) == 0)
    def _():
        run_copies(weight_copies(piece_refs, weight_ref), sems)


def weight_of(weight_ref, start, size):
    part = weight_ref[:, :, :, start : start + size]
    return part.reshape(-1, size)


def call_kernel(kernel, length, in_specs, out, scratch, args, name, flops):
    block = block_of(length)
    return pl.pallas_call(
        kernel,
        grid=(length // block,),
        in_specs=in_specs,
        out_specs=[spec for _, spec in out],
        out_shape=[shape for shape, _ in out],
        scratch_shapes=scratch,
        compiler_params=pltpu.CompilerParams(
            vmem_limit_bytes=VMEM_BYTES, dimension_semantics=("arbitrary",)
        ),
        cost_estimate=pl.CostEstimate(
            flops=flops, bytes_accessed=flops // 500, transcendentals=0
        ),
        name=name,
    )(*args)


def rows_out(length, columns, kind):
    return (jax.ShapeDtypeStruct((length, columns), kind), block_spec(block_of(length), columns))


def sums_out(columns):
    return (jax.ShapeDtypeStruct((8, columns), f32), whole_spec(8, columns))


def add_sums(ref, *rows):
    @pl.when(pl.program_id(0) == 0)
    def _():
        ref[...] = jnp.zeros_like(ref)

    for i, row in enumerate(rows):
        ref[i : i + 1, :] += jnp.sum(row, axis=0, keepdims=True)


def heads_kernel(n, n_seq, *refs):
    gain_ref, shift_ref, bias_ref, cos_ref, left_ref, right_ref = refs[:6]
    pieces = refs[6 : 6 + n]
    center_pieces = refs[6 + n : 6 + n + n_seq]
    low_ref, input_ref, center_ref, weight_ref, all_ref, sems = refs[6 + n + n_seq :]
    local = all_ref.shape[1]

    @pl.when(pl.program_id(0) == 0)
    def _():
        copies = [
            (ref.at[pl.ds(0, local), :], all_ref.at[at])
            for at, ref in zip(arrival(n_seq), center_pieces)
        ]
        run_copies(copies + weight_copies(pieces, weight_ref), sems)

    total = low_ref.shape[1]
    columns = total // 3
    block, width = center_ref.shape
    many = block // local
    center = all_ref[pl.ds(pl.program_id(0) * many, many)].reshape(block, width)
    center_ref[...] = center
    unit, _ = unit_of(center.astype(f32))
    first_input = (unit * gain_ref[...] + shift_ref[...]).astype(bf16)
    input_ref[...] = first_input
    joint = dot(first_input, weight_of(weight_ref, 0, total), ((1,), (0,))) + bias_ref[...]
    tables = [wide(t[...], columns) for t in (cos_ref, left_ref, right_ref)]
    scale = 1.0 / math.sqrt(HEAD_DIM)
    query = turn(joint[:, :columns], *tables).astype(bf16)
    low_ref[:, :columns] = (query.astype(f32) * scale).astype(bf16)
    low_ref[:, columns : 2 * columns] = turn(joint[:, columns : 2 * columns], *tables).astype(bf16)
    low_ref[:, 2 * columns :] = joint[:, 2 * columns :].astype(bf16)


def make_heads(center_pieces, gain, shift, bias, tables, pieces, rows, local):
    n_seq, n = len(center_pieces), len(pieces)
    length, width = local * n_seq, gain.shape[1]
    total = bias.shape[1]
    block = block_of(length)
    return call_kernel(
        lambda *refs: heads_kernel(n, n_seq, *refs),
        length,
        [whole_spec(1, width), whole_spec(1, width), whole_spec(1, total)]
        + [block_spec(block, 128)] * 3
        + any_specs(n + n_seq),
        [
            rows_out(length, total, bf16),
            rows_out(length, width, bf16),
            rows_out(length, width, bf16),
        ],
        [
            pltpu.VMEM((n_seq, n, rows, total), bf16),
            pltpu.VMEM((n_seq, local, width), bf16),
            pltpu.SemaphoreType.DMA((n + n_seq,)),
        ],
        (gain, shift, bias, *tables, *pieces, *center_pieces),
        "make_heads",
        2 * length * width * total,
    )


def middle_kernel(n, n_seq, many, *refs):
    center_ref, gain_ref, shift_ref = refs[:3]
    pieces, mixed_pieces = refs[3 : 3 + n], refs[3 + n : 3 + n + many]
    input_ref, unit_ref, inverse_ref, mixed_ref, out_ref = refs[3 + n + many : 8 + n + many]
    weight_ref, all_ref, sems, out_sem = refs[8 + n + many :]
    rows, width = weight_ref.shape[2:]
    columns = width // n_seq
    step = pl.program_id(0)
    give = pltpu.make_async_copy(weight_ref, out_ref, out_sem)

    @pl.when(step == 0)
    def _():
        me = lax.axis_index("batch")
        places = arrival(n_seq)
        copies = [
            (ref.at[pl.ds(j * rows, rows), :], weight_ref.at[at, me ^ k])
            for k, ref in enumerate(pieces)
            for j, at in enumerate(places)
        ]
        if many == 1:
            copies.append((mixed_pieces[0], all_ref))
        else:
            for at, ref in zip(places, mixed_pieces):
                span = pl.ds(pl.multiple_of(at * columns, columns), columns)
                copies.append((ref, all_ref.at[:, span]))
        run_copies(copies, sems)
        give.start()

    block = center_ref.shape[0]
    mixed = all_ref[pl.ds(pl.multiple_of(step * block, block), block), :]
    mixed_ref[...] = mixed
    projected = dot(mixed, weight_ref[...].reshape(width, width), ((1,), (0,)))
    unit, inverse = unit_of(center_ref[...].astype(f32) + projected)
    input_ref[...] = (unit * gain_ref[...] + shift_ref[...]).astype(bf16)
    unit_ref[...] = unit.astype(bf16)
    inverse_ref[...] = jnp.broadcast_to(inverse, inverse_ref.shape)

    @pl.when(step == pl.num_programs(0) - 1)
    def _():
        give.wait()


def make_middle(mixed_pieces, pieces, center, gain, shift, n_seq, rows):
    length, width = center.shape
    n, many = len(pieces), len(mixed_pieces)
    block = block_of(length)
    row = whole_spec(1, width)
    weight_shape = (n_seq, n, rows, width)
    return call_kernel(
        lambda *refs: middle_kernel(n, n_seq, many, *refs),
        length,
        [block_spec(block, width), row, row] + any_specs(n + many),
        [
            rows_out(length, width, bf16),
            rows_out(length, width, bf16),
            rows_out(length, 128, f32),
            rows_out(length, width, bf16),
            (jax.ShapeDtypeStruct(weight_shape, bf16), pl.BlockSpec(memory_space=pl.ANY)),
        ],
        [
            pltpu.VMEM(weight_shape, bf16),
            pltpu.VMEM((length, width), bf16),
            pltpu.SemaphoreType.DMA((n * n_seq + many,)),
            pltpu.SemaphoreType.DMA,
        ],
        (center, gain, shift, *pieces, *mixed_pieces),
        "make_middle",
        2 * length * width * width,
    )


def feed_kernel(n, *refs):
    input_ref, grad_ref, unit_ref, inverse_ref, gain_ref, output_ref = refs[:6]
    pieces = refs[6 : 6 + n]
    hidden_ref, grads_ref, result_ref, back_ref, through_ref, sums_ref = refs[6 + n : 12 + n]
    weight_ref, sems = refs[12 + n :]
    load_pieces(pieces, weight_ref, sems)
    size = hidden_ref.shape[1]
    second_input = input_ref[...]
    gate = dot(second_input, weight_of(weight_ref, 0, size), ((1,), (0,)))
    upper = dot(second_input, weight_of(weight_ref, size, size), ((1,), (0,)))
    hidden_grad = dot(grad_ref[...], weight_of(weight_ref, 2 * size, size), ((1,), (0,)))
    sigmoid = jax.nn.sigmoid(gate)
    activated = gate * sigmoid
    hidden = (activated * upper).astype(bf16)
    hidden_ref[...] = hidden
    gate_grad = (hidden_grad * upper * sigmoid * (1.0 + gate * (1.0 - sigmoid))).astype(bf16)
    grads_ref[:, :size] = gate_grad
    up_grad = (hidden_grad * activated).astype(bf16)
    grads_ref[:, size:] = up_grad
    result_ref[...] = dot(hidden, weight_of(weight_ref, 2 * size, size), ((1,), (1,))).astype(bf16)
    second = dot(gate_grad, weight_of(weight_ref, 0, size), ((1,), (1,)))
    second += dot(up_grad, weight_of(weight_ref, size, size), ((1,), (1,)))
    unit = unit_ref[...].astype(f32)
    add_sums(sums_ref, second * unit, second)
    back = norm_back(second, unit, inverse_ref[:, 0:1], gain_ref[...]).astype(bf16)
    back_ref[...] = back
    through = dot(back, output_ref[...], ((1,), (1,))).astype(bf16)
    columns = through_ref.shape[2]
    for i in range(through_ref.shape[0]):
        through_ref[i] = through[:, i * columns : (i + 1) * columns]


def feed(second_input, down_grad, unit, inverse, gain, output_all, pieces, rows, n_seq):
    length, width = second_input.shape
    size = pieces[0].shape[2] // 3
    n = len(pieces)
    block = block_of(length)
    full = block_spec(block, width)
    return call_kernel(
        lambda *refs: feed_kernel(n, *refs),
        length,
        [full, full, full, block_spec(block, 128), whole_spec(1, width), once_spec(width, width)]
        + any_specs(n),
        [rows_out(length, size, bf16), rows_out(length, 2 * size, bf16)]
        + [rows_out(length, width, bf16)] * 2
        + [
            (
                jax.ShapeDtypeStruct((n_seq, length, width // n_seq), bf16),
                pl.BlockSpec((n_seq, block, width // n_seq), lambda i: (0, i, 0)),
            ),
            sums_out(width),
        ],
        [
            pltpu.VMEM((pieces[0].shape[0], n, rows, 3 * size), bf16),
            pltpu.SemaphoreType.DMA((n,)),
        ],
        (second_input, down_grad, unit, inverse, gain, output_all, *pieces),
        "feed",
        12 * length * width * size + 2 * length * width * width,
    )


def first_kernel(n, *refs):
    grad_ref, center_ref, gain_ref, back_ref = refs[:4]
    pieces = refs[4 : 4 + n]
    both_ref, sums_ref, bias_ref, weight_ref, sems = refs[4 + n :]
    load_pieces(pieces, weight_ref, sems)
    grad = grad_ref[...]
    first = dot(grad, weight_of(weight_ref, 0, grad.shape[1]), ((1,), (1,)))
    unit, inverse = unit_of(center_ref[...].astype(f32))
    add_sums(sums_ref, first * unit, first)
    add_sums(bias_ref, grad.astype(f32))
    both = back_ref[...].astype(f32) + norm_back(first, unit, inverse, gain_ref[...])
    both_ref[...] = both.astype(bf16)


def first_back(joint_grad, center, gain, back, pieces, rows):
    length, width = center.shape
    total = joint_grad.shape[1]
    n = len(pieces)
    block = block_of(length)
    full = block_spec(block, width)
    return call_kernel(
        lambda *refs: first_kernel(n, *refs),
        length,
        [block_spec(block, total), full, whole_spec(1, width), full] + any_specs(n),
        [rows_out(length, width, bf16), sums_out(width), sums_out(total)],
        [
            pltpu.VMEM((pieces[0].shape[0], n, rows, total), bf16),
            pltpu.SemaphoreType.DMA((n,)),
        ],
        (joint_grad, center, gain, back, *pieces),
        "first_back",
        2 * length * width * total,
    )


def grad_kernel(rows, has_rest, has_below, *refs):
    left_ref, right_ref = refs[:2]
    refs = refs[2:]
    part = dot(left_ref[...], right_ref[...], ((0,), (0,)))
    if has_rest:
        rest_ref, refs = refs[0], refs[1:]
        local = rest_ref.shape[0]
        first = pl.multiple_of(lax.axis_index("seq") * local, local)
        part += dot(left_ref[pl.ds(first, local), :], rest_ref[...], ((0,), (0,)))
    if has_below:
        below_ref, refs = refs[0], refs[1:]
    keep_ref, send_ref, part_ref = refs
    me = lax.axis_index("batch")
    part_ref[...] = part.astype(bf16).reshape(part_ref.shape)
    for far in range(2):
        for near, ref in enumerate((keep_ref, send_ref)):
            batch_at = me ^ (2 * far + near)
            ref[far, 0, :rows] = part_ref[batch_at]
            if has_below:
                ref[far, 0, rows:] = below_ref[0, batch_at]


def weight_grad(left, right, n_seq, n_batch, rest=None, below=None):
    length, width = left.shape
    c = right.shape[1]
    rows = width // (n_seq * n_batch)
    if n_seq != 8 or n_batch != 4:
        if rest is not None:
            first = lax.axis_index("seq") * rest.shape[0]
            mine = lax.dynamic_slice_in_dim(right, first, rest.shape[0], 0) + rest
            right = lax.dynamic_update_slice_in_dim(right, mine, first, 0)
        part = dot(left, right, ((0,), (0,))).astype(bf16).reshape(n_seq, n_batch, rows, c)
        if below is not None:
            part = jnp.concatenate([part, below], axis=2)
        return part, None
    args = [left, right]
    specs = [pl.BlockSpec((length, width // n_seq), lambda i: (0, i)), once_spec(length, c)]
    high = rows
    if rest is not None:
        args.append(rest)
        specs.append(once_spec(*rest.shape))
    if below is not None:
        high += below.shape[2]
        args.append(below)
        specs.append(pl.BlockSpec((1,) + below.shape[1:], lambda i: (i, 0, 0, 0)))
    shape = jax.ShapeDtypeStruct((2, n_seq, high, c), bf16)
    spec = pl.BlockSpec((2, 1, high, c), lambda i: (0, i, 0, 0))
    return pl.pallas_call(
        lambda *refs: grad_kernel(rows, rest is not None, below is not None, *refs),
        grid=(n_seq,),
        in_specs=specs,
        out_specs=[spec, spec],
        out_shape=[shape, shape],
        scratch_shapes=[pltpu.VMEM((n_batch, rows, c), bf16)],
        compiler_params=pltpu.CompilerParams(
            vmem_limit_bytes=VMEM_BYTES, dimension_semantics=("arbitrary",)
        ),
        cost_estimate=pl.CostEstimate(
            flops=2 * length * width * c,
            bytes_accessed=2 * (length * width + length * c + 2 * width * c),
            transcendentals=0,
        ),
        name="weight_grad",
    )(*args)


def grad_near(halves, n_batch):
    keep, send = halves
    if send is None:
        return scatter_near(keep, n_batch), None
    return keep, swap(send, "batch", n_batch, 1)


def grad_far_begin(halves, n_batch):
    keep, got = halves
    if got is None:
        return scatter_far(keep, n_batch), None
    keep, got = keep.astype(f32), got.astype(f32)
    other = swap((keep[1] + got[1]).astype(bf16), "batch", n_batch, 2)
    return (keep[0] + got[0]).astype(bf16), other


def grad_far_end(state):
    keep, other = state
    if other is None:
        return keep
    return (keep.astype(f32) + other.astype(f32)).astype(bf16)


def make_body(n_seq, n_batch):
    def body(
        tokens,
        language,
        language_weight,
        output_grad,
        attention_gain,
        attention_shift,
        joint_weight,
        joint_bias,
        output_weight,
        feedfwd_gain,
        feedfwd_shift,
        gate_weight,
        up_weight,
        down_weight,
    ):
        _, local, width = tokens.shape
        rows, ff_width = gate_weight.shape
        length = local * n_seq
        columns = width // n_seq
        tiles = -(-ff_width // (128 * n_seq))
        ff_local = 128 * tiles
        seq_at = lax.axis_index("seq")
        first_row = seq_at * local
        values = tokens[0]
        tables = [jnp.asarray(t) for t in turn_tables(length)]

        center_own = values - mean_of(values)
        ring = Gather(jnp.concatenate([center_own.astype(bf16), output_weight]), n_seq)

        small = jnp.concatenate(
            [attention_gain, attention_shift, feedfwd_gain, feedfwd_shift, joint_bias]
        )
        small = jnp.pad(small[None], ((0, 15), (0, 3 * columns - small.shape[0])))
        blocks = jnp.transpose(joint_weight.reshape(rows, 3, n_seq, columns), (2, 0, 1, 3))
        blocks = blocks.reshape(n_seq, rows, 3 * columns)
        blocks = jnp.concatenate(
            [blocks, jnp.broadcast_to(small[None], (n_seq,) + small.shape)], axis=1
        )
        ff_blocks = [
            jnp.pad(w, ((0, 0), (0, n_seq * ff_local - ff_width))).reshape(rows, tiles, n_seq, 128)
            for w in (gate_weight, up_weight, down_weight)
        ]
        ff_blocks = jnp.transpose(jnp.stack(ff_blocks, 1), (3, 0, 1, 2, 4))
        ff_blocks = ff_blocks.reshape(n_seq, rows, 3 * ff_local)

        ring.step()
        flight = exchange_begin(blocks, n_seq, 1)
        ff_flight = exchange_begin(ff_blocks, n_seq, 4)
        (flight,) = ring.tie(flight)
        blocks = exchange_end(flight, n_seq, 1)
        ring.step()
        flight = exchange_begin(blocks, n_seq, 2)
        flight, ff_flight = ring.tie(flight, ff_flight)
        blocks = exchange_end(flight, n_seq, 2)
        ff_blocks = rest_of_exchange(exchange_end(ff_flight, n_seq, 4), n_seq)
        ring.step()
        flight = exchange_begin(blocks, n_seq, 4)
        ff_flight = exchange_begin(ff_blocks, n_seq, 1)
        flight, ff_flight = ring.tie(flight, ff_flight)
        blocks = rest_of_exchange(exchange_end(flight, n_seq, 4), n_seq)
        ff_blocks = exchange_end(ff_flight, n_seq, 1)
        ring.step()
        held = gather_far(blocks, n_batch)
        ff_flight = exchange_begin(ff_blocks, n_seq, 2)
        (held_last,) = ring.tie(held[-1][1])
        held[-1] = (held[-1][0], held_last)
        pieces = gather_near(held, n_batch)
        center_pieces = [v for _, v in ring.pieces]
        output_held = jnp.concatenate([v[local:] for v in center_pieces])
        output_held, *pieces = tie(output_held, *pieces)
        output_held = gather_far(output_held, n_batch)

        small = jnp.stack([v[:, rows] for v in pieces], axis=1)
        batch_at = lax.axis_index("batch")
        for bit in bits_of(n_batch):
            flipped = small.reshape(n_seq, -1, 2, bit, small.shape[2])[:, :, ::-1]
            small = jnp.where((batch_at & bit) == 0, small, flipped.reshape(small.shape))
        piece = width // (n_seq * n_batch)

        def small_part(start, size):
            return small[:, :, start : start + size].reshape(1, -1).astype(f32)

        gain_one = small_part(0, piece)
        shift_one = small_part(piece, piece)
        gain_two = small_part(2 * piece, piece)
        shift_two = small_part(3 * piece, piece)
        bias_all = small_part(4 * piece, 3 * piece).reshape(3, n_seq, columns)
        bias = lax.dynamic_slice_in_dim(bias_all, seq_at, 1, 1).reshape(1, 3 * columns)

        chosen = language[:, None] == jnp.arange(LANGS, dtype=jnp.int32)[None, :]
        row_scale = jnp.sum(jnp.where(chosen, language_weight[None, :], 0.0), axis=1)
        cotangent = output_grad[0] * row_scale[:, None]
        down_grad = after(cotangent.astype(bf16), pieces[0])
        down_grad = lax.all_gather(down_grad, "seq", axis=0, tiled=True)

        low, first_input, center = make_heads(
            center_pieces, gain_one, shift_one, bias, tables, pieces, rows, local
        )
        context, mixed, lse = attend(low)

        mixed, held_last, ff_flight = tie(mixed, output_held[-1][1], ff_flight)
        output_held[-1] = (output_held[-1][0], held_last)
        ring = Gather(mixed, n_seq)
        ring.step()
        held = gather_far(exchange_end(ff_flight, n_seq, 2), n_batch)
        ring.tie()
        ring.step()
        output_pieces = gather_near(output_held, n_batch)
        output_pieces = ring.tie(*output_pieces)
        ring.step()
        ring.tie()
        ring.step()
        (held_last,) = ring.tie(held[-1][1])
        held[-1] = (held[-1][0], held_last)
        ff_pieces = gather_near(held, n_batch)
        mixed_pieces = [v for _, v in ring.pieces]
        if columns % 128:
            mixed_pieces = [join(ring.pieces, n_seq, 1)]
        second_input, unit_two, inverse_two, mixed_all, output_all = make_middle(
            mixed_pieces, output_pieces, center, gain_two, shift_two, n_seq, rows
        )
        output_all = output_all.reshape(width, width)

        hidden, middle_grads, result_part, back, through, second_sums = feed(
            second_input,
            down_grad,
            unit_two,
            inverse_two,
            gain_two,
            output_all,
            ff_pieces,
            rows,
            n_seq,
        )
        result_sum = lax.psum_scatter(result_part, "seq", scatter_dimension=0, tiled=True)

        def own(array):
            return lax.dynamic_slice_in_dim(array, first_row, local, 0)

        ring = Scatter(lambda at: lax.dynamic_index_in_dim(through, at, 0, False), n_seq)
        ring.step()
        grad_down = grad_near(weight_grad(down_grad, hidden, n_seq, n_batch), n_batch)
        (grad_down,) = ring.tie(grad_down)
        ring.step()
        grad_down = grad_far_begin(grad_down, n_batch)
        grad_both = weight_grad(second_input, middle_grads, n_seq, n_batch)
        grad_both, grad_down = ring.tie(grad_both, grad_down)
        ring.step()
        grad_both = grad_near(grad_both, n_batch)
        grad_down = exchange_begin(grad_far_end(grad_down), n_seq, 4)
        grad_output = weight_grad(
            mixed_all, back, n_seq, n_batch, rest=cotangent.astype(bf16)
        )
        grad_both, grad_output = ring.tie(grad_both, grad_output)
        ring.step()
        grad_both = grad_far_begin(grad_both, n_batch)
        grad_output = grad_near(grad_output, n_batch)
        heads_weight = lax.dynamic_slice_in_dim(output_all, seq_at * columns, columns, 0)
        from_cot = dot(down_grad, heads_weight, ((1,), (1,)))
        from_cot, grad_output, grad_down = ring.tie(from_cot, grad_output, grad_down)
        context_grad = (ring.total() + from_cot).astype(bf16)
        grad_down = rest_of_exchange(exchange_end(grad_down, n_seq, 4), n_seq)
        grad_down = exchange_begin(grad_down, n_seq, 1)
        joint_grad = attend_back(low, context_grad, context, lse, tables)
        joint_grad, grad_both, grad_down = tie(joint_grad, grad_both, grad_down)
        grad_output = grad_far_begin(grad_output, n_batch)
        grad_both = exchange_begin(grad_far_end(grad_both), n_seq, 4)
        grad_down = exchange_begin(exchange_end(grad_down, n_seq, 1), n_seq, 2)
        both, first_sums, bias_sums = first_back(joint_grad, center, gain_one, back, pieces, rows)

        ring = Scatter(lambda at: lax.dynamic_slice_in_dim(both, at * local, local, 0), n_seq)
        ring.step()
        bias_part = lax.dynamic_update_slice_in_dim(
            jnp.zeros((3, n_seq, columns), f32), bias_sums[:1].reshape(3, 1, columns), seq_at, 1
        )
        vectors = [first_sums[0], first_sums[1], second_sums[0], second_sums[1], bias_part]
        vectors = [v.reshape(n_seq, n_batch, 1, -1).astype(bf16) for v in vectors]
        vectors = jnp.concatenate(vectors, axis=3)
        vectors = jnp.pad(vectors, ((0, 0), (0, 0), (0, 15), (0, 3 * columns - 7 * piece)))
        grad_joint = weight_grad(first_input, joint_grad, n_seq, n_batch, below=vectors)
        grad_joint, grad_both, grad_down = ring.tie(grad_joint, grad_both, grad_down)
        ring.step()
        grad_joint = grad_near(grad_joint, n_batch)
        grad_both = rest_of_exchange(exchange_end(grad_both, n_seq, 4), n_seq)
        grad_both = exchange_begin(grad_both, n_seq, 1)
        grad_down = exchange_end(grad_down, n_seq, 2)
        projected_own = dot(own(mixed_all), output_all, ((1,), (0,)))
        result = values + projected_own + result_sum.astype(f32)
        grad_joint, grad_output, result = ring.tie(grad_joint, grad_output, result)
        grad_output = lax.psum_scatter(
            grad_far_end(grad_output), "seq", scatter_dimension=0, tiled=False
        )
        ring.step()
        grad_joint = grad_far_begin(grad_joint, n_batch)
        grad_joint, grad_both = ring.tie(grad_joint, grad_both)
        ring.step()
        grad_joint = exchange_begin(grad_far_end(grad_joint), n_seq, 1)
        grad_both = exchange_begin(exchange_end(grad_both, n_seq, 1), n_seq, 2)
        (grad_joint,) = ring.tie(grad_joint)
        grad_joint = exchange_far(exchange_end(grad_joint, n_seq, 1), n_seq)
        grad_both = exchange_end(grad_both, n_seq, 2)
        token_grad = cotangent + ring.total()
        grad_output = grad_output.astype(f32)

        def unsplit(grad):
            grad = grad.reshape(n_seq, rows, tiles, 128).astype(f32)
            return jnp.transpose(grad, (1, 2, 0, 3)).reshape(rows, n_seq * ff_local)[:, :ff_width]

        grad_gate = unsplit(grad_both[:, :, :ff_local])
        grad_up = unsplit(grad_both[:, :, ff_local:])
        grad_down = unsplit(grad_down)
        grad_joint = grad_joint.astype(f32)
        vectors = jnp.sum(grad_joint[:, rows], axis=0)
        grad_joint = grad_joint[:, :rows].reshape(n_seq, rows, 3, columns)
        grad_joint = jnp.transpose(grad_joint, (1, 2, 0, 3)).reshape(rows, 3 * width)
        return (
            result[None],
            token_grad[None],
            vectors[:piece],
            vectors[piece : 2 * piece],
            grad_joint,
            vectors[4 * piece : 7 * piece],
            grad_output,
            vectors[2 * piece : 3 * piece],
            vectors[3 * piece : 4 * piece],
            grad_gate,
            grad_up,
            grad_down,
        )

    return body


def solution(mesh):
    rows = P(("seq", "batch"))
    matrix = P(("seq", "batch"), None)
    data = P("batch", "seq", None)
    return jax.shard_map(
        make_body(mesh.shape["seq"], mesh.shape["batch"]),
        mesh=mesh,
        in_specs=(
            data,
            P("batch"),
            P(),
            data,
            rows,
            rows,
            matrix,
            rows,
            matrix,
            rows,
            rows,
            matrix,
            matrix,
            matrix,
        ),
        out_specs=(data, data, rows, rows, matrix, rows, matrix, rows, rows, matrix, matrix, matrix),
        check_vma=False,
    )
```

```python
import math

import numpy as np

import jax
import jax.numpy as jnp
from jax import lax
from jax.experimental import pallas as pl
from jax.experimental.pallas import tpu as pltpu
from jax.sharding import PartitionSpec as P

HEADS = 32
HEAD_DIM = 64
ROT_DIMS = 16
LANGS = 7

EPSILON = 1e-05
THETA_BASE = 10000.0
NEGATIVE = -1e30
VMEM_BYTES = 56 * 1024 * 1024
GRAD_BLOCKS = 2

bf16 = jnp.bfloat16
f32 = jnp.float32


def swap(value, axis, number, bit):
    return lax.ppermute(value, axis, [(i, i ^ bit) for i in range(number)])


def bits_of(number):
    return [1 << i for i in range(number.bit_length() - 1)]


def tie(*values):
    return lax.optimization_barrier(values)


def after(value, *others):
    return tie(value, *others)[0]


def exchange_begin(blocks, number, bit):
    mine = (lax.axis_index("seq") // bit) % 2
    pairs = blocks.reshape((number // (2 * bit), 2, bit) + blocks.shape[1:])
    return pairs, swap(lax.dynamic_slice_in_dim(pairs, 1 - mine, 1, 1), "seq", number, bit)


def exchange_end(state, number, bit):
    pairs, got = state
    mine = (lax.axis_index("seq") // bit) % 2
    out = lax.dynamic_update_slice_in_dim(pairs, got, 1 - mine, 1)
    return out.reshape((number,) + pairs.shape[3:])


def exchange(blocks, number, bit):
    return exchange_end(exchange_begin(blocks, number, bit), number, bit)


def exchange_far(blocks, number):
    for bit in bits_of(number)[1:]:
        blocks = exchange(blocks, number, bit)
    return blocks


def exchange_parts(blocks):
    place = lax.axis_index("seq") // 2
    pairs = blocks.reshape((4, 2) + blocks.shape[1:])
    return [
        swap(lax.dynamic_slice_in_dim(pairs, place ^ k, 1, 0), "seq", 8, k * 2)[0]
        for k in range(1, 4)
    ]


def rest_of_exchange(blocks, number):
    for bit in bits_of(number)[3:]:
        blocks = exchange(blocks, number, bit)
    return blocks


def gather_far(value, number):
    held = [(0, value)]
    for bit in reversed(bits_of(number)[1:]):
        held = held + [(k ^ bit, swap(v, "batch", number, bit)) for k, v in held]
    return held


def gather_near(held, number):
    held = dict(held + [(k ^ 1, swap(v, "batch", number, 1)) for k, v in held])
    return [held[k] for k in range(number)]


def scatter_stage(value, number, bit):
    n, _, r, c = value.shape
    pairs = value.reshape(n, -1, 2, r, c)
    mine = (lax.axis_index("batch") // bit) % 2
    keep = lax.dynamic_index_in_dim(pairs, mine, 2, False)
    send = lax.dynamic_index_in_dim(pairs, 1 - mine, 2, False).astype(bf16)
    return (keep.astype(f32) + swap(send, "batch", number, bit).astype(f32)).astype(bf16)


def scatter_near(value, number):
    return scatter_stage(value, number, 1)


def scatter_far(value, number):
    for bit in bits_of(number)[1:]:
        value = scatter_stage(value, number, bit)
    return value[:, 0]


RING = (0, 2, 4, 6, 7, 5, 3, 1)


def ring_place():
    s = lax.axis_index("seq")
    return jnp.where(s % 2 == 0, s // 2, 7 - s // 2)


def ring_index(place):
    place = (place + 16) % 8
    return jnp.where(place < 4, 2 * place, 15 - 2 * place)


ARRIVAL = (0, 1, -1, 2, -2, 3, -3, -4)


def arrival(number):
    if number != 8:
        return list(range(number))
    return [ring_index(ring_place() + step) for step in ARRIVAL]


def ring_step(value, way):
    return lax.ppermute(value, "seq", [(RING[i], RING[(i + way) % 8]) for i in range(8)])


class Ring:
    ahead = behind = None
    taken = 0

    def tie(self, *others):
        if self.number != 8:
            return others
        self.ahead, self.behind, *others = tie(self.ahead, self.behind, *others)
        return others


class Gather(Ring):
    def __init__(self, value, number):
        self.number = number
        if number != 8:
            every = lax.all_gather(value, "seq", axis=0, tiled=False)
            self.pieces = [(i, every[i]) for i in range(number)]
            return
        self.pieces = [(lax.axis_index("seq"), value)]
        self.ahead = self.behind = value
        self.place = ring_place()

    def step(self):
        if self.number != 8:
            return
        self.taken += 1
        k = self.taken
        self.ahead = ring_step(self.ahead, 1)
        if k < 4:
            self.behind = ring_step(self.behind, -1)
            self.pieces.append((ring_index(self.place + k), self.behind))
        self.pieces.append((ring_index(self.place - k), self.ahead))


class Scatter(Ring):
    def __init__(self, block, number):
        self.number = number
        self.block = block
        self.place = ring_place()

    def step(self):
        if self.number != 8:
            return
        k = 4 - self.taken
        self.taken += 1
        part = self.block(ring_index(self.place + k))
        if self.ahead is not None:
            part = (part.astype(f32) + self.ahead.astype(f32)).astype(bf16)
        self.ahead = ring_step(part, 1)
        if k > 1:
            part = self.block(ring_index(self.place - k + 1))
            if self.behind is not None:
                part = (part.astype(f32) + self.behind.astype(f32)).astype(bf16)
            self.behind = ring_step(part, -1)

    def total(self):
        if self.number != 8:
            every = jnp.stack([self.block(i) for i in range(self.number)])
            return lax.psum_scatter(every, "seq", scatter_dimension=0, tiled=False).astype(f32)
        own = self.block(lax.axis_index("seq"))
        return own.astype(f32) + self.ahead.astype(f32) + self.behind.astype(f32)


def join(pieces, number, axis):
    at, first = pieces[0]
    size = first.shape[axis]
    shape = first.shape[:axis] + (number * size,) + first.shape[axis + 1 :]
    out = jnp.zeros(shape, first.dtype)
    for at, piece in pieces:
        out = lax.dynamic_update_slice_in_dim(out, piece, at * size, axis)
    return out


def turn_tables(length):
    half = ROT_DIMS // 2
    frequency = THETA_BASE ** (-np.arange(half, dtype=np.float32) / np.float32(half))
    angle = (np.arange(length, dtype=np.float32)[:, None] * frequency.astype(np.float32)[None]).astype(
        np.float32
    )
    cosine = np.ones((length, HEAD_DIM), np.float32)
    left = np.zeros((length, HEAD_DIM), np.float32)
    right = np.zeros((length, HEAD_DIM), np.float32)
    cosine[:, :half] = np.cos(angle)
    cosine[:, half:ROT_DIMS] = np.cos(angle)
    left[:, :half] = -np.sin(angle)
    right[:, half:ROT_DIMS] = np.sin(angle)
    return [np.concatenate([t, t], 1) for t in (cosine, left, right)]


def wide(table, columns):
    if columns < table.shape[1]:
        return table[:, :columns]
    return jnp.concatenate([table] * (columns // table.shape[1]), axis=1)


def lane_roll(value, amount):
    columns = value.shape[1]
    if columns % 128 == 0:
        return pltpu.roll(value, amount % columns, 1)
    amount = amount % columns
    return jnp.concatenate([value[:, columns - amount :], value[:, : columns - amount]], axis=1)


def turn(value, cosine, left, right):
    half = ROT_DIMS // 2
    return value * cosine + lane_roll(value, -half) * left + lane_roll(value, half) * right


def turn_back(value, cosine, left, right):
    half = ROT_DIMS // 2
    return value * cosine - lane_roll(value, -half) * left - lane_roll(value, half) * right


def head_mask(columns, head):
    lane = lax.broadcasted_iota(jnp.int32, (1, columns), 1)
    return (lane >= head * HEAD_DIM) & (lane < (head + 1) * HEAD_DIM)


def block_of(length):
    return math.gcd(length, 256)


def attend_kernel(low_ref, context_ref, mixed_ref, lse_ref):
    length, total = low_ref.shape
    columns = total // 3
    heads = columns // HEAD_DIM
    block = block_of(length)
    for i in range(length // block):
        rows = pl.ds(i * block, block)
        reach = (i + 1) * block
        query = low_ref[rows, 0:columns]
        key = low_ref[0:reach, columns : 2 * columns]
        value = low_ref[0:reach, 2 * columns :]
        total_out = jnp.zeros((block, columns), f32)
        lse_all = jnp.zeros((block, 128), f32)
        lane = lax.broadcasted_iota(jnp.int32, (block, 128), 1)
        ahead = lax.broadcasted_iota(jnp.int32, (block, reach), 1) > (
            i * block + lax.broadcasted_iota(jnp.int32, (block, reach), 0)
        )
        for h in range(heads):
            mask = head_mask(columns, h)
            scores = lax.dot_general(
                jnp.where(mask, query, jnp.zeros_like(query)),
                key,
                (((1,), (1,)), ((), ())),
                preferred_element_type=f32,
            )
            scores = jnp.where(ahead, NEGATIVE, scores)
            top = jnp.max(scores, axis=1, keepdims=True)
            weight = jnp.exp(scores - top)
            denominator = jnp.sum(weight, axis=1, keepdims=True)
            probs = (weight * (1.0 / denominator)).astype(bf16)
            total_out += jnp.dot(
                probs, jnp.where(mask, value, jnp.zeros_like(value)), preferred_element_type=f32
            )
            lse_all = jnp.where(lane == h, top + jnp.log(denominator), lse_all)
        context_ref[rows, :] = total_out
        mixed_ref[rows, :] = total_out.astype(bf16)
        lse_ref[rows, :] = lse_all


def attend(low):
    length, total = low.shape
    columns = total // 3
    return pl.pallas_call(
        attend_kernel,
        out_shape=(
            jax.ShapeDtypeStruct((length, columns), f32),
            jax.ShapeDtypeStruct((length, columns), bf16),
            jax.ShapeDtypeStruct((length, 128), f32),
        ),
        compiler_params=pltpu.CompilerParams(vmem_limit_bytes=VMEM_BYTES),
        cost_estimate=pl.CostEstimate(
            flops=4 * length * length * columns * 2,
            bytes_accessed=16 * length * total,
            transcendentals=length * length * columns // HEAD_DIM,
        ),
        name="attend",
    )(low)


def attend_back_kernel(
    low_ref, grad_ref, context_ref, lse_ref, cos_ref, left_ref, right_ref, out_ref, dq_ref, dk_ref, dv_ref
):
    length, total = low_ref.shape
    columns = total // 3
    heads = columns // HEAD_DIM
    block = block_of(length)
    scale = 1.0 / math.sqrt(HEAD_DIM)
    dk_ref[...] = jnp.zeros_like(dk_ref)
    dv_ref[...] = jnp.zeros_like(dv_ref)
    for i in range(length // block):
        rows = pl.ds(i * block, block)
        reach = (i + 1) * block
        query = low_ref[rows, 0:columns]
        grad = grad_ref[rows, :]
        grad_wide = grad.astype(f32)
        query_t = query.astype(f32).T.astype(bf16)
        grad_t = grad_wide.T.astype(bf16)
        product = grad_wide * context_ref[rows, :]
        key = low_ref[0:reach, columns : 2 * columns]
        value = low_ref[0:reach, 2 * columns :]
        dq = jnp.zeros((block, columns), f32)
        ahead = lax.broadcasted_iota(jnp.int32, (block, reach), 1) > (
            i * block + lax.broadcasted_iota(jnp.int32, (block, reach), 0)
        )
        for h in range(heads):
            mask = head_mask(columns, h)
            span = slice(h * HEAD_DIM, (h + 1) * HEAD_DIM)
            scores = lax.dot_general(
                jnp.where(mask, query, jnp.zeros_like(query)),
                key,
                (((1,), (1,)), ((), ())),
                preferred_element_type=f32,
            )
            scores = jnp.where(ahead, NEGATIVE, scores)
            probs = jnp.exp(scores - lse_ref[rows, h : h + 1])
            dots = lax.dot_general(
                jnp.where(mask, grad, jnp.zeros_like(grad)),
                value,
                (((1,), (1,)), ((), ())),
                preferred_element_type=f32,
            )
            balance = jnp.sum(jnp.where(mask, product, 0.0), axis=1, keepdims=True)
            score_grad = (probs * (dots - balance)).astype(bf16)
            dq += jnp.dot(
                score_grad, jnp.where(mask, key, jnp.zeros_like(key)), preferred_element_type=f32
            )
            dk_ref[span, 0:reach] += jnp.dot(query_t[span], score_grad, preferred_element_type=f32)
            dv_ref[span, 0:reach] += jnp.dot(
                grad_t[span], probs.astype(bf16), preferred_element_type=f32
            )
        dq_ref[rows, :] = dq
    for i in range(length // block):
        rows = pl.ds(i * block, block)
        tables = [wide(t[rows, :], columns) for t in (cos_ref, left_ref, right_ref)]
        out_ref[rows, 0:columns] = turn_back(dq_ref[rows, :] * scale, *tables).astype(bf16)
        out_ref[rows, columns : 2 * columns] = turn_back(dk_ref[:, rows].T, *tables).astype(bf16)
        out_ref[rows, 2 * columns :] = dv_ref[:, rows].T.astype(bf16)


def attend_back(low, grad, context, lse, tables):
    length, total = low.shape
    columns = total // 3
    return pl.pallas_call(
        attend_back_kernel,
        out_shape=jax.ShapeDtypeStruct((length, total), bf16),
        scratch_shapes=[
            pltpu.VMEM((length, columns), f32),
            pltpu.VMEM((columns, length), f32),
            pltpu.VMEM((columns, length), f32),
        ],
        compiler_params=pltpu.CompilerParams(vmem_limit_bytes=VMEM_BYTES),
        cost_estimate=pl.CostEstimate(
            flops=10 * length * length * columns * 2,
            bytes_accessed=16 * length * total,
            transcendentals=length * length * columns // HEAD_DIM,
        ),
        name="attend_back",
    )(low, grad, context, lse, *tables)


def mean_of(values):
    return jnp.mean(values, axis=-1, keepdims=True)


def unit_of(values):
    center = values - mean_of(values)
    inverse_std = lax.rsqrt(mean_of(center * center) + EPSILON)
    return center * inverse_std, inverse_std


def unit_of_centered(center):
    inverse_std = lax.rsqrt(mean_of(center * center) + EPSILON)
    return center * inverse_std, inverse_std


def norm_back(incoming, unit_rows, inverse_std, gain_values):
    inner = incoming * gain_values
    return inverse_std * (inner - mean_of(inner) - unit_rows * mean_of(inner * unit_rows))


def dot(left, right, contract):
    return lax.dot_general(left, right, (contract, ((), ())), preferred_element_type=f32)


def block_spec(block, columns):
    return pl.BlockSpec((block, columns), lambda i: (i, 0))


def whole_spec(rows, columns):
    return pl.BlockSpec((rows, columns), lambda i: (0, 0))


def once_spec(rows, columns):
    return pl.BlockSpec((rows, columns), lambda i: (0, 0), pipeline_mode=pl.Buffered(1))


def any_specs(number):
    return [pl.BlockSpec(memory_space=pl.ANY)] * number


def run_copies(copies, sems):
    copies = [pltpu.make_async_copy(*pair, sems.at[i]) for i, pair in enumerate(copies)]
    for copy in copies:
        copy.start()
    for copy in copies:
        copy.wait()


def weight_copies(piece_refs, weight_ref):
    me = lax.axis_index("batch")
    rows = weight_ref.shape[2]
    return [
        (ref.at[:, pl.ds(0, rows), :], weight_ref.at[:, me ^ k])
        for k, ref in enumerate(piece_refs)
    ]


def load_pieces(piece_refs, weight_ref, sems):
    @pl.when(pl.program_id(0) == 0)
    def _():
        run_copies(weight_copies(piece_refs, weight_ref), sems)


def weight_of(weight_ref, start, size):
    part = weight_ref[:, :, :, start : start + size]
    return part.reshape(-1, size)


def call_kernel(kernel, length, in_specs, out, scratch, args, name, flops):
    block = block_of(length)
    return pl.pallas_call(
        kernel,
        grid=(length // block,),
        in_specs=in_specs,
        out_specs=[spec for _, spec in out],
        out_shape=[shape for shape, _ in out],
        scratch_shapes=scratch,
        compiler_params=pltpu.CompilerParams(
            vmem_limit_bytes=VMEM_BYTES, dimension_semantics=("arbitrary",)
        ),
        cost_estimate=pl.CostEstimate(
            flops=flops, bytes_accessed=flops // 500, transcendentals=0
        ),
        name=name,
    )(*args)


def rows_out(length, columns, kind):
    return (jax.ShapeDtypeStruct((length, columns), kind), block_spec(block_of(length), columns))


def sums_out(columns):
    return (jax.ShapeDtypeStruct((8, columns), f32), whole_spec(8, columns))


def add_sums(ref, *rows):
    @pl.when(pl.program_id(0) == 0)
    def _():
        ref[...] = jnp.zeros_like(ref)

    for i, row in enumerate(rows):
        ref[i : i + 1, :] += jnp.sum(row, axis=0, keepdims=True)


def heads_kernel(n, n_seq, *refs):
    gain_ref, shift_ref, bias_ref, cos_ref, left_ref, right_ref = refs[:6]
    pieces = refs[6 : 6 + n]
    center_pieces = refs[6 + n : 6 + n + n_seq]
    low_ref, input_ref, center_ref, weight_ref, all_ref, sems = refs[6 + n + n_seq :]
    local = all_ref.shape[1]

    @pl.when(pl.program_id(0) == 0)
    def _():
        copies = [
            (ref.at[pl.ds(0, local), :], all_ref.at[at])
            for at, ref in zip(arrival(n_seq), center_pieces)
        ]
        run_copies(copies + weight_copies(pieces, weight_ref), sems)

    total = low_ref.shape[1]
    columns = total // 3
    block, width = center_ref.shape
    many = block // local
    center = all_ref[pl.ds(pl.program_id(0) * many, many)].reshape(block, width)
    center_ref[...] = center
    unit, _ = unit_of_centered(center.astype(f32))
    first_input = (unit * gain_ref[...] + shift_ref[...]).astype(bf16)
    input_ref[...] = first_input
    joint = dot(first_input, weight_of(weight_ref, 0, total), ((1,), (0,))) + bias_ref[...]
    tables = [wide(t[...], columns) for t in (cos_ref, left_ref, right_ref)]
    scale = 1.0 / math.sqrt(HEAD_DIM)
    query = turn(joint[:, :columns], *tables).astype(bf16)
    low_ref[:, :columns] = (query.astype(f32) * scale).astype(bf16)
    low_ref[:, columns : 2 * columns] = turn(joint[:, columns : 2 * columns], *tables).astype(bf16)
    low_ref[:, 2 * columns :] = joint[:, 2 * columns :].astype(bf16)


def make_heads(center_pieces, gain, shift, bias, tables, pieces, rows, local):
    n_seq, n = len(center_pieces), len(pieces)
    length, width = local * n_seq, gain.shape[1]
    total = bias.shape[1]
    block = block_of(length)
    return call_kernel(
        lambda *refs: heads_kernel(n, n_seq, *refs),
        length,
        [whole_spec(1, width), whole_spec(1, width), whole_spec(1, total)]
        + [block_spec(block, 128)] * 3
        + any_specs(n + n_seq),
        [
            rows_out(length, total, bf16),
            rows_out(length, width, bf16),
            rows_out(length, width, bf16),
        ],
        [
            pltpu.VMEM((n_seq, n, rows, total), bf16),
            pltpu.VMEM((n_seq, local, width), bf16),
            pltpu.SemaphoreType.DMA((n + n_seq,)),
        ],
        (gain, shift, bias, *tables, *pieces, *center_pieces),
        "make_heads",
        2 * length * width * total,
    )


def middle_kernel(n, n_seq, many, *refs):
    center_ref, gain_ref, shift_ref = refs[:3]
    pieces, mixed_pieces = refs[3 : 3 + n], refs[3 + n : 3 + n + many]
    input_ref, unit_ref, inverse_ref, mixed_ref, out_ref = refs[3 + n + many : 8 + n + many]
    weight_ref, all_ref, sems, out_sem = refs[8 + n + many :]
    rows, width = weight_ref.shape[2:]
    columns = width // n_seq
    step = pl.program_id(0)
    give = pltpu.make_async_copy(weight_ref, out_ref, out_sem)

    @pl.when(step == 0)
    def _():
        me = lax.axis_index("batch")
        places = arrival(n_seq)
        copies = [
            (ref.at[pl.ds(j * rows, rows), :], weight_ref.at[at, me ^ k])
            for k, ref in enumerate(pieces)
            for j, at in enumerate(places)
        ]
        if many == 1:
            copies.append((mixed_pieces[0], all_ref))
        else:
            for at, ref in zip(places, mixed_pieces):
                span = pl.ds(pl.multiple_of(at * columns, columns), columns)
                copies.append((ref, all_ref.at[:, span]))
        run_copies(copies, sems)
        give.start()

    block = center_ref.shape[0]
    mixed = all_ref[pl.ds(pl.multiple_of(step * block, block), block), :]
    mixed_ref[...] = mixed
    projected = dot(mixed, weight_ref[...].reshape(width, width), ((1,), (0,)))
    unit, inverse = unit_of(center_ref[...].astype(f32) + projected)
    input_ref[...] = (unit * gain_ref[...] + shift_ref[...]).astype(bf16)
    unit_ref[...] = unit.astype(bf16)
    inverse_ref[...] = jnp.broadcast_to(inverse, inverse_ref.shape)

    @pl.when(step == pl.num_programs(0) - 1)
    def _():
        give.wait()


def make_middle(mixed_pieces, pieces, center, gain, shift, n_seq, rows):
    length, width = center.shape
    n, many = len(pieces), len(mixed_pieces)
    block = block_of(length)
    row = whole_spec(1, width)
    weight_shape = (n_seq, n, rows, width)
    return call_kernel(
        lambda *refs: middle_kernel(n, n_seq, many, *refs),
        length,
        [block_spec(block, width), row, row] + any_specs(n + many),
        [
            rows_out(length, width, bf16),
            rows_out(length, width, bf16),
            rows_out(length, 128, f32),
            rows_out(length, width, bf16),
            (jax.ShapeDtypeStruct(weight_shape, bf16), pl.BlockSpec(memory_space=pl.ANY)),
        ],
        [
            pltpu.VMEM(weight_shape, bf16),
            pltpu.VMEM((length, width), bf16),
            pltpu.SemaphoreType.DMA((n * n_seq + many,)),
            pltpu.SemaphoreType.DMA,
        ],
        (center, gain, shift, *pieces, *mixed_pieces),
        "make_middle",
        2 * length * width * width,
    )


def feed_kernel(n, *refs):
    input_ref = refs[0]
    pieces = refs[1 : 1 + n]
    gate_ref, upper_ref, hidden_ref, result_ref, weight_ref, sems = refs[1 + n :]
    load_pieces(pieces, weight_ref, sems)
    size = hidden_ref.shape[1]
    second_input = input_ref[...]
    gate = dot(second_input, weight_of(weight_ref, 0, size), ((1,), (0,)))
    upper = dot(second_input, weight_of(weight_ref, size, size), ((1,), (0,)))
    gate_ref[...] = gate
    upper_ref[...] = upper
    hidden = (gate * jax.nn.sigmoid(gate) * upper).astype(bf16)
    hidden_ref[...] = hidden
    result_ref[...] = dot(hidden, weight_of(weight_ref, 2 * size, size), ((1,), (1,))).astype(bf16)


def feed(second_input, pieces, rows):
    length, width = second_input.shape
    size = pieces[0].shape[2] // 3
    n = len(pieces)
    return call_kernel(
        lambda *refs: feed_kernel(n, *refs),
        length,
        [block_spec(block_of(length), width)] + any_specs(n),
        [rows_out(length, size, f32)] * 2
        + [rows_out(length, size, bf16), rows_out(length, width, bf16)],
        [
            pltpu.VMEM((pieces[0].shape[0], n, rows, 3 * size), bf16),
            pltpu.SemaphoreType.DMA((n,)),
        ],
        (second_input, *pieces),
        "feed",
        6 * length * width * size,
    )


def feed_back_kernel(n, *refs):
    gate_ref, upper_ref, grad_ref, unit_ref, inverse_ref, gain_ref, output_ref = refs[:7]
    pieces = refs[7 : 7 + n]
    grads_ref, back_ref, through_ref, sums_ref, weight_ref, sems = refs[7 + n :]
    load_pieces(pieces, weight_ref, sems)
    size = gate_ref.shape[1]
    gate = gate_ref[...]
    upper = upper_ref[...]
    hidden_grad = dot(grad_ref[...], weight_of(weight_ref, 2 * size, size), ((1,), (0,)))
    sigmoid = jax.nn.sigmoid(gate)
    gate_grad = (hidden_grad * upper * sigmoid * (1.0 + gate * (1.0 - sigmoid))).astype(bf16)
    grads_ref[:, :size] = gate_grad
    up_grad = (hidden_grad * (gate * sigmoid)).astype(bf16)
    grads_ref[:, size:] = up_grad
    second = dot(gate_grad, weight_of(weight_ref, 0, size), ((1,), (1,)))
    second += dot(up_grad, weight_of(weight_ref, size, size), ((1,), (1,)))
    unit = unit_ref[...].astype(f32)
    add_sums(sums_ref, second * unit, second)
    back = norm_back(second, unit, inverse_ref[:, 0:1], gain_ref[...]).astype(bf16)
    back_ref[...] = back
    through = dot(back, output_ref[...], ((1,), (1,))).astype(bf16)
    columns = through_ref.shape[2]
    for i in range(through_ref.shape[0]):
        through_ref[i] = through[:, i * columns : (i + 1) * columns]


def feed_back(gate, upper, down_grad, unit, inverse, gain, output_all, pieces, rows, n_seq):
    length, width = down_grad.shape
    size = gate.shape[1]
    n = len(pieces)
    block = block_of(length)
    half = block_spec(block, size)
    full = block_spec(block, width)
    return call_kernel(
        lambda *refs: feed_back_kernel(n, *refs),
        length,
        [
            half,
            half,
            full,
            full,
            block_spec(block, 128),
            whole_spec(1, width),
            once_spec(width, width),
        ]
        + any_specs(n),
        [
            rows_out(length, 2 * size, bf16),
            rows_out(length, width, bf16),
            (
                jax.ShapeDtypeStruct((n_seq, length, width // n_seq), bf16),
                pl.BlockSpec((n_seq, block, width // n_seq), lambda i: (0, i, 0)),
            ),
            sums_out(width),
        ],
        [
            pltpu.VMEM((pieces[0].shape[0], n, rows, 3 * size), bf16),
            pltpu.SemaphoreType.DMA((n,)),
        ],
        (gate, upper, down_grad, unit, inverse, gain, output_all, *pieces),
        "feed_back",
        6 * length * width * size + 2 * length * width * width,
    )


def first_kernel(n, *refs):
    grad_ref, center_ref, gain_ref, back_ref = refs[:4]
    pieces = refs[4 : 4 + n]
    both_ref, sums_ref, bias_ref, weight_ref, sems = refs[4 + n :]
    load_pieces(pieces, weight_ref, sems)
    grad = grad_ref[...]
    first = dot(grad, weight_of(weight_ref, 0, grad.shape[1]), ((1,), (1,)))
    unit, inverse = unit_of_centered(center_ref[...].astype(f32))
    add_sums(sums_ref, first * unit, first)
    add_sums(bias_ref, grad.astype(f32))
    both = back_ref[...].astype(f32) + norm_back(first, unit, inverse, gain_ref[...])
    both_ref[...] = both.astype(bf16)


def first_back(joint_grad, center, gain, back, pieces, rows):
    length, width = center.shape
    total = joint_grad.shape[1]
    n = len(pieces)
    block = block_of(length)
    full = block_spec(block, width)
    return call_kernel(
        lambda *refs: first_kernel(n, *refs),
        length,
        [block_spec(block, total), full, whole_spec(1, width), full] + any_specs(n),
        [rows_out(length, width, bf16), sums_out(width), sums_out(total)],
        [
            pltpu.VMEM((pieces[0].shape[0], n, rows, total), bf16),
            pltpu.SemaphoreType.DMA((n,)),
        ],
        (joint_grad, center, gain, back, *pieces),
        "first_back",
        2 * length * width * total,
    )


def grad_kernel(rows, has_rest, has_below, *refs):
    left_ref, right_ref = refs[:2]
    refs = refs[2:]
    part = dot(left_ref[...], right_ref[...], ((0,), (0,)))
    if has_rest:
        rest_ref, refs = refs[0], refs[1:]
        local = rest_ref.shape[0]
        first = pl.multiple_of(lax.axis_index("seq") * local, local)
        part += dot(left_ref[pl.ds(first, local), :], rest_ref[...], ((0,), (0,)))
    if has_below:
        below_ref, refs = refs[0], refs[1:]
    keep_ref, send_ref, part_ref = refs
    me = lax.axis_index("batch")
    part_ref[...] = part.astype(bf16).reshape(part_ref.shape)
    for far in range(2):
        for near, ref in enumerate((keep_ref, send_ref)):
            batch_at = me ^ (2 * far + near)
            for i in range(part_ref.shape[0]):
                ref[far, i, :rows] = part_ref[i, batch_at]
                if has_below:
                    ref[far, i, rows:] = below_ref[i, batch_at]


def weight_grad(left, right, n_seq, n_batch, rest=None, below=None):
    length, width = left.shape
    c = right.shape[1]
    rows = width // (n_seq * n_batch)
    if n_seq != 8 or n_batch != 4:
        if rest is not None:
            first = lax.axis_index("seq") * rest.shape[0]
            mine = lax.dynamic_slice_in_dim(right, first, rest.shape[0], 0) + rest
            right = lax.dynamic_update_slice_in_dim(right, mine, first, 0)
        part = dot(left, right, ((0,), (0,))).astype(bf16).reshape(n_seq, n_batch, rows, c)
        if below is not None:
            part = jnp.concatenate([part, below], axis=2)
        return part, None
    args = [left, right]
    many = GRAD_BLOCKS
    specs = [pl.BlockSpec((length, many * width // n_seq), lambda i: (0, i)), once_spec(length, c)]
    high = rows
    if rest is not None:
        args.append(rest)
        specs.append(once_spec(*rest.shape))
    if below is not None:
        high += below.shape[2]
        args.append(below)
        specs.append(pl.BlockSpec((many,) + below.shape[1:], lambda i: (i, 0, 0, 0)))
    shape = jax.ShapeDtypeStruct((2, n_seq, high, c), bf16)
    spec = pl.BlockSpec((2, many, high, c), lambda i: (0, i, 0, 0))
    return pl.pallas_call(
        lambda *refs: grad_kernel(rows, rest is not None, below is not None, *refs),
        grid=(n_seq // many,),
        in_specs=specs,
        out_specs=[spec, spec],
        out_shape=[shape, shape],
        scratch_shapes=[pltpu.VMEM((many, n_batch, rows, c), bf16)],
        compiler_params=pltpu.CompilerParams(
            vmem_limit_bytes=VMEM_BYTES, dimension_semantics=("arbitrary",)
        ),
        cost_estimate=pl.CostEstimate(
            flops=2 * length * width * c,
            bytes_accessed=2 * (length * width + length * c + 2 * width * c),
            transcendentals=0,
        ),
        name="weight_grad",
    )(*args)


def unpack_kernel(blocks_ref, *refs):
    parts, (out_ref, vectors_ref) = refs[:3], refs[3:]
    rows = out_ref.shape[0]
    width = out_ref.shape[1] // 3
    columns = blocks_ref.shape[2] // 3
    place = lax.axis_index("seq") // 2
    total = jnp.zeros(vectors_ref.shape, f32)
    for k in range(4):
        far = place ^ k
        for near in range(2):
            at = far * 2 + near
            block = (blocks_ref[at] if k == 0 else parts[k - 1][near]).astype(f32)
            for i in range(3):
                span = pl.ds(pl.multiple_of(i * width + at * columns, columns), columns)
                out_ref[:, span] = block[:rows, i * columns : (i + 1) * columns]
            total += block[rows : rows + 8]
    vectors_ref[...] = total


def unpack_joint(blocks, parts, rows):
    n_seq, _, total = blocks.shape
    return pl.pallas_call(
        unpack_kernel,
        out_shape=(
            jax.ShapeDtypeStruct((rows, n_seq * total), f32),
            jax.ShapeDtypeStruct((8, total), f32),
        ),
        compiler_params=pltpu.CompilerParams(vmem_limit_bytes=VMEM_BYTES),
        cost_estimate=pl.CostEstimate(
            flops=n_seq * rows * total, bytes_accessed=6 * n_seq * rows * total, transcendentals=0
        ),
        name="unpack_joint",
    )(blocks, *parts)


def grad_near(halves, n_batch):
    keep, send = halves
    if send is None:
        return scatter_near(keep, n_batch), None
    return keep, swap(send, "batch", n_batch, 1)


def grad_far_begin(halves, n_batch):
    keep, got = halves
    if got is None:
        return scatter_far(keep, n_batch), None
    keep, got = keep.astype(f32), got.astype(f32)
    other = swap((keep[1] + got[1]).astype(bf16), "batch", n_batch, 2)
    return (keep[0] + got[0]).astype(bf16), other


def grad_far_end(state):
    keep, other = state
    if other is None:
        return keep
    return (keep.astype(f32) + other.astype(f32)).astype(bf16)


def make_body(n_seq, n_batch):
    def body(
        tokens,
        language,
        language_weight,
        output_grad,
        attention_gain,
        attention_shift,
        joint_weight,
        joint_bias,
        output_weight,
        feedfwd_gain,
        feedfwd_shift,
        gate_weight,
        up_weight,
        down_weight,
    ):
        _, local, width = tokens.shape
        rows, ff_width = gate_weight.shape
        length = local * n_seq
        columns = width // n_seq
        tiles = -(-ff_width // (128 * n_seq))
        ff_local = 128 * tiles
        seq_at = lax.axis_index("seq")
        first_row = seq_at * local
        values = tokens[0]
        tables = [jnp.asarray(t) for t in turn_tables(length)]

        center_own = values - mean_of(values)
        ring = Gather(jnp.concatenate([center_own.astype(bf16), output_weight]), n_seq)

        chosen = language[:, None] == jnp.arange(LANGS, dtype=jnp.int32)[None, :]
        row_scale = jnp.sum(jnp.where(chosen, language_weight[None, :], 0.0), axis=1)
        cotangent = output_grad[0] * row_scale[:, None]

        small = jnp.concatenate(
            [attention_gain, attention_shift, feedfwd_gain, feedfwd_shift, joint_bias]
        )
        small = jnp.pad(small[None], ((0, 15), (0, 3 * columns - small.shape[0])))
        blocks = jnp.transpose(joint_weight.reshape(rows, 3, n_seq, columns), (2, 0, 1, 3))
        blocks = blocks.reshape(n_seq, rows, 3 * columns)
        blocks = jnp.concatenate(
            [blocks, jnp.broadcast_to(small[None], (n_seq,) + small.shape)], axis=1
        )
        ff_blocks = [
            jnp.pad(w, ((0, 0), (0, n_seq * ff_local - ff_width))).reshape(rows, tiles, n_seq, 128)
            for w in (gate_weight, up_weight, down_weight)
        ]
        ff_blocks = jnp.transpose(jnp.stack(ff_blocks, 1), (3, 0, 1, 2, 4))
        ff_blocks = ff_blocks.reshape(n_seq, rows, 3 * ff_local)

        ring.step()
        flight = exchange_begin(blocks, n_seq, 1)
        ff_flight = exchange_begin(ff_blocks, n_seq, 4)
        (flight,) = ring.tie(flight)
        blocks = exchange_end(flight, n_seq, 1)
        ring.step()
        flight = exchange_begin(blocks, n_seq, 2)
        flight, ff_flight, down_grad = ring.tie(flight, ff_flight, cotangent.astype(bf16))
        down_grad = lax.all_gather(down_grad, "seq", axis=0, tiled=True)
        blocks = exchange_end(flight, n_seq, 2)
        ff_blocks = rest_of_exchange(exchange_end(ff_flight, n_seq, 4), n_seq)
        ring.step()
        flight = exchange_begin(blocks, n_seq, 4)
        ff_flight = exchange_begin(ff_blocks, n_seq, 1)
        flight, ff_flight = ring.tie(flight, ff_flight)
        blocks = rest_of_exchange(exchange_end(flight, n_seq, 4), n_seq)
        ff_blocks = exchange_end(ff_flight, n_seq, 1)
        ring.step()
        held = gather_far(blocks, n_batch)
        ff_flight = exchange_begin(ff_blocks, n_seq, 2)
        (held_last,) = ring.tie(held[-1][1])
        held[-1] = (held[-1][0], held_last)
        pieces = gather_near(held, n_batch)
        center_pieces = [v for _, v in ring.pieces]
        output_held = jnp.concatenate([v[local:] for v in center_pieces])
        output_held, *pieces = tie(output_held, *pieces)
        output_held = gather_far(output_held, n_batch)

        small = jnp.stack([v[:, rows] for v in pieces], axis=1)
        batch_at = lax.axis_index("batch")
        for bit in bits_of(n_batch):
            flipped = small.reshape(n_seq, -1, 2, bit, small.shape[2])[:, :, ::-1]
            small = jnp.where((batch_at & bit) == 0, small, flipped.reshape(small.shape))
        piece = width // (n_seq * n_batch)

        def small_part(start, size):
            return small[:, :, start : start + size].reshape(1, -1).astype(f32)

        gain_one = small_part(0, piece)
        shift_one = small_part(piece, piece)
        gain_two = small_part(2 * piece, piece)
        shift_two = small_part(3 * piece, piece)
        bias_all = small_part(4 * piece, 3 * piece).reshape(3, n_seq, columns)
        bias = lax.dynamic_slice_in_dim(bias_all, seq_at, 1, 1).reshape(1, 3 * columns)

        low, first_input, center = make_heads(
            center_pieces, gain_one, shift_one, bias, tables, pieces, rows, local
        )
        context, mixed, lse = attend(low)

        mixed, held_last, ff_flight = tie(mixed, output_held[-1][1], ff_flight)
        output_held[-1] = (output_held[-1][0], held_last)
        ring = Gather(mixed, n_seq)
        ring.step()
        held = gather_far(exchange_end(ff_flight, n_seq, 2), n_batch)
        ring.tie()
        ring.step()
        output_pieces = gather_near(output_held, n_batch)
        output_pieces = ring.tie(*output_pieces)
        ring.step()
        ring.tie()
        ring.step()
        (held_last,) = ring.tie(held[-1][1])
        held[-1] = (held[-1][0], held_last)
        ff_pieces = gather_near(held, n_batch)
        mixed_pieces = [v for _, v in ring.pieces]
        if columns % 128:
            mixed_pieces = [join(ring.pieces, n_seq, 1)]
        second_input, unit_two, inverse_two, mixed_all, output_all = make_middle(
            mixed_pieces, output_pieces, center, gain_two, shift_two, n_seq, rows
        )
        output_all = output_all.reshape(width, width)

        gate, upper, hidden, result_part = feed(second_input, ff_pieces, rows)
        middle_grads, back, through, second_sums = feed_back(
            gate,
            upper,
            down_grad,
            unit_two,
            inverse_two,
            gain_two,
            output_all,
            ff_pieces,
            rows,
            n_seq,
        )
        result_sum = lax.psum_scatter(result_part, "seq", scatter_dimension=0, tiled=True)

        def own(array):
            return lax.dynamic_slice_in_dim(array, first_row, local, 0)

        ring = Scatter(lambda at: lax.dynamic_index_in_dim(through, at, 0, False), n_seq)
        ring.step()
        grad_down = weight_grad(down_grad, hidden, n_seq, n_batch)
        (grad_down,) = ring.tie(grad_down)
        ring.step()
        grad_down = grad_near(grad_down, n_batch)
        grad_both = weight_grad(second_input, middle_grads, n_seq, n_batch)
        grad_both, grad_down = ring.tie(grad_both, grad_down)
        ring.step()
        grad_both = grad_near(grad_both, n_batch)
        grad_down = grad_far_begin(grad_down, n_batch)
        grad_output = weight_grad(
            mixed_all, back, n_seq, n_batch, rest=cotangent.astype(bf16)
        )
        grad_both, grad_output, grad_down, result_sum = ring.tie(
            grad_both, grad_output, grad_down, result_sum
        )
        ring.step()
        grad_both = grad_far_begin(grad_both, n_batch)
        grad_output = grad_near(grad_output, n_batch)
        grad_down = exchange_begin(grad_far_end(grad_down), n_seq, 4)
        heads_weight = lax.dynamic_slice_in_dim(output_all, seq_at * columns, columns, 0)
        from_cot = dot(down_grad, heads_weight, ((1,), (1,)))
        from_cot, grad_output = ring.tie(from_cot, grad_output)
        context_grad = (ring.total() + from_cot).astype(bf16)
        joint_grad = attend_back(low, context_grad, context, lse, tables)
        joint_grad, grad_both, grad_down = tie(joint_grad, grad_both, grad_down)
        grad_output = grad_far_begin(grad_output, n_batch)
        grad_both = exchange_begin(grad_far_end(grad_both), n_seq, 4)
        grad_down = rest_of_exchange(exchange_end(grad_down, n_seq, 4), n_seq)
        grad_down = exchange_begin(grad_down, n_seq, 1)
        both, first_sums, bias_sums = first_back(joint_grad, center, gain_one, back, pieces, rows)

        ring = Scatter(lambda at: lax.dynamic_slice_in_dim(both, at * local, local, 0), n_seq)
        ring.step()
        bias_part = lax.dynamic_update_slice_in_dim(
            jnp.zeros((3, n_seq, columns), f32), bias_sums[:1].reshape(3, 1, columns), seq_at, 1
        )
        vectors = [first_sums[0], first_sums[1], second_sums[0], second_sums[1], bias_part]
        vectors = [v.reshape(n_seq, n_batch, 1, -1).astype(bf16) for v in vectors]
        vectors = jnp.concatenate(vectors, axis=3)
        vectors = jnp.pad(vectors, ((0, 0), (0, 0), (0, 15), (0, 3 * columns - 7 * piece)))
        grad_joint = weight_grad(first_input, joint_grad, n_seq, n_batch, below=vectors)
        grad_joint, grad_down, grad_both = ring.tie(grad_joint, grad_down, grad_both)
        ring.step()
        grad_joint = grad_near(grad_joint, n_batch)
        grad_both = rest_of_exchange(exchange_end(grad_both, n_seq, 4), n_seq)
        grad_both = exchange_begin(grad_both, n_seq, 1)
        grad_joint, grad_output = ring.tie(grad_joint, grad_output)
        grad_output = lax.psum_scatter(
            grad_far_end(grad_output), "seq", scatter_dimension=0, tiled=False
        )
        ring.step()
        grad_joint = grad_far_begin(grad_joint, n_batch)
        grad_down = exchange_begin(exchange_end(grad_down, n_seq, 1), n_seq, 2)
        projected_own = dot(own(mixed_all), output_all, ((1,), (0,)))
        result = values + projected_own + result_sum.astype(f32)
        grad_joint, grad_both, grad_down, result = ring.tie(
            grad_joint, grad_both, grad_down, result
        )
        grad_down = exchange_end(grad_down, n_seq, 2)
        ring.step()
        grad_joint = exchange_begin(grad_far_end(grad_joint), n_seq, 1)
        grad_both = exchange_begin(exchange_end(grad_both, n_seq, 1), n_seq, 2)
        (grad_joint,) = ring.tie(grad_joint)
        grad_joint = exchange_end(grad_joint, n_seq, 1)
        if n_seq == 8:
            parts = exchange_parts(grad_joint)
        grad_both = exchange_end(grad_both, n_seq, 2)
        token_grad = cotangent + ring.total()
        grad_output = grad_output.astype(f32)

        def unsplit(grad):
            grad = grad.reshape(n_seq, rows, tiles, 128).astype(f32)
            return jnp.transpose(grad, (1, 2, 0, 3)).reshape(rows, n_seq * ff_local)[:, :ff_width]

        grad_gate = unsplit(grad_both[:, :, :ff_local])
        grad_up = unsplit(grad_both[:, :, ff_local:])
        grad_down = unsplit(grad_down)
        if n_seq == 8:
            done = tie(*parts, grad_gate, grad_up, grad_down, token_grad)
            parts, (grad_gate, grad_up, grad_down, token_grad) = done[:3], done[3:]
            grad_joint, vectors = unpack_joint(grad_joint, parts, rows)
            vectors = vectors[0]
        else:
            grad_joint = exchange_far(grad_joint, n_seq).astype(f32)
            vectors = jnp.sum(grad_joint[:, rows], axis=0)
            grad_joint = grad_joint[:, :rows].reshape(n_seq, rows, 3, columns)
            grad_joint = jnp.transpose(grad_joint, (1, 2, 0, 3)).reshape(rows, 3 * width)
        return (
            result[None],
            token_grad[None],
            vectors[:piece],
            vectors[piece : 2 * piece],
            grad_joint,
            vectors[4 * piece : 7 * piece],
            grad_output,
            vectors[2 * piece : 3 * piece],
            vectors[3 * piece : 4 * piece],
            grad_gate,
            grad_up,
            grad_down,
        )

    return body


def solution(mesh):
    rows = P(("seq", "batch"))
    matrix = P(("seq", "batch"), None)
    data = P("batch", "seq", None)
    return jax.shard_map(
        make_body(mesh.shape["seq"], mesh.shape["batch"]),
        mesh=mesh,
        in_specs=(
            data,
            P("batch"),
            P(),
            data,
            rows,
            rows,
            matrix,
            rows,
            matrix,
            rows,
            rows,
            matrix,
            matrix,
            matrix,
        ),
        out_specs=(data, data, rows, rows, matrix, rows, matrix, rows, rows, matrix, matrix, matrix),
        check_vma=False,
    )
```

```python
import math

import numpy as np

import jax
import jax.numpy as jnp
from jax import lax
from jax.experimental import pallas as pl
from jax.experimental.pallas import tpu as pltpu
from jax.sharding import PartitionSpec as P

HEADS = 32
HEAD_DIM = 64
ROT_DIMS = 16
LANGS = 7

EPSILON = 1e-05
THETA_BASE = 10000.0
NEGATIVE = -1e30
VMEM_BYTES = 56 * 1024 * 1024
GRAD_BLOCKS = 2

bf16 = jnp.bfloat16
f32 = jnp.float32


def swap(value, axis, number, bit):
    return lax.ppermute(value, axis, [(i, i ^ bit) for i in range(number)])


def bits_of(number):
    return [1 << i for i in range(number.bit_length() - 1)]


def tie(*values):
    return lax.optimization_barrier(values)


def after(value, *others):
    return tie(value, *others)[0]


def exchange_begin(blocks, number, bit):
    mine = (lax.axis_index("seq") // bit) % 2
    pairs = blocks.reshape((number // (2 * bit), 2, bit) + blocks.shape[1:])
    return pairs, swap(lax.dynamic_slice_in_dim(pairs, 1 - mine, 1, 1), "seq", number, bit)


def exchange_end(state, number, bit):
    pairs, got = state
    mine = (lax.axis_index("seq") // bit) % 2
    out = lax.dynamic_update_slice_in_dim(pairs, got, 1 - mine, 1)
    return out.reshape((number,) + pairs.shape[3:])


def exchange(blocks, number, bit):
    return exchange_end(exchange_begin(blocks, number, bit), number, bit)


def exchange_far(blocks, number):
    for bit in bits_of(number)[1:]:
        blocks = exchange(blocks, number, bit)
    return blocks


def exchange_parts(blocks):
    place = lax.axis_index("seq") // 2
    pairs = blocks.reshape((4, 2) + blocks.shape[1:])
    return [
        swap(lax.dynamic_slice_in_dim(pairs, place ^ k, 1, 0), "seq", 8, k * 2)[0]
        for k in range(1, 4)
    ]


def rest_of_exchange(blocks, number):
    for bit in bits_of(number)[3:]:
        blocks = exchange(blocks, number, bit)
    return blocks


def gather_far(value, number):
    held = [(0, value)]
    for bit in reversed(bits_of(number)[1:]):
        held = held + [(k ^ bit, swap(v, "batch", number, bit)) for k, v in held]
    return held


def gather_near(held, number):
    held = dict(held + [(k ^ 1, swap(v, "batch", number, 1)) for k, v in held])
    return [held[k] for k in range(number)]


def scatter_stage(value, number, bit):
    n, _, r, c = value.shape
    pairs = value.reshape(n, -1, 2, r, c)
    mine = (lax.axis_index("batch") // bit) % 2
    keep = lax.dynamic_index_in_dim(pairs, mine, 2, False)
    send = lax.dynamic_index_in_dim(pairs, 1 - mine, 2, False).astype(bf16)
    return (keep.astype(f32) + swap(send, "batch", number, bit).astype(f32)).astype(bf16)


def scatter_near(value, number):
    return scatter_stage(value, number, 1)


def scatter_far(value, number):
    for bit in bits_of(number)[1:]:
        value = scatter_stage(value, number, bit)
    return value[:, 0]


RING = (0, 2, 4, 6, 7, 5, 3, 1)


def ring_place():
    s = lax.axis_index("seq")
    return jnp.where(s % 2 == 0, s // 2, 7 - s // 2)


def ring_index(place):
    place = (place + 16) % 8
    return jnp.where(place < 4, 2 * place, 15 - 2 * place)


ARRIVAL = (0, 1, -1, 2, -2, 3, -3, -4)


def arrival(number):
    if number != 8:
        return list(range(number))
    return [ring_index(ring_place() + step) for step in ARRIVAL]


def ring_step(value, way):
    return lax.ppermute(value, "seq", [(RING[i], RING[(i + way) % 8]) for i in range(8)])


class Ring:
    ahead = behind = None
    taken = 0

    def tie(self, *others):
        if self.number != 8:
            return others
        self.ahead, self.behind, *others = tie(self.ahead, self.behind, *others)
        return others


class Gather(Ring):
    def __init__(self, value, number):
        self.number = number
        if number != 8:
            every = lax.all_gather(value, "seq", axis=0, tiled=False)
            self.pieces = [(i, every[i]) for i in range(number)]
            return
        self.pieces = [(lax.axis_index("seq"), value)]
        self.ahead = self.behind = value
        self.place = ring_place()

    def step(self):
        if self.number != 8:
            return
        self.taken += 1
        k = self.taken
        self.ahead = ring_step(self.ahead, 1)
        if k < 4:
            self.behind = ring_step(self.behind, -1)
            self.pieces.append((ring_index(self.place + k), self.behind))
        self.pieces.append((ring_index(self.place - k), self.ahead))


class Scatter(Ring):
    def __init__(self, block, number):
        self.number = number
        self.block = block
        self.place = ring_place()

    def step(self):
        if self.number != 8:
            return
        k = 4 - self.taken
        self.taken += 1
        part = self.block(ring_index(self.place + k))
        if self.ahead is not None:
            part = (part.astype(f32) + self.ahead.astype(f32)).astype(bf16)
        self.ahead = ring_step(part, 1)
        if k > 1:
            part = self.block(ring_index(self.place - k + 1))
            if self.behind is not None:
                part = (part.astype(f32) + self.behind.astype(f32)).astype(bf16)
            self.behind = ring_step(part, -1)

    def total(self):
        if self.number != 8:
            every = jnp.stack([self.block(i) for i in range(self.number)])
            return lax.psum_scatter(every, "seq", scatter_dimension=0, tiled=False).astype(f32)
        own = self.block(lax.axis_index("seq"))
        return own.astype(f32) + self.ahead.astype(f32) + self.behind.astype(f32)


def join(pieces, number, axis):
    at, first = pieces[0]
    size = first.shape[axis]
    shape = first.shape[:axis] + (number * size,) + first.shape[axis + 1 :]
    out = jnp.zeros(shape, first.dtype)
    for at, piece in pieces:
        out = lax.dynamic_update_slice_in_dim(out, piece, at * size, axis)
    return out


def turn_tables(length):
    half = ROT_DIMS // 2
    frequency = THETA_BASE ** (-np.arange(half, dtype=np.float32) / np.float32(half))
    angle = (np.arange(length, dtype=np.float32)[:, None] * frequency.astype(np.float32)[None]).astype(
        np.float32
    )
    cosine = np.ones((length, HEAD_DIM), np.float32)
    left = np.zeros((length, HEAD_DIM), np.float32)
    right = np.zeros((length, HEAD_DIM), np.float32)
    cosine[:, :half] = np.cos(angle)
    cosine[:, half:ROT_DIMS] = np.cos(angle)
    left[:, :half] = -np.sin(angle)
    right[:, half:ROT_DIMS] = np.sin(angle)
    return [np.concatenate([t, t], 1) for t in (cosine, left, right)]


def wide(table, columns):
    if columns < table.shape[1]:
        return table[:, :columns]
    return jnp.concatenate([table] * (columns // table.shape[1]), axis=1)


def lane_roll(value, amount):
    columns = value.shape[1]
    if columns % 128 == 0:
        return pltpu.roll(value, amount % columns, 1)
    amount = amount % columns
    return jnp.concatenate([value[:, columns - amount :], value[:, : columns - amount]], axis=1)


def turn(value, cosine, left, right):
    half = ROT_DIMS // 2
    return value * cosine + lane_roll(value, -half) * left + lane_roll(value, half) * right


def turn_back(value, cosine, left, right):
    half = ROT_DIMS // 2
    return value * cosine - lane_roll(value, -half) * left - lane_roll(value, half) * right


def head_mask(columns, head):
    lane = lax.broadcasted_iota(jnp.int32, (1, columns), 1)
    return (lane >= head * HEAD_DIM) & (lane < (head + 1) * HEAD_DIM)


def block_of(length):
    return math.gcd(length, 256)


def attend_kernel(low_ref, context_ref, mixed_ref, lse_ref):
    length, total = low_ref.shape
    columns = total // 3
    heads = columns // HEAD_DIM
    block = block_of(length)
    for i in range(length // block):
        rows = pl.ds(i * block, block)
        reach = (i + 1) * block
        query = low_ref[rows, 0:columns]
        key = low_ref[0:reach, columns : 2 * columns]
        value = low_ref[0:reach, 2 * columns :]
        total_out = jnp.zeros((block, columns), f32)
        lse_all = jnp.zeros((block, 128), f32)
        lane = lax.broadcasted_iota(jnp.int32, (block, 128), 1)
        ahead = lax.broadcasted_iota(jnp.int32, (block, reach), 1) > (
            i * block + lax.broadcasted_iota(jnp.int32, (block, reach), 0)
        )
        for h in range(heads):
            mask = head_mask(columns, h)
            scores = lax.dot_general(
                jnp.where(mask, query, jnp.zeros_like(query)),
                key,
                (((1,), (1,)), ((), ())),
                preferred_element_type=f32,
            )
            scores = jnp.where(ahead, NEGATIVE, scores)
            top = jnp.max(scores, axis=1, keepdims=True)
            weight = jnp.exp(scores - top)
            denominator = jnp.sum(weight, axis=1, keepdims=True)
            probs = (weight * (1.0 / denominator)).astype(bf16)
            total_out += jnp.dot(
                probs, jnp.where(mask, value, jnp.zeros_like(value)), preferred_element_type=f32
            )
            lse_all = jnp.where(lane == h, top + jnp.log(denominator), lse_all)
        context_ref[rows, :] = total_out
        mixed_ref[rows, :] = total_out.astype(bf16)
        lse_ref[rows, :] = lse_all


def attend(low):
    length, total = low.shape
    columns = total // 3
    return pl.pallas_call(
        attend_kernel,
        out_shape=(
            jax.ShapeDtypeStruct((length, columns), f32),
            jax.ShapeDtypeStruct((length, columns), bf16),
            jax.ShapeDtypeStruct((length, 128), f32),
        ),
        compiler_params=pltpu.CompilerParams(vmem_limit_bytes=VMEM_BYTES),
        cost_estimate=pl.CostEstimate(
            flops=4 * length * length * columns * 2,
            bytes_accessed=16 * length * total,
            transcendentals=length * length * columns // HEAD_DIM,
        ),
        name="attend",
    )(low)


def attend_back_kernel(
    low_ref, grad_ref, context_ref, lse_ref, cos_ref, left_ref, right_ref, out_ref, dq_ref, dk_ref, dv_ref
):
    length, total = low_ref.shape
    columns = total // 3
    heads = columns // HEAD_DIM
    block = block_of(length)
    scale = 1.0 / math.sqrt(HEAD_DIM)
    dk_ref[...] = jnp.zeros_like(dk_ref)
    dv_ref[...] = jnp.zeros_like(dv_ref)
    for i in range(length // block):
        rows = pl.ds(i * block, block)
        reach = (i + 1) * block
        query = low_ref[rows, 0:columns]
        grad = grad_ref[rows, :]
        grad_wide = grad.astype(f32)
        query_t = query.astype(f32).T.astype(bf16)
        grad_t = grad_wide.T.astype(bf16)
        product = grad_wide * context_ref[rows, :]
        key = low_ref[0:reach, columns : 2 * columns]
        value = low_ref[0:reach, 2 * columns :]
        dq = jnp.zeros((block, columns), f32)
        ahead = lax.broadcasted_iota(jnp.int32, (block, reach), 1) > (
            i * block + lax.broadcasted_iota(jnp.int32, (block, reach), 0)
        )
        for h in range(heads):
            mask = head_mask(columns, h)
            span = slice(h * HEAD_DIM, (h + 1) * HEAD_DIM)
            scores = lax.dot_general(
                jnp.where(mask, query, jnp.zeros_like(query)),
                key,
                (((1,), (1,)), ((), ())),
                preferred_element_type=f32,
            )
            scores = jnp.where(ahead, NEGATIVE, scores)
            probs = jnp.exp(scores - lse_ref[rows, h : h + 1])
            dots = lax.dot_general(
                jnp.where(mask, grad, jnp.zeros_like(grad)),
                value,
                (((1,), (1,)), ((), ())),
                preferred_element_type=f32,
            )
            balance = jnp.sum(jnp.where(mask, product, 0.0), axis=1, keepdims=True)
            score_grad = (probs * (dots - balance)).astype(bf16)
            dq += jnp.dot(
                score_grad, jnp.where(mask, key, jnp.zeros_like(key)), preferred_element_type=f32
            )
            dk_ref[span, 0:reach] += jnp.dot(query_t[span], score_grad, preferred_element_type=f32)
            dv_ref[span, 0:reach] += jnp.dot(
                grad_t[span], probs.astype(bf16), preferred_element_type=f32
            )
        dq_ref[rows, :] = dq
    for i in range(length // block):
        rows = pl.ds(i * block, block)
        tables = [wide(t[rows, :], columns) for t in (cos_ref, left_ref, right_ref)]
        out_ref[rows, 0:columns] = turn_back(dq_ref[rows, :] * scale, *tables).astype(bf16)
        out_ref[rows, columns : 2 * columns] = turn_back(dk_ref[:, rows].T, *tables).astype(bf16)
        out_ref[rows, 2 * columns :] = dv_ref[:, rows].T.astype(bf16)


def attend_back(low, grad, context, lse, tables):
    length, total = low.shape
    columns = total // 3
    return pl.pallas_call(
        attend_back_kernel,
        out_shape=jax.ShapeDtypeStruct((length, total), bf16),
        scratch_shapes=[
            pltpu.VMEM((length, columns), f32),
            pltpu.VMEM((columns, length), f32),
            pltpu.VMEM((columns, length), f32),
        ],
        compiler_params=pltpu.CompilerParams(vmem_limit_bytes=VMEM_BYTES),
        cost_estimate=pl.CostEstimate(
            flops=10 * length * length * columns * 2,
            bytes_accessed=16 * length * total,
            transcendentals=length * length * columns // HEAD_DIM,
        ),
        name="attend_back",
    )(low, grad, context, lse, *tables)


def mean_of(values):
    return jnp.mean(values, axis=-1, keepdims=True)


def unit_of(values):
    center = values - mean_of(values)
    inverse_std = lax.rsqrt(mean_of(center * center) + EPSILON)
    return center * inverse_std, inverse_std


def unit_of_centered(center):
    inverse_std = lax.rsqrt(mean_of(center * center) + EPSILON)
    return center * inverse_std, inverse_std


def norm_back(incoming, unit_rows, inverse_std, gain_values):
    inner = incoming * gain_values
    return inverse_std * (inner - mean_of(inner) - unit_rows * mean_of(inner * unit_rows))


def dot(left, right, contract):
    return lax.dot_general(left, right, (contract, ((), ())), preferred_element_type=f32)


def block_spec(block, columns):
    return pl.BlockSpec((block, columns), lambda i: (i, 0))


def whole_spec(rows, columns):
    return pl.BlockSpec((rows, columns), lambda i: (0, 0))


def once_spec(rows, columns):
    return pl.BlockSpec((rows, columns), lambda i: (0, 0), pipeline_mode=pl.Buffered(1))


def any_specs(number):
    return [pl.BlockSpec(memory_space=pl.ANY)] * number


def run_copies(copies, sems):
    copies = [pltpu.make_async_copy(*pair, sems.at[i]) for i, pair in enumerate(copies)]
    for copy in copies:
        copy.start()
    for copy in copies:
        copy.wait()


def weight_copies(piece_refs, weight_ref):
    me = lax.axis_index("batch")
    rows = weight_ref.shape[2]
    return [
        (ref.at[:, pl.ds(0, rows), :], weight_ref.at[:, me ^ k])
        for k, ref in enumerate(piece_refs)
    ]


def load_pieces(piece_refs, weight_ref, sems):
    @pl.when(pl.program_id(0) == 0)
    def _():
        run_copies(weight_copies(piece_refs, weight_ref), sems)


def weight_of(weight_ref, start, size):
    part = weight_ref[:, :, :, start : start + size]
    return part.reshape(-1, size)


def call_kernel(kernel, length, in_specs, out, scratch, args, name, flops):
    block = block_of(length)
    return pl.pallas_call(
        kernel,
        grid=(length // block,),
        in_specs=in_specs,
        out_specs=[spec for _, spec in out],
        out_shape=[shape for shape, _ in out],
        scratch_shapes=scratch,
        compiler_params=pltpu.CompilerParams(
            vmem_limit_bytes=VMEM_BYTES, dimension_semantics=("arbitrary",)
        ),
        cost_estimate=pl.CostEstimate(
            flops=flops, bytes_accessed=flops // 500, transcendentals=0
        ),
        name=name,
    )(*args)


def rows_out(length, columns, kind):
    return (jax.ShapeDtypeStruct((length, columns), kind), block_spec(block_of(length), columns))


def sums_out(columns):
    return (jax.ShapeDtypeStruct((8, columns), f32), whole_spec(8, columns))


def add_sums(ref, *rows):
    @pl.when(pl.program_id(0) == 0)
    def _():
        ref[...] = jnp.zeros_like(ref)

    for i, row in enumerate(rows):
        ref[i : i + 1, :] += jnp.sum(row, axis=0, keepdims=True)


def heads_kernel(n, n_seq, *refs):
    gain_ref, shift_ref, bias_ref, cos_ref, left_ref, right_ref = refs[:6]
    pieces = refs[6 : 6 + n]
    center_pieces = refs[6 + n : 6 + n + n_seq]
    low_ref, input_ref, center_ref, weight_ref, all_ref, sems = refs[6 + n + n_seq :]
    local = all_ref.shape[1]

    @pl.when(pl.program_id(0) == 0)
    def _():
        copies = [
            (ref.at[pl.ds(0, local), :], all_ref.at[at])
            for at, ref in zip(arrival(n_seq), center_pieces)
        ]
        run_copies(copies + weight_copies(pieces, weight_ref), sems)

    total = low_ref.shape[1]
    columns = total // 3
    block, width = center_ref.shape
    many = block // local
    center = all_ref[pl.ds(pl.program_id(0) * many, many)].reshape(block, width)
    center_ref[...] = center
    unit, _ = unit_of_centered(center.astype(f32))
    first_input = (unit * gain_ref[...] + shift_ref[...]).astype(bf16)
    input_ref[...] = first_input
    joint = dot(first_input, weight_of(weight_ref, 0, total), ((1,), (0,))) + bias_ref[...]
    tables = [wide(t[...], columns) for t in (cos_ref, left_ref, right_ref)]
    scale = 1.0 / math.sqrt(HEAD_DIM)
    query = turn(joint[:, :columns], *tables).astype(bf16)
    low_ref[:, :columns] = (query.astype(f32) * scale).astype(bf16)
    low_ref[:, columns : 2 * columns] = turn(joint[:, columns : 2 * columns], *tables).astype(bf16)
    low_ref[:, 2 * columns :] = joint[:, 2 * columns :].astype(bf16)


def make_heads(center_pieces, gain, shift, bias, tables, pieces, rows, local):
    n_seq, n = len(center_pieces), len(pieces)
    length, width = local * n_seq, gain.shape[1]
    total = bias.shape[1]
    block = block_of(length)
    return call_kernel(
        lambda *refs: heads_kernel(n, n_seq, *refs),
        length,
        [whole_spec(1, width), whole_spec(1, width), whole_spec(1, total)]
        + [block_spec(block, 128)] * 3
        + any_specs(n + n_seq),
        [
            rows_out(length, total, bf16),
            rows_out(length, width, bf16),
            rows_out(length, width, bf16),
        ],
        [
            pltpu.VMEM((n_seq, n, rows, total), bf16),
            pltpu.VMEM((n_seq, local, width), bf16),
            pltpu.SemaphoreType.DMA((n + n_seq,)),
        ],
        (gain, shift, bias, *tables, *pieces, *center_pieces),
        "make_heads",
        2 * length * width * total,
    )


def middle_kernel(n, n_seq, many, *refs):
    center_ref, gain_ref, shift_ref = refs[:3]
    pieces, mixed_pieces = refs[3 : 3 + n], refs[3 + n : 3 + n + many]
    input_ref, unit_ref, inverse_ref, mixed_ref, out_ref = refs[3 + n + many : 8 + n + many]
    weight_ref, all_ref, sems, out_sem = refs[8 + n + many :]
    rows, width = weight_ref.shape[2:]
    columns = width // n_seq
    step = pl.program_id(0)
    give = pltpu.make_async_copy(weight_ref, out_ref, out_sem)

    @pl.when(step == 0)
    def _():
        me = lax.axis_index("batch")
        places = arrival(n_seq)
        copies = [
            (ref.at[pl.ds(j * rows, rows), :], weight_ref.at[at, me ^ k])
            for k, ref in enumerate(pieces)
            for j, at in enumerate(places)
        ]
        if many == 1:
            copies.append((mixed_pieces[0], all_ref))
        else:
            for at, ref in zip(places, mixed_pieces):
                span = pl.ds(pl.multiple_of(at * columns, columns), columns)
                copies.append((ref, all_ref.at[:, span]))
        run_copies(copies, sems)
        give.start()

    block = center_ref.shape[0]
    mixed = all_ref[pl.ds(pl.multiple_of(step * block, block), block), :]
    mixed_ref[...] = mixed
    projected = dot(mixed, weight_ref[...].reshape(width, width), ((1,), (0,)))
    unit, inverse = unit_of(center_ref[...].astype(f32) + projected)
    input_ref[...] = (unit * gain_ref[...] + shift_ref[...]).astype(bf16)
    unit_ref[...] = unit.astype(bf16)
    inverse_ref[...] = jnp.broadcast_to(inverse, inverse_ref.shape)

    @pl.when(step == pl.num_programs(0) - 1)
    def _():
        give.wait()


def make_middle(mixed_pieces, pieces, center, gain, shift, n_seq, rows):
    length, width = center.shape
    n, many = len(pieces), len(mixed_pieces)
    block = block_of(length)
    row = whole_spec(1, width)
    weight_shape = (n_seq, n, rows, width)
    return call_kernel(
        lambda *refs: middle_kernel(n, n_seq, many, *refs),
        length,
        [block_spec(block, width), row, row] + any_specs(n + many),
        [
            rows_out(length, width, bf16),
            rows_out(length, width, bf16),
            rows_out(length, 128, f32),
            rows_out(length, width, bf16),
            (jax.ShapeDtypeStruct(weight_shape, bf16), pl.BlockSpec(memory_space=pl.ANY)),
        ],
        [
            pltpu.VMEM(weight_shape, bf16),
            pltpu.VMEM((length, width), bf16),
            pltpu.SemaphoreType.DMA((n * n_seq + many,)),
            pltpu.SemaphoreType.DMA,
        ],
        (center, gain, shift, *pieces, *mixed_pieces),
        "make_middle",
        2 * length * width * width,
    )


def feed_kernel(n, *refs):
    input_ref = refs[0]
    pieces = refs[1 : 1 + n]
    gate_ref, upper_ref, hidden_ref, result_ref, weight_ref, sems = refs[1 + n :]
    load_pieces(pieces, weight_ref, sems)
    size = hidden_ref.shape[1]
    second_input = input_ref[...]
    gate = dot(second_input, weight_of(weight_ref, 0, size), ((1,), (0,)))
    upper = dot(second_input, weight_of(weight_ref, size, size), ((1,), (0,)))
    gate_ref[...] = gate
    upper_ref[...] = upper
    hidden = (gate * jax.nn.sigmoid(gate) * upper).astype(bf16)
    hidden_ref[...] = hidden
    result_ref[...] = dot(hidden, weight_of(weight_ref, 2 * size, size), ((1,), (1,))).astype(bf16)


def feed(second_input, pieces, rows):
    length, width = second_input.shape
    size = pieces[0].shape[2] // 3
    n = len(pieces)
    return call_kernel(
        lambda *refs: feed_kernel(n, *refs),
        length,
        [block_spec(block_of(length), width)] + any_specs(n),
        [rows_out(length, size, f32)] * 2
        + [rows_out(length, size, bf16), rows_out(length, width, bf16)],
        [
            pltpu.VMEM((pieces[0].shape[0], n, rows, 3 * size), bf16),
            pltpu.SemaphoreType.DMA((n,)),
        ],
        (second_input, *pieces),
        "feed",
        6 * length * width * size,
    )


def feed_back_kernel(n, *refs):
    gate_ref, upper_ref, grad_ref, unit_ref, inverse_ref, gain_ref, output_ref = refs[:7]
    pieces = refs[7 : 7 + n]
    grads_ref, back_ref, through_ref, sums_ref, weight_ref, sems = refs[7 + n :]
    load_pieces(pieces, weight_ref, sems)
    size = gate_ref.shape[1]
    gate = gate_ref[...]
    upper = upper_ref[...]
    hidden_grad = dot(grad_ref[...], weight_of(weight_ref, 2 * size, size), ((1,), (0,)))
    sigmoid = jax.nn.sigmoid(gate)
    gate_grad = (hidden_grad * upper * sigmoid * (1.0 + gate * (1.0 - sigmoid))).astype(bf16)
    grads_ref[:, :size] = gate_grad
    up_grad = (hidden_grad * (gate * sigmoid)).astype(bf16)
    grads_ref[:, size:] = up_grad
    second = dot(gate_grad, weight_of(weight_ref, 0, size), ((1,), (1,)))
    second += dot(up_grad, weight_of(weight_ref, size, size), ((1,), (1,)))
    unit = unit_ref[...].astype(f32)
    add_sums(sums_ref, second * unit, second)
    back = norm_back(second, unit, inverse_ref[:, 0:1], gain_ref[...]).astype(bf16)
    back_ref[...] = back
    through = dot(back, output_ref[...], ((1,), (1,))).astype(bf16)
    columns = through_ref.shape[2]
    for i in range(through_ref.shape[0]):
        through_ref[i] = through[:, i * columns : (i + 1) * columns]


def feed_back(gate, upper, down_grad, unit, inverse, gain, output_all, pieces, rows, n_seq):
    length, width = down_grad.shape
    size = gate.shape[1]
    n = len(pieces)
    block = block_of(length)
    half = block_spec(block, size)
    full = block_spec(block, width)
    return call_kernel(
        lambda *refs: feed_back_kernel(n, *refs),
        length,
        [
            half,
            half,
            full,
            full,
            block_spec(block, 128),
            whole_spec(1, width),
            once_spec(width, width),
        ]
        + any_specs(n),
        [
            rows_out(length, 2 * size, bf16),
            rows_out(length, width, bf16),
            (
                jax.ShapeDtypeStruct((n_seq, length, width // n_seq), bf16),
                pl.BlockSpec((n_seq, block, width // n_seq), lambda i: (0, i, 0)),
            ),
            sums_out(width),
        ],
        [
            pltpu.VMEM((pieces[0].shape[0], n, rows, 3 * size), bf16),
            pltpu.SemaphoreType.DMA((n,)),
        ],
        (gate, upper, down_grad, unit, inverse, gain, output_all, *pieces),
        "feed_back",
        6 * length * width * size + 2 * length * width * width,
    )


def first_kernel(n, *refs):
    grad_ref, center_ref, gain_ref, back_ref = refs[:4]
    pieces = refs[4 : 4 + n]
    both_ref, sums_ref, bias_ref, weight_ref, sems = refs[4 + n :]
    load_pieces(pieces, weight_ref, sems)
    grad = grad_ref[...]
    first = dot(grad, weight_of(weight_ref, 0, grad.shape[1]), ((1,), (1,)))
    unit, inverse = unit_of_centered(center_ref[...].astype(f32))
    add_sums(sums_ref, first * unit, first)
    add_sums(bias_ref, grad.astype(f32))
    both = back_ref[...].astype(f32) + norm_back(first, unit, inverse, gain_ref[...])
    both_ref[...] = both.astype(bf16)


def first_back(joint_grad, center, gain, back, pieces, rows):
    length, width = center.shape
    total = joint_grad.shape[1]
    n = len(pieces)
    block = block_of(length)
    full = block_spec(block, width)
    return call_kernel(
        lambda *refs: first_kernel(n, *refs),
        length,
        [block_spec(block, total), full, whole_spec(1, width), full] + any_specs(n),
        [rows_out(length, width, bf16), sums_out(width), sums_out(total)],
        [
            pltpu.VMEM((pieces[0].shape[0], n, rows, total), bf16),
            pltpu.SemaphoreType.DMA((n,)),
        ],
        (joint_grad, center, gain, back, *pieces),
        "first_back",
        2 * length * width * total,
    )


def grad_kernel(rows, has_rest, has_below, *refs):
    left_ref, right_ref = refs[:2]
    refs = refs[2:]
    part = dot(left_ref[...], right_ref[...], ((0,), (0,)))
    if has_rest:
        rest_ref, refs = refs[0], refs[1:]
        local = rest_ref.shape[0]
        first = pl.multiple_of(lax.axis_index("seq") * local, local)
        part += dot(left_ref[pl.ds(first, local), :], rest_ref[...], ((0,), (0,)))
    if has_below:
        below_ref, refs = refs[0], refs[1:]
    keep_ref, send_ref, part_ref = refs
    me = lax.axis_index("batch")
    part_ref[...] = part.astype(bf16).reshape(part_ref.shape)
    for far in range(2):
        for near, ref in enumerate((keep_ref, send_ref)):
            batch_at = me ^ (2 * far + near)
            for i in range(part_ref.shape[0]):
                ref[far, i, :rows] = part_ref[i, batch_at]
                if has_below:
                    ref[far, i, rows:] = below_ref[i, batch_at]


def weight_grad(left, right, n_seq, n_batch, rest=None, below=None):
    length, width = left.shape
    c = right.shape[1]
    rows = width // (n_seq * n_batch)
    if n_seq != 8 or n_batch != 4:
        if rest is not None:
            first = lax.axis_index("seq") * rest.shape[0]
            mine = lax.dynamic_slice_in_dim(right, first, rest.shape[0], 0) + rest
            right = lax.dynamic_update_slice_in_dim(right, mine, first, 0)
        part = dot(left, right, ((0,), (0,))).astype(bf16).reshape(n_seq, n_batch, rows, c)
        if below is not None:
            part = jnp.concatenate([part, below], axis=2)
        return part, None
    args = [left, right]
    many = GRAD_BLOCKS
    specs = [pl.BlockSpec((length, many * width // n_seq), lambda i: (0, i)), once_spec(length, c)]
    high = rows
    if rest is not None:
        args.append(rest)
        specs.append(once_spec(*rest.shape))
    if below is not None:
        high += below.shape[2]
        args.append(below)
        specs.append(pl.BlockSpec((many,) + below.shape[1:], lambda i: (i, 0, 0, 0)))
    shape = jax.ShapeDtypeStruct((2, n_seq, high, c), bf16)
    spec = pl.BlockSpec((2, many, high, c), lambda i: (0, i, 0, 0))
    return pl.pallas_call(
        lambda *refs: grad_kernel(rows, rest is not None, below is not None, *refs),
        grid=(n_seq // many,),
        in_specs=specs,
        out_specs=[spec, spec],
        out_shape=[shape, shape],
        scratch_shapes=[pltpu.VMEM((many, n_batch, rows, c), bf16)],
        compiler_params=pltpu.CompilerParams(
            vmem_limit_bytes=VMEM_BYTES, dimension_semantics=("arbitrary",)
        ),
        cost_estimate=pl.CostEstimate(
            flops=2 * length * width * c,
            bytes_accessed=2 * (length * width + length * c + 2 * width * c),
            transcendentals=0,
        ),
        name="weight_grad",
    )(*args)


def unpack_kernel(blocks_ref, *refs):
    parts, (out_ref, vectors_ref) = refs[:3], refs[3:]
    rows = out_ref.shape[0]
    width = out_ref.shape[1] // 3
    columns = blocks_ref.shape[2] // 3
    place = lax.axis_index("seq") // 2
    total = jnp.zeros(vectors_ref.shape, f32)
    for k in range(4):
        far = place ^ k
        for near in range(2):
            at = far * 2 + near
            block = (blocks_ref[at] if k == 0 else parts[k - 1][near]).astype(f32)
            for i in range(3):
                span = pl.ds(pl.multiple_of(i * width + at * columns, columns), columns)
                out_ref[:, span] = block[:rows, i * columns : (i + 1) * columns]
            total += block[rows : rows + 8]
    vectors_ref[...] = total


def unpack_joint(blocks, parts, rows):
    n_seq, _, total = blocks.shape
    return pl.pallas_call(
        unpack_kernel,
        out_shape=(
            jax.ShapeDtypeStruct((rows, n_seq * total), f32),
            jax.ShapeDtypeStruct((8, total), f32),
        ),
        compiler_params=pltpu.CompilerParams(vmem_limit_bytes=VMEM_BYTES),
        cost_estimate=pl.CostEstimate(
            flops=n_seq * rows * total, bytes_accessed=6 * n_seq * rows * total, transcendentals=0
        ),
        name="unpack_joint",
    )(blocks, *parts)


def grad_near(halves, n_batch):
    keep, send = halves
    if send is None:
        return scatter_near(keep, n_batch), None
    return keep, swap(send, "batch", n_batch, 1)


def grad_far_begin(halves, n_batch):
    keep, got = halves
    if got is None:
        return scatter_far(keep, n_batch), None
    send = (keep[1].astype(f32) + got[1].astype(f32)).astype(bf16)
    return (keep, got), swap(send, "batch", n_batch, 2)


def grad_far_end(state):
    halves, other = state
    if other is None:
        return halves
    keep, got = halves
    return (keep[0].astype(f32) + got[0].astype(f32) + other.astype(f32)).astype(bf16)


def make_body(n_seq, n_batch):
    def body(
        tokens,
        language,
        language_weight,
        output_grad,
        attention_gain,
        attention_shift,
        joint_weight,
        joint_bias,
        output_weight,
        feedfwd_gain,
        feedfwd_shift,
        gate_weight,
        up_weight,
        down_weight,
    ):
        _, local, width = tokens.shape
        rows, ff_width = gate_weight.shape
        length = local * n_seq
        columns = width // n_seq
        tiles = -(-ff_width // (128 * n_seq))
        ff_local = 128 * tiles
        seq_at = lax.axis_index("seq")
        first_row = seq_at * local
        values = tokens[0]
        tables = [jnp.asarray(t) for t in turn_tables(length)]

        center_own = values - mean_of(values)
        ring = Gather(jnp.concatenate([center_own.astype(bf16), output_weight]), n_seq)

        chosen = language[:, None] == jnp.arange(LANGS, dtype=jnp.int32)[None, :]
        row_scale = jnp.sum(jnp.where(chosen, language_weight[None, :], 0.0), axis=1)
        cotangent = output_grad[0] * row_scale[:, None]

        small = jnp.concatenate(
            [attention_gain, attention_shift, feedfwd_gain, feedfwd_shift, joint_bias]
        )
        small = jnp.pad(small[None], ((0, 15), (0, 3 * columns - small.shape[0])))
        blocks = jnp.transpose(joint_weight.reshape(rows, 3, n_seq, columns), (2, 0, 1, 3))
        blocks = blocks.reshape(n_seq, rows, 3 * columns)
        blocks = jnp.concatenate(
            [blocks, jnp.broadcast_to(small[None], (n_seq,) + small.shape)], axis=1
        )
        ff_blocks = [
            jnp.pad(w, ((0, 0), (0, n_seq * ff_local - ff_width))).reshape(rows, tiles, n_seq, 128)
            for w in (gate_weight, up_weight, down_weight)
        ]
        ff_blocks = jnp.transpose(jnp.stack(ff_blocks, 1), (3, 0, 1, 2, 4))
        ff_blocks = ff_blocks.reshape(n_seq, rows, 3 * ff_local)

        ring.step()
        flight = exchange_begin(blocks, n_seq, 1)
        ff_flight = exchange_begin(ff_blocks, n_seq, 4)
        (flight,) = ring.tie(flight)
        blocks = exchange_end(flight, n_seq, 1)
        ring.step()
        flight = exchange_begin(blocks, n_seq, 2)
        flight, ff_flight, down_grad = ring.tie(flight, ff_flight, cotangent.astype(bf16))
        down_grad = lax.all_gather(down_grad, "seq", axis=0, tiled=True)
        blocks = exchange_end(flight, n_seq, 2)
        ff_blocks = rest_of_exchange(exchange_end(ff_flight, n_seq, 4), n_seq)
        ring.step()
        flight = exchange_begin(blocks, n_seq, 4)
        ff_flight = exchange_begin(ff_blocks, n_seq, 1)
        flight, ff_flight = ring.tie(flight, ff_flight)
        blocks = rest_of_exchange(exchange_end(flight, n_seq, 4), n_seq)
        ff_blocks = exchange_end(ff_flight, n_seq, 1)
        ring.step()
        held = gather_far(blocks, n_batch)
        ff_flight = exchange_begin(ff_blocks, n_seq, 2)
        (held_last,) = ring.tie(held[-1][1])
        held[-1] = (held[-1][0], held_last)
        pieces = gather_near(held, n_batch)
        center_pieces = [v for _, v in ring.pieces]
        output_held = jnp.concatenate([v[local:] for v in center_pieces])
        output_held, *pieces = tie(output_held, *pieces)
        output_held = gather_far(output_held, n_batch)

        small = jnp.stack([v[:, rows] for v in pieces], axis=1)
        batch_at = lax.axis_index("batch")
        for bit in bits_of(n_batch):
            flipped = small.reshape(n_seq, -1, 2, bit, small.shape[2])[:, :, ::-1]
            small = jnp.where((batch_at & bit) == 0, small, flipped.reshape(small.shape))
        piece = width // (n_seq * n_batch)

        def small_part(start, size):
            return small[:, :, start : start + size].reshape(1, -1).astype(f32)

        gain_one = small_part(0, piece)
        shift_one = small_part(piece, piece)
        gain_two = small_part(2 * piece, piece)
        shift_two = small_part(3 * piece, piece)
        bias_all = small_part(4 * piece, 3 * piece).reshape(3, n_seq, columns)
        bias = lax.dynamic_slice_in_dim(bias_all, seq_at, 1, 1).reshape(1, 3 * columns)

        low, first_input, center = make_heads(
            center_pieces, gain_one, shift_one, bias, tables, pieces, rows, local
        )
        context, mixed, lse = attend(low)

        mixed, held_last, ff_flight = tie(mixed, output_held[-1][1], ff_flight)
        output_held[-1] = (output_held[-1][0], held_last)
        ring = Gather(mixed, n_seq)
        ring.step()
        held = gather_far(exchange_end(ff_flight, n_seq, 2), n_batch)
        ring.tie()
        ring.step()
        output_pieces = gather_near(output_held, n_batch)
        output_pieces = ring.tie(*output_pieces)
        ring.step()
        ring.tie()
        ring.step()
        (held_last,) = ring.tie(held[-1][1])
        held[-1] = (held[-1][0], held_last)
        ff_pieces = gather_near(held, n_batch)
        mixed_pieces = [v for _, v in ring.pieces]
        if columns % 128:
            mixed_pieces = [join(ring.pieces, n_seq, 1)]
        second_input, unit_two, inverse_two, mixed_all, output_all = make_middle(
            mixed_pieces, output_pieces, center, gain_two, shift_two, n_seq, rows
        )
        output_all = output_all.reshape(width, width)

        gate, upper, hidden, result_part = feed(second_input, ff_pieces, rows)
        middle_grads, back, through, second_sums = feed_back(
            gate,
            upper,
            down_grad,
            unit_two,
            inverse_two,
            gain_two,
            output_all,
            ff_pieces,
            rows,
            n_seq,
        )
        result_sum = lax.psum_scatter(result_part, "seq", scatter_dimension=0, tiled=True)

        def own(array):
            return lax.dynamic_slice_in_dim(array, first_row, local, 0)

        ring = Scatter(lambda at: lax.dynamic_index_in_dim(through, at, 0, False), n_seq)
        ring.step()
        grad_down = weight_grad(down_grad, hidden, n_seq, n_batch)
        (grad_down,) = ring.tie(grad_down)
        ring.step()
        grad_down = grad_near(grad_down, n_batch)
        grad_both = weight_grad(second_input, middle_grads, n_seq, n_batch)
        grad_both, grad_down = ring.tie(grad_both, grad_down)
        ring.step()
        grad_both = grad_near(grad_both, n_batch)
        grad_down = grad_far_begin(grad_down, n_batch)
        grad_output = weight_grad(
            mixed_all, back, n_seq, n_batch, rest=cotangent.astype(bf16)
        )
        grad_both, grad_output, grad_down, result_sum = ring.tie(
            grad_both, grad_output, grad_down, result_sum
        )
        ring.step()
        grad_both = grad_far_begin(grad_both, n_batch)
        grad_output = grad_near(grad_output, n_batch)
        grad_down = exchange_begin(grad_far_end(grad_down), n_seq, 4)
        heads_weight = lax.dynamic_slice_in_dim(output_all, seq_at * columns, columns, 0)
        from_cot = dot(down_grad, heads_weight, ((1,), (1,)))
        from_cot, grad_output = ring.tie(from_cot, grad_output)
        context_grad = (ring.total() + from_cot).astype(bf16)
        joint_grad = attend_back(low, context_grad, context, lse, tables)
        joint_grad, grad_both, grad_down = tie(joint_grad, grad_both, grad_down)
        grad_output = grad_far_begin(grad_output, n_batch)
        grad_both = exchange_begin(grad_far_end(grad_both), n_seq, 4)
        grad_down = rest_of_exchange(exchange_end(grad_down, n_seq, 4), n_seq)
        grad_down = exchange_begin(grad_down, n_seq, 1)
        both, first_sums, bias_sums = first_back(joint_grad, center, gain_one, back, pieces, rows)

        ring = Scatter(lambda at: lax.dynamic_slice_in_dim(both, at * local, local, 0), n_seq)
        ring.step()
        bias_part = lax.dynamic_update_slice_in_dim(
            jnp.zeros((3, n_seq, columns), f32), bias_sums[:1].reshape(3, 1, columns), seq_at, 1
        )
        vectors = [first_sums[0], first_sums[1], second_sums[0], second_sums[1], bias_part]
        vectors = [v.reshape(n_seq, n_batch, 1, -1).astype(bf16) for v in vectors]
        vectors = jnp.concatenate(vectors, axis=3)
        vectors = jnp.pad(vectors, ((0, 0), (0, 0), (0, 15), (0, 3 * columns - 7 * piece)))
        grad_joint = weight_grad(first_input, joint_grad, n_seq, n_batch, below=vectors)
        grad_joint, grad_down, grad_both, grad_output = ring.tie(
            grad_joint, grad_down, grad_both, grad_output
        )
        grad_output = lax.psum_scatter(
            grad_far_end(grad_output), "seq", scatter_dimension=0, tiled=False
        )
        ring.step()
        grad_joint = grad_near(grad_joint, n_batch)
        grad_both = rest_of_exchange(exchange_end(grad_both, n_seq, 4), n_seq)
        grad_both = exchange_begin(grad_both, n_seq, 1)
        (grad_joint,) = ring.tie(grad_joint)
        ring.step()
        grad_joint = grad_far_begin(grad_joint, n_batch)
        grad_down = exchange_begin(exchange_end(grad_down, n_seq, 1), n_seq, 2)
        projected_own = dot(own(mixed_all), output_all, ((1,), (0,)))
        result = values + projected_own + result_sum.astype(f32)
        grad_joint, grad_both, grad_down, result = ring.tie(
            grad_joint, grad_both, grad_down, result
        )
        grad_down = exchange_end(grad_down, n_seq, 2)
        ring.step()
        grad_joint = exchange_begin(grad_far_end(grad_joint), n_seq, 1)
        grad_both = exchange_begin(exchange_end(grad_both, n_seq, 1), n_seq, 2)
        (grad_joint,) = ring.tie(grad_joint)
        grad_joint = exchange_end(grad_joint, n_seq, 1)
        if n_seq == 8:
            parts = exchange_parts(grad_joint)
        grad_both = exchange_end(grad_both, n_seq, 2)
        token_grad = cotangent + ring.total()
        grad_output = grad_output.astype(f32)

        def unsplit(grad):
            grad = grad.reshape(n_seq, rows, tiles, 128).astype(f32)
            return jnp.transpose(grad, (1, 2, 0, 3)).reshape(rows, n_seq * ff_local)[:, :ff_width]

        grad_gate = unsplit(grad_both[:, :, :ff_local])
        grad_up = unsplit(grad_both[:, :, ff_local:])
        grad_down = unsplit(grad_down)
        if n_seq == 8:
            done = tie(*parts, grad_gate, grad_up, grad_down, token_grad)
            parts, (grad_gate, grad_up, grad_down, token_grad) = done[:3], done[3:]
            grad_joint, vectors = unpack_joint(grad_joint, parts, rows)
            vectors = vectors[0]
        else:
            grad_joint = exchange_far(grad_joint, n_seq).astype(f32)
            vectors = jnp.sum(grad_joint[:, rows], axis=0)
            grad_joint = grad_joint[:, :rows].reshape(n_seq, rows, 3, columns)
            grad_joint = jnp.transpose(grad_joint, (1, 2, 0, 3)).reshape(rows, 3 * width)
        return (
            result[None],
            token_grad[None],
            vectors[:piece],
            vectors[piece : 2 * piece],
            grad_joint,
            vectors[4 * piece : 7 * piece],
            grad_output,
            vectors[2 * piece : 3 * piece],
            vectors[3 * piece : 4 * piece],
            grad_gate,
            grad_up,
            grad_down,
        )

    return body


def solution(mesh):
    rows = P(("seq", "batch"))
    matrix = P(("seq", "batch"), None)
    data = P("batch", "seq", None)
    return jax.shard_map(
        make_body(mesh.shape["seq"], mesh.shape["batch"]),
        mesh=mesh,
        in_specs=(
            data,
            P("batch"),
            P(),
            data,
            rows,
            rows,
            matrix,
            rows,
            matrix,
            rows,
            rows,
            matrix,
            matrix,
            matrix,
        ),
        out_specs=(data, data, rows, rows, matrix, rows, matrix, rows, rows, matrix, matrix, matrix),
        check_vma=False,
    )
```

```python
import math

import numpy as np

import jax
import jax.numpy as jnp
from jax import lax
from jax.experimental import pallas as pl
from jax.experimental.pallas import tpu as pltpu
from jax.sharding import PartitionSpec as P

HEADS = 32
HEAD_DIM = 64
ROT_DIMS = 16
LANGS = 7

EPSILON = 1e-05
THETA_BASE = 10000.0
NEGATIVE = -1e30
VMEM_BYTES = 56 * 1024 * 1024
GRAD_BLOCKS = 2

bf16 = jnp.bfloat16
f32 = jnp.float32


def swap(value, axis, number, bit):
    return lax.ppermute(value, axis, [(i, i ^ bit) for i in range(number)])


def bits_of(number):
    return [1 << i for i in range(number.bit_length() - 1)]


def tie(*values):
    return lax.optimization_barrier(values)


def after(value, *others):
    return tie(value, *others)[0]


def exchange_begin(blocks, number, bit):
    mine = (lax.axis_index("seq") // bit) % 2
    pairs = blocks.reshape((number // (2 * bit), 2, bit) + blocks.shape[1:])
    return pairs, swap(lax.dynamic_slice_in_dim(pairs, 1 - mine, 1, 1), "seq", number, bit)


def exchange_end(state, number, bit):
    pairs, got = state
    mine = (lax.axis_index("seq") // bit) % 2
    out = lax.dynamic_update_slice_in_dim(pairs, got, 1 - mine, 1)
    return out.reshape((number,) + pairs.shape[3:])


def exchange(blocks, number, bit):
    return exchange_end(exchange_begin(blocks, number, bit), number, bit)


def exchange_far(blocks, number):
    for bit in bits_of(number)[1:]:
        blocks = exchange(blocks, number, bit)
    return blocks


def exchange_parts(blocks):
    place = lax.axis_index("seq") // 2
    pairs = blocks.reshape((4, 2) + blocks.shape[1:])
    return [
        swap(lax.dynamic_slice_in_dim(pairs, place ^ k, 1, 0), "seq", 8, k * 2)[0]
        for k in range(1, 4)
    ]


def rest_of_exchange(blocks, number):
    for bit in bits_of(number)[3:]:
        blocks = exchange(blocks, number, bit)
    return blocks


def gather_far(value, number):
    held = [(0, value)]
    for bit in reversed(bits_of(number)[1:]):
        held = held + [(k ^ bit, swap(v, "batch", number, bit)) for k, v in held]
    return held


def gather_near(held, number):
    held = dict(held + [(k ^ 1, swap(v, "batch", number, 1)) for k, v in held])
    return [held[k] for k in range(number)]


def scatter_stage(value, number, bit):
    n, _, r, c = value.shape
    pairs = value.reshape(n, -1, 2, r, c)
    mine = (lax.axis_index("batch") // bit) % 2
    keep = lax.dynamic_index_in_dim(pairs, mine, 2, False)
    send = lax.dynamic_index_in_dim(pairs, 1 - mine, 2, False).astype(bf16)
    return (keep.astype(f32) + swap(send, "batch", number, bit).astype(f32)).astype(bf16)


def scatter_near(value, number):
    return scatter_stage(value, number, 1)


def scatter_far(value, number):
    for bit in bits_of(number)[1:]:
        value = scatter_stage(value, number, bit)
    return value[:, 0]


RING = (0, 2, 4, 6, 7, 5, 3, 1)


def ring_place():
    s = lax.axis_index("seq")
    return jnp.where(s % 2 == 0, s // 2, 7 - s // 2)


def ring_index(place):
    place = (place + 16) % 8
    return jnp.where(place < 4, 2 * place, 15 - 2 * place)


ARRIVAL = (0, 1, -1, 2, -2, 3, -3, -4)


def arrival(number):
    if number != 8:
        return list(range(number))
    return [ring_index(ring_place() + step) for step in ARRIVAL]


def ring_step(value, way):
    return lax.ppermute(value, "seq", [(RING[i], RING[(i + way) % 8]) for i in range(8)])


class Ring:
    ahead = behind = None
    taken = 0

    def tie(self, *others):
        if self.number != 8:
            return others
        self.ahead, self.behind, *others = tie(self.ahead, self.behind, *others)
        return others


class Gather(Ring):
    def __init__(self, value, number):
        self.number = number
        if number != 8:
            every = lax.all_gather(value, "seq", axis=0, tiled=False)
            self.pieces = [(i, every[i]) for i in range(number)]
            return
        self.pieces = [(lax.axis_index("seq"), value)]
        self.ahead = self.behind = value
        self.place = ring_place()

    def step(self):
        if self.number != 8:
            return
        self.taken += 1
        k = self.taken
        self.ahead = ring_step(self.ahead, 1)
        if k < 4:
            self.behind = ring_step(self.behind, -1)
            self.pieces.append((ring_index(self.place + k), self.behind))
        self.pieces.append((ring_index(self.place - k), self.ahead))


class Scatter(Ring):
    def __init__(self, block, number):
        self.number = number
        self.block = block
        self.place = ring_place()

    def step(self):
        if self.number != 8:
            return
        k = 4 - self.taken
        self.taken += 1
        part = self.block(ring_index(self.place + k))
        if self.ahead is not None:
            part = (part.astype(f32) + self.ahead.astype(f32)).astype(bf16)
        self.ahead = ring_step(part, 1)
        if k > 1:
            part = self.block(ring_index(self.place - k + 1))
            if self.behind is not None:
                part = (part.astype(f32) + self.behind.astype(f32)).astype(bf16)
            self.behind = ring_step(part, -1)

    def total(self):
        if self.number != 8:
            every = jnp.stack([self.block(i) for i in range(self.number)])
            return lax.psum_scatter(every, "seq", scatter_dimension=0, tiled=False).astype(f32)
        own = self.block(lax.axis_index("seq"))
        return own.astype(f32) + self.ahead.astype(f32) + self.behind.astype(f32)


def join(pieces, number, axis):
    at, first = pieces[0]
    size = first.shape[axis]
    shape = first.shape[:axis] + (number * size,) + first.shape[axis + 1 :]
    out = jnp.zeros(shape, first.dtype)
    for at, piece in pieces:
        out = lax.dynamic_update_slice_in_dim(out, piece, at * size, axis)
    return out


def turn_tables(length):
    half = ROT_DIMS // 2
    frequency = THETA_BASE ** (-np.arange(half, dtype=np.float32) / np.float32(half))
    angle = (np.arange(length, dtype=np.float32)[:, None] * frequency.astype(np.float32)[None]).astype(
        np.float32
    )
    cosine = np.ones((length, HEAD_DIM), np.float32)
    left = np.zeros((length, HEAD_DIM), np.float32)
    right = np.zeros((length, HEAD_DIM), np.float32)
    cosine[:, :half] = np.cos(angle)
    cosine[:, half:ROT_DIMS] = np.cos(angle)
    left[:, :half] = -np.sin(angle)
    right[:, half:ROT_DIMS] = np.sin(angle)
    return [np.concatenate([t, t], 1) for t in (cosine, left, right)]


def wide(table, columns):
    if columns < table.shape[1]:
        return table[:, :columns]
    return jnp.concatenate([table] * (columns // table.shape[1]), axis=1)


def lane_roll(value, amount):
    columns = value.shape[1]
    if columns % 128 == 0:
        return pltpu.roll(value, amount % columns, 1)
    amount = amount % columns
    return jnp.concatenate([value[:, columns - amount :], value[:, : columns - amount]], axis=1)


def turn(value, cosine, left, right):
    half = ROT_DIMS // 2
    return value * cosine + lane_roll(value, -half) * left + lane_roll(value, half) * right


def turn_back(value, cosine, left, right):
    half = ROT_DIMS // 2
    return value * cosine - lane_roll(value, -half) * left - lane_roll(value, half) * right


def head_mask(columns, head):
    lane = lax.broadcasted_iota(jnp.int32, (1, columns), 1)
    return (lane >= head * HEAD_DIM) & (lane < (head + 1) * HEAD_DIM)


def block_of(length):
    return math.gcd(length, 256)


def attend_kernel(low_ref, context_ref, mixed_ref, lse_ref):
    length, total = low_ref.shape
    columns = total // 3
    heads = columns // HEAD_DIM
    block = block_of(length)
    for i in range(length // block):
        rows = pl.ds(i * block, block)
        reach = (i + 1) * block
        query = low_ref[rows, 0:columns]
        key = low_ref[0:reach, columns : 2 * columns]
        value = low_ref[0:reach, 2 * columns :]
        total_out = jnp.zeros((block, columns), f32)
        lse_all = jnp.zeros((block, 128), f32)
        lane = lax.broadcasted_iota(jnp.int32, (block, 128), 1)
        ahead = lax.broadcasted_iota(jnp.int32, (block, reach), 1) > (
            i * block + lax.broadcasted_iota(jnp.int32, (block, reach), 0)
        )
        for h in range(heads):
            mask = head_mask(columns, h)
            scores = lax.dot_general(
                jnp.where(mask, query, jnp.zeros_like(query)),
                key,
                (((1,), (1,)), ((), ())),
                preferred_element_type=f32,
            )
            scores = jnp.where(ahead, NEGATIVE, scores)
            top = jnp.max(scores, axis=1, keepdims=True)
            weight = jnp.exp(scores - top)
            denominator = jnp.sum(weight, axis=1, keepdims=True)
            probs = (weight * (1.0 / denominator)).astype(bf16)
            total_out += jnp.dot(
                probs, jnp.where(mask, value, jnp.zeros_like(value)), preferred_element_type=f32
            )
            lse_all = jnp.where(lane == h, top + jnp.log(denominator), lse_all)
        context_ref[rows, :] = total_out
        mixed_ref[rows, :] = total_out.astype(bf16)
        lse_ref[rows, :] = lse_all


def attend(low):
    length, total = low.shape
    columns = total // 3
    return pl.pallas_call(
        attend_kernel,
        out_shape=(
            jax.ShapeDtypeStruct((length, columns), f32),
            jax.ShapeDtypeStruct((length, columns), bf16),
            jax.ShapeDtypeStruct((length, 128), f32),
        ),
        compiler_params=pltpu.CompilerParams(vmem_limit_bytes=VMEM_BYTES),
        cost_estimate=pl.CostEstimate(
            flops=4 * length * length * columns * 2,
            bytes_accessed=16 * length * total,
            transcendentals=length * length * columns // HEAD_DIM,
        ),
        name="attend",
    )(low)


def attend_back_kernel(
    low_ref, grad_ref, context_ref, lse_ref, cos_ref, left_ref, right_ref, out_ref, dq_ref, dk_ref, dv_ref
):
    length, total = low_ref.shape
    columns = total // 3
    heads = columns // HEAD_DIM
    block = block_of(length)
    scale = 1.0 / math.sqrt(HEAD_DIM)
    dk_ref[...] = jnp.zeros_like(dk_ref)
    dv_ref[...] = jnp.zeros_like(dv_ref)
    for i in range(length // block):
        rows = pl.ds(i * block, block)
        reach = (i + 1) * block
        query = low_ref[rows, 0:columns]
        grad = grad_ref[rows, :]
        grad_wide = grad.astype(f32)
        query_t = query.astype(f32).T.astype(bf16)
        grad_t = grad_wide.T.astype(bf16)
        product = grad_wide * context_ref[rows, :]
        key = low_ref[0:reach, columns : 2 * columns]
        value = low_ref[0:reach, 2 * columns :]
        dq = jnp.zeros((block, columns), f32)
        ahead = lax.broadcasted_iota(jnp.int32, (block, reach), 1) > (
            i * block + lax.broadcasted_iota(jnp.int32, (block, reach), 0)
        )
        for h in range(heads):
            mask = head_mask(columns, h)
            span = slice(h * HEAD_DIM, (h + 1) * HEAD_DIM)
            scores = lax.dot_general(
                jnp.where(mask, query, jnp.zeros_like(query)),
                key,
                (((1,), (1,)), ((), ())),
                preferred_element_type=f32,
            )
            scores = jnp.where(ahead, NEGATIVE, scores)
            probs = jnp.exp(scores - lse_ref[rows, h : h + 1])
            dots = lax.dot_general(
                jnp.where(mask, grad, jnp.zeros_like(grad)),
                value,
                (((1,), (1,)), ((), ())),
                preferred_element_type=f32,
            )
            balance = jnp.sum(jnp.where(mask, product, 0.0), axis=1, keepdims=True)
            score_grad = (probs * (dots - balance)).astype(bf16)
            dq += jnp.dot(
                score_grad, jnp.where(mask, key, jnp.zeros_like(key)), preferred_element_type=f32
            )
            dk_ref[span, 0:reach] += jnp.dot(query_t[span], score_grad, preferred_element_type=f32)
            dv_ref[span, 0:reach] += jnp.dot(
                grad_t[span], probs.astype(bf16), preferred_element_type=f32
            )
        dq_ref[rows, :] = dq
    for i in range(length // block):
        rows = pl.ds(i * block, block)
        tables = [wide(t[rows, :], columns) for t in (cos_ref, left_ref, right_ref)]
        out_ref[rows, 0:columns] = turn_back(dq_ref[rows, :] * scale, *tables).astype(bf16)
        out_ref[rows, columns : 2 * columns] = turn_back(dk_ref[:, rows].T, *tables).astype(bf16)
        out_ref[rows, 2 * columns :] = dv_ref[:, rows].T.astype(bf16)


def attend_back(low, grad, context, lse, tables):
    length, total = low.shape
    columns = total // 3
    return pl.pallas_call(
        attend_back_kernel,
        out_shape=jax.ShapeDtypeStruct((length, total), bf16),
        scratch_shapes=[
            pltpu.VMEM((length, columns), f32),
            pltpu.VMEM((columns, length), f32),
            pltpu.VMEM((columns, length), f32),
        ],
        compiler_params=pltpu.CompilerParams(vmem_limit_bytes=VMEM_BYTES),
        cost_estimate=pl.CostEstimate(
            flops=10 * length * length * columns * 2,
            bytes_accessed=16 * length * total,
            transcendentals=length * length * columns // HEAD_DIM,
        ),
        name="attend_back",
    )(low, grad, context, lse, *tables)


def mean_of(values):
    return jnp.mean(values, axis=-1, keepdims=True)


def unit_of(values):
    center = values - mean_of(values)
    inverse_std = lax.rsqrt(mean_of(center * center) + EPSILON)
    return center * inverse_std, inverse_std


def unit_of_centered(center):
    inverse_std = lax.rsqrt(mean_of(center * center) + EPSILON)
    return center * inverse_std, inverse_std


def norm_back(incoming, unit_rows, inverse_std, gain_values):
    inner = incoming * gain_values
    return inverse_std * (inner - mean_of(inner) - unit_rows * mean_of(inner * unit_rows))


def dot(left, right, contract):
    return lax.dot_general(left, right, (contract, ((), ())), preferred_element_type=f32)


def block_spec(block, columns):
    return pl.BlockSpec((block, columns), lambda i: (i, 0))


def whole_spec(rows, columns):
    return pl.BlockSpec((rows, columns), lambda i: (0, 0))


def once_spec(rows, columns):
    return pl.BlockSpec((rows, columns), lambda i: (0, 0), pipeline_mode=pl.Buffered(1))


def any_specs(number):
    return [pl.BlockSpec(memory_space=pl.ANY)] * number


def run_copies(copies, sems):
    copies = [pltpu.make_async_copy(*pair, sems.at[i]) for i, pair in enumerate(copies)]
    for copy in copies:
        copy.start()
    for copy in copies:
        copy.wait()


def weight_copies(piece_refs, weight_ref):
    me = lax.axis_index("batch")
    rows = weight_ref.shape[2]
    return [
        (ref.at[:, pl.ds(0, rows), :], weight_ref.at[:, me ^ k])
        for k, ref in enumerate(piece_refs)
    ]


def load_pieces(piece_refs, weight_ref, sems):
    @pl.when(pl.program_id(0) == 0)
    def _():
        run_copies(weight_copies(piece_refs, weight_ref), sems)


def weight_of(weight_ref, start, size):
    part = weight_ref[:, :, :, start : start + size]
    return part.reshape(-1, size)


def call_kernel(kernel, length, in_specs, out, scratch, args, name, flops):
    block = block_of(length)
    return pl.pallas_call(
        kernel,
        grid=(length // block,),
        in_specs=in_specs,
        out_specs=[spec for _, spec in out],
        out_shape=[shape for shape, _ in out],
        scratch_shapes=scratch,
        compiler_params=pltpu.CompilerParams(
            vmem_limit_bytes=VMEM_BYTES, dimension_semantics=("arbitrary",)
        ),
        cost_estimate=pl.CostEstimate(
            flops=flops, bytes_accessed=flops // 500, transcendentals=0
        ),
        name=name,
    )(*args)


def rows_out(length, columns, kind):
    return (jax.ShapeDtypeStruct((length, columns), kind), block_spec(block_of(length), columns))


def sums_out(columns):
    return (jax.ShapeDtypeStruct((8, columns), f32), whole_spec(8, columns))


def add_sums(ref, *rows):
    @pl.when(pl.program_id(0) == 0)
    def _():
        ref[...] = jnp.zeros_like(ref)

    for i, row in enumerate(rows):
        ref[i : i + 1, :] += jnp.sum(row, axis=0, keepdims=True)


def heads_kernel(n, n_seq, *refs):
    gain_ref, shift_ref, bias_ref, cos_ref, left_ref, right_ref = refs[:6]
    pieces = refs[6 : 6 + n]
    center_pieces = refs[6 + n : 6 + n + n_seq]
    low_ref, input_ref, center_ref, weight_ref, all_ref, sems = refs[6 + n + n_seq :]
    local = all_ref.shape[1]

    @pl.when(pl.program_id(0) == 0)
    def _():
        copies = [
            (ref.at[pl.ds(0, local), :], all_ref.at[at])
            for at, ref in zip(arrival(n_seq), center_pieces)
        ]
        run_copies(copies + weight_copies(pieces, weight_ref), sems)

    total = low_ref.shape[1]
    columns = total // 3
    block, width = center_ref.shape
    many = block // local
    center = all_ref[pl.ds(pl.program_id(0) * many, many)].reshape(block, width)
    center_ref[...] = center
    unit, _ = unit_of_centered(center.astype(f32))
    first_input = (unit * gain_ref[...] + shift_ref[...]).astype(bf16)
    input_ref[...] = first_input
    joint = dot(first_input, weight_of(weight_ref, 0, total), ((1,), (0,))) + bias_ref[...]
    tables = [wide(t[...], columns) for t in (cos_ref, left_ref, right_ref)]
    scale = 1.0 / math.sqrt(HEAD_DIM)
    query = turn(joint[:, :columns], *tables).astype(bf16)
    low_ref[:, :columns] = (query.astype(f32) * scale).astype(bf16)
    low_ref[:, columns : 2 * columns] = turn(joint[:, columns : 2 * columns], *tables).astype(bf16)
    low_ref[:, 2 * columns :] = joint[:, 2 * columns :].astype(bf16)


def make_heads(center_pieces, gain, shift, bias, tables, pieces, rows, local):
    n_seq, n = len(center_pieces), len(pieces)
    length, width = local * n_seq, gain.shape[1]
    total = bias.shape[1]
    block = block_of(length)
    return call_kernel(
        lambda *refs: heads_kernel(n, n_seq, *refs),
        length,
        [whole_spec(1, width), whole_spec(1, width), whole_spec(1, total)]
        + [block_spec(block, 128)] * 3
        + any_specs(n + n_seq),
        [
            rows_out(length, total, bf16),
            rows_out(length, width, bf16),
            rows_out(length, width, bf16),
        ],
        [
            pltpu.VMEM((n_seq, n, rows, total), bf16),
            pltpu.VMEM((n_seq, local, width), bf16),
            pltpu.SemaphoreType.DMA((n + n_seq,)),
        ],
        (gain, shift, bias, *tables, *pieces, *center_pieces),
        "make_heads",
        2 * length * width * total,
    )


def middle_kernel(n, n_seq, many, *refs):
    center_ref, gain_ref, shift_ref = refs[:3]
    pieces, mixed_pieces = refs[3 : 3 + n], refs[3 + n : 3 + n + many]
    input_ref, unit_ref, inverse_ref, mixed_ref, out_ref = refs[3 + n + many : 8 + n + many]
    weight_ref, all_ref, sems, out_sem = refs[8 + n + many :]
    rows, width = weight_ref.shape[2:]
    columns = width // n_seq
    step = pl.program_id(0)
    give = pltpu.make_async_copy(weight_ref, out_ref, out_sem)

    @pl.when(step == 0)
    def _():
        me = lax.axis_index("batch")
        places = arrival(n_seq)
        copies = [
            (ref.at[pl.ds(j * rows, rows), :], weight_ref.at[at, me ^ k])
            for k, ref in enumerate(pieces)
            for j, at in enumerate(places)
        ]
        if many == 1:
            copies.append((mixed_pieces[0], all_ref))
        else:
            for at, ref in zip(places, mixed_pieces):
                span = pl.ds(pl.multiple_of(at * columns, columns), columns)
                copies.append((ref, all_ref.at[:, span]))
        run_copies(copies, sems)
        give.start()

    block = center_ref.shape[0]
    mixed = all_ref[pl.ds(pl.multiple_of(step * block, block), block), :]
    mixed_ref[...] = mixed
    projected = dot(mixed, weight_ref[...].reshape(width, width), ((1,), (0,)))
    unit, inverse = unit_of(center_ref[...].astype(f32) + projected)
    input_ref[...] = (unit * gain_ref[...] + shift_ref[...]).astype(bf16)
    unit_ref[...] = unit.astype(bf16)
    inverse_ref[...] = jnp.broadcast_to(inverse, inverse_ref.shape)

    @pl.when(step == pl.num_programs(0) - 1)
    def _():
        give.wait()


def make_middle(mixed_pieces, pieces, center, gain, shift, n_seq, rows):
    length, width = center.shape
    n, many = len(pieces), len(mixed_pieces)
    block = block_of(length)
    row = whole_spec(1, width)
    weight_shape = (n_seq, n, rows, width)
    return call_kernel(
        lambda *refs: middle_kernel(n, n_seq, many, *refs),
        length,
        [block_spec(block, width), row, row] + any_specs(n + many),
        [
            rows_out(length, width, bf16),
            rows_out(length, width, bf16),
            rows_out(length, 128, f32),
            rows_out(length, width, bf16),
            (jax.ShapeDtypeStruct(weight_shape, bf16), pl.BlockSpec(memory_space=pl.ANY)),
        ],
        [
            pltpu.VMEM(weight_shape, bf16),
            pltpu.VMEM((length, width), bf16),
            pltpu.SemaphoreType.DMA((n * n_seq + many,)),
            pltpu.SemaphoreType.DMA,
        ],
        (center, gain, shift, *pieces, *mixed_pieces),
        "make_middle",
        2 * length * width * width,
    )


def feed_kernel(n, *refs):
    input_ref = refs[0]
    pieces = refs[1 : 1 + n]
    gate_ref, upper_ref, hidden_ref, result_ref, weight_ref, sems = refs[1 + n :]
    load_pieces(pieces, weight_ref, sems)
    size = hidden_ref.shape[1]
    second_input = input_ref[...]
    gate = dot(second_input, weight_of(weight_ref, 0, size), ((1,), (0,)))
    upper = dot(second_input, weight_of(weight_ref, size, size), ((1,), (0,)))
    gate_ref[...] = gate
    upper_ref[...] = upper
    hidden = (gate * jax.nn.sigmoid(gate) * upper).astype(bf16)
    hidden_ref[...] = hidden
    result_ref[...] = dot(hidden, weight_of(weight_ref, 2 * size, size), ((1,), (1,))).astype(bf16)


def feed(second_input, pieces, rows):
    length, width = second_input.shape
    size = pieces[0].shape[2] // 3
    n = len(pieces)
    return call_kernel(
        lambda *refs: feed_kernel(n, *refs),
        length,
        [block_spec(block_of(length), width)] + any_specs(n),
        [rows_out(length, size, f32)] * 2
        + [rows_out(length, size, bf16), rows_out(length, width, bf16)],
        [
            pltpu.VMEM((pieces[0].shape[0], n, rows, 3 * size), bf16),
            pltpu.SemaphoreType.DMA((n,)),
        ],
        (second_input, *pieces),
        "feed",
        6 * length * width * size,
    )


def feed_back_kernel(n, *refs):
    gate_ref, upper_ref, grad_ref, unit_ref, inverse_ref, gain_ref, output_ref = refs[:7]
    pieces = refs[7 : 7 + n]
    grads_ref, back_ref, through_ref, sums_ref, weight_ref, sems = refs[7 + n :]
    load_pieces(pieces, weight_ref, sems)
    size = gate_ref.shape[1]
    gate = gate_ref[...]
    upper = upper_ref[...]
    hidden_grad = dot(grad_ref[...], weight_of(weight_ref, 2 * size, size), ((1,), (0,)))
    sigmoid = jax.nn.sigmoid(gate)
    gate_grad = (hidden_grad * upper * sigmoid * (1.0 + gate * (1.0 - sigmoid))).astype(bf16)
    grads_ref[:, :size] = gate_grad
    up_grad = (hidden_grad * (gate * sigmoid)).astype(bf16)
    grads_ref[:, size:] = up_grad
    second = dot(gate_grad, weight_of(weight_ref, 0, size), ((1,), (1,)))
    second += dot(up_grad, weight_of(weight_ref, size, size), ((1,), (1,)))
    unit = unit_ref[...].astype(f32)
    add_sums(sums_ref, second * unit, second)
    back = norm_back(second, unit, inverse_ref[:, 0:1], gain_ref[...]).astype(bf16)
    back_ref[...] = back
    through = dot(back, output_ref[...], ((1,), (1,))).astype(bf16)
    columns = through_ref.shape[2]
    for i in range(through_ref.shape[0]):
        through_ref[i] = through[:, i * columns : (i + 1) * columns]


def feed_back(gate, upper, down_grad, unit, inverse, gain, output_all, pieces, rows, n_seq):
    length, width = down_grad.shape
    size = gate.shape[1]
    n = len(pieces)
    block = block_of(length)
    half = block_spec(block, size)
    full = block_spec(block, width)
    return call_kernel(
        lambda *refs: feed_back_kernel(n, *refs),
        length,
        [
            half,
            half,
            full,
            full,
            block_spec(block, 128),
            whole_spec(1, width),
            once_spec(width, width),
        ]
        + any_specs(n),
        [
            rows_out(length, 2 * size, bf16),
            rows_out(length, width, bf16),
            (
                jax.ShapeDtypeStruct((n_seq, length, width // n_seq), bf16),
                pl.BlockSpec((n_seq, block, width // n_seq), lambda i: (0, i, 0)),
            ),
            sums_out(width),
        ],
        [
            pltpu.VMEM((pieces[0].shape[0], n, rows, 3 * size), bf16),
            pltpu.SemaphoreType.DMA((n,)),
        ],
        (gate, upper, down_grad, unit, inverse, gain, output_all, *pieces),
        "feed_back",
        6 * length * width * size + 2 * length * width * width,
    )


def first_kernel(n, *refs):
    grad_ref, center_ref, gain_ref, back_ref = refs[:4]
    pieces = refs[4 : 4 + n]
    both_ref, sums_ref, bias_ref, weight_ref, sems = refs[4 + n :]
    load_pieces(pieces, weight_ref, sems)
    grad = grad_ref[...]
    first = dot(grad, weight_of(weight_ref, 0, grad.shape[1]), ((1,), (1,)))
    unit, inverse = unit_of_centered(center_ref[...].astype(f32))
    add_sums(sums_ref, first * unit, first)
    add_sums(bias_ref, grad.astype(f32))
    both = back_ref[...].astype(f32) + norm_back(first, unit, inverse, gain_ref[...])
    both_ref[...] = both.astype(bf16)


def first_back(joint_grad, center, gain, back, pieces, rows):
    length, width = center.shape
    total = joint_grad.shape[1]
    n = len(pieces)
    block = block_of(length)
    full = block_spec(block, width)
    return call_kernel(
        lambda *refs: first_kernel(n, *refs),
        length,
        [block_spec(block, total), full, whole_spec(1, width), full] + any_specs(n),
        [rows_out(length, width, bf16), sums_out(width), sums_out(total)],
        [
            pltpu.VMEM((pieces[0].shape[0], n, rows, total), bf16),
            pltpu.SemaphoreType.DMA((n,)),
        ],
        (joint_grad, center, gain, back, *pieces),
        "first_back",
        2 * length * width * total,
    )


def grad_kernel(rows, has_rest, has_below, *refs):
    left_ref, right_ref = refs[:2]
    refs = refs[2:]
    part = dot(left_ref[...], right_ref[...], ((0,), (0,)))
    if has_rest:
        rest_ref, refs = refs[0], refs[1:]
        local = rest_ref.shape[0]
        first = pl.multiple_of(lax.axis_index("seq") * local, local)
        part += dot(left_ref[pl.ds(first, local), :], rest_ref[...], ((0,), (0,)))
    if has_below:
        below_ref, refs = refs[0], refs[1:]
    keep_ref, send_ref, part_ref = refs
    me = lax.axis_index("batch")
    part_ref[...] = part.astype(bf16).reshape(part_ref.shape)
    for far in range(2):
        for near, ref in enumerate((keep_ref, send_ref)):
            batch_at = me ^ (2 * far + near)
            for i in range(part_ref.shape[0]):
                ref[far, i, :rows] = part_ref[i, batch_at]
                if has_below:
                    ref[far, i, rows:] = below_ref[i, batch_at]


def weight_grad(left, right, n_seq, n_batch, rest=None, below=None):
    length, width = left.shape
    c = right.shape[1]
    rows = width // (n_seq * n_batch)
    if n_seq != 8 or n_batch != 4:
        if rest is not None:
            first = lax.axis_index("seq") * rest.shape[0]
            mine = lax.dynamic_slice_in_dim(right, first, rest.shape[0], 0) + rest
            right = lax.dynamic_update_slice_in_dim(right, mine, first, 0)
        part = dot(left, right, ((0,), (0,))).astype(bf16).reshape(n_seq, n_batch, rows, c)
        if below is not None:
            part = jnp.concatenate([part, below], axis=2)
        return part, None
    args = [left, right]
    many = GRAD_BLOCKS
    specs = [pl.BlockSpec((length, many * width // n_seq), lambda i: (0, i)), once_spec(length, c)]
    high = rows
    if rest is not None:
        args.append(rest)
        specs.append(once_spec(*rest.shape))
    if below is not None:
        high += below.shape[2]
        args.append(below)
        specs.append(pl.BlockSpec((many,) + below.shape[1:], lambda i: (i, 0, 0, 0)))
    shape = jax.ShapeDtypeStruct((2, n_seq, high, c), bf16)
    spec = pl.BlockSpec((2, many, high, c), lambda i: (0, i, 0, 0))
    return pl.pallas_call(
        lambda *refs: grad_kernel(rows, rest is not None, below is not None, *refs),
        grid=(n_seq // many,),
        in_specs=specs,
        out_specs=[spec, spec],
        out_shape=[shape, shape],
        scratch_shapes=[pltpu.VMEM((many, n_batch, rows, c), bf16)],
        compiler_params=pltpu.CompilerParams(
            vmem_limit_bytes=VMEM_BYTES, dimension_semantics=("arbitrary",)
        ),
        cost_estimate=pl.CostEstimate(
            flops=2 * length * width * c,
            bytes_accessed=2 * (length * width + length * c + 2 * width * c),
            transcendentals=0,
        ),
        name="weight_grad",
    )(*args)


def unpack_kernel(blocks_ref, *refs):
    parts, (out_ref, vectors_ref) = refs[:3], refs[3:]
    rows = out_ref.shape[0]
    width = out_ref.shape[1] // 3
    columns = blocks_ref.shape[2] // 3
    place = lax.axis_index("seq") // 2
    total = jnp.zeros(vectors_ref.shape, f32)
    for k in range(4):
        far = place ^ k
        for near in range(2):
            at = far * 2 + near
            block = (blocks_ref[at] if k == 0 else parts[k - 1][near]).astype(f32)
            for i in range(3):
                span = pl.ds(pl.multiple_of(i * width + at * columns, columns), columns)
                out_ref[:, span] = block[:rows, i * columns : (i + 1) * columns]
            total += block[rows : rows + 8]
    vectors_ref[...] = total


def unpack_joint(blocks, parts, rows):
    n_seq, _, total = blocks.shape
    return pl.pallas_call(
        unpack_kernel,
        out_shape=(
            jax.ShapeDtypeStruct((rows, n_seq * total), f32),
            jax.ShapeDtypeStruct((8, total), f32),
        ),
        compiler_params=pltpu.CompilerParams(vmem_limit_bytes=VMEM_BYTES),
        cost_estimate=pl.CostEstimate(
            flops=n_seq * rows * total, bytes_accessed=6 * n_seq * rows * total, transcendentals=0
        ),
        name="unpack_joint",
    )(blocks, *parts)


def grad_near(halves, n_batch):
    keep, send = halves
    if send is None:
        return scatter_near(keep, n_batch), None
    return keep, swap(send, "batch", n_batch, 1)


def grad_far_begin(halves, n_batch):
    keep, got = halves
    if got is None:
        return scatter_far(keep, n_batch), None
    send = (keep[1].astype(f32) + got[1].astype(f32)).astype(bf16)
    return (keep, got), swap(send, "batch", n_batch, 2)


def grad_far_end(state):
    halves, other = state
    if other is None:
        return halves
    keep, got = halves
    return (keep[0].astype(f32) + got[0].astype(f32) + other.astype(f32)).astype(bf16)


def make_body(n_seq, n_batch):
    def body(
        tokens,
        language,
        language_weight,
        output_grad,
        attention_gain,
        attention_shift,
        joint_weight,
        joint_bias,
        output_weight,
        feedfwd_gain,
        feedfwd_shift,
        gate_weight,
        up_weight,
        down_weight,
    ):
        _, local, width = tokens.shape
        rows, ff_width = gate_weight.shape
        length = local * n_seq
        columns = width // n_seq
        tiles = -(-ff_width // (128 * n_seq))
        ff_local = 128 * tiles
        seq_at = lax.axis_index("seq")
        first_row = seq_at * local
        values = tokens[0]
        tables = [jnp.asarray(t) for t in turn_tables(length)]

        center_own = values - mean_of(values)
        ring = Gather(jnp.concatenate([center_own.astype(bf16), output_weight]), n_seq)

        chosen = language[:, None] == jnp.arange(LANGS, dtype=jnp.int32)[None, :]
        row_scale = jnp.sum(jnp.where(chosen, language_weight[None, :], 0.0), axis=1)
        cotangent = output_grad[0] * row_scale[:, None]

        small = jnp.concatenate(
            [attention_gain, attention_shift, feedfwd_gain, feedfwd_shift, joint_bias]
        )
        small = jnp.pad(small[None], ((0, 15), (0, 3 * columns - small.shape[0])))
        blocks = jnp.transpose(joint_weight.reshape(rows, 3, n_seq, columns), (2, 0, 1, 3))
        blocks = blocks.reshape(n_seq, rows, 3 * columns)
        blocks = jnp.concatenate(
            [blocks, jnp.broadcast_to(small[None], (n_seq,) + small.shape)], axis=1
        )
        ff_blocks = [
            jnp.pad(w, ((0, 0), (0, n_seq * ff_local - ff_width))).reshape(rows, tiles, n_seq, 128)
            for w in (gate_weight, up_weight, down_weight)
        ]
        ff_blocks = jnp.transpose(jnp.stack(ff_blocks, 1), (3, 0, 1, 2, 4))
        ff_blocks = ff_blocks.reshape(n_seq, rows, 3 * ff_local)

        ring.step()
        flight = exchange_begin(blocks, n_seq, 1)
        ff_flight = exchange_begin(ff_blocks, n_seq, 4)
        (flight,) = ring.tie(flight)
        blocks = exchange_end(flight, n_seq, 1)
        ring.step()
        flight = exchange_begin(blocks, n_seq, 2)
        flight, ff_flight, down_grad = ring.tie(flight, ff_flight, cotangent.astype(bf16))
        down_grad = lax.all_gather(down_grad, "seq", axis=0, tiled=True)
        blocks = exchange_end(flight, n_seq, 2)
        ff_blocks = rest_of_exchange(exchange_end(ff_flight, n_seq, 4), n_seq)
        ring.step()
        flight = exchange_begin(blocks, n_seq, 4)
        ff_flight = exchange_begin(ff_blocks, n_seq, 1)
        flight, ff_flight = ring.tie(flight, ff_flight)
        blocks = rest_of_exchange(exchange_end(flight, n_seq, 4), n_seq)
        ff_blocks = exchange_end(ff_flight, n_seq, 1)
        ring.step()
        held = gather_far(blocks, n_batch)
        ff_flight = exchange_begin(ff_blocks, n_seq, 2)
        (held_last,) = ring.tie(held[-1][1])
        held[-1] = (held[-1][0], held_last)
        pieces = gather_near(held, n_batch)
        center_pieces = [v for _, v in ring.pieces]
        output_held = jnp.concatenate([v[local:] for v in center_pieces])
        output_held, *pieces = tie(output_held, *pieces)
        output_held = gather_far(output_held, n_batch)

        small = jnp.stack([v[:, rows] for v in pieces], axis=1)
        batch_at = lax.axis_index("batch")
        for bit in bits_of(n_batch):
            flipped = small.reshape(n_seq, -1, 2, bit, small.shape[2])[:, :, ::-1]
            small = jnp.where((batch_at & bit) == 0, small, flipped.reshape(small.shape))
        piece = width // (n_seq * n_batch)

        def small_part(start, size):
            return small[:, :, start : start + size].reshape(1, -1).astype(f32)

        gain_one = small_part(0, piece)
        shift_one = small_part(piece, piece)
        gain_two = small_part(2 * piece, piece)
        shift_two = small_part(3 * piece, piece)
        bias_all = small_part(4 * piece, 3 * piece).reshape(3, n_seq, columns)
        bias = lax.dynamic_slice_in_dim(bias_all, seq_at, 1, 1).reshape(1, 3 * columns)

        low, first_input, center = make_heads(
            center_pieces, gain_one, shift_one, bias, tables, pieces, rows, local
        )
        context, mixed, lse = attend(low)

        mixed, held_last, ff_flight = tie(mixed, output_held[-1][1], ff_flight)
        output_held[-1] = (output_held[-1][0], held_last)
        ring = Gather(mixed, n_seq)
        ring.step()
        held = gather_far(exchange_end(ff_flight, n_seq, 2), n_batch)
        ring.tie()
        ring.step()
        output_pieces = gather_near(output_held, n_batch)
        output_pieces = ring.tie(*output_pieces)
        ring.step()
        ring.tie()
        ring.step()
        (held_last,) = ring.tie(held[-1][1])
        held[-1] = (held[-1][0], held_last)
        ff_pieces = gather_near(held, n_batch)
        mixed_pieces = [v for _, v in ring.pieces]
        if columns % 128:
            mixed_pieces = [join(ring.pieces, n_seq, 1)]
        second_input, unit_two, inverse_two, mixed_all, output_all = make_middle(
            mixed_pieces, output_pieces, center, gain_two, shift_two, n_seq, rows
        )
        output_all = output_all.reshape(width, width)

        gate, upper, hidden, result_part = feed(second_input, ff_pieces, rows)
        middle_grads, back, through, second_sums = feed_back(
            gate,
            upper,
            down_grad,
            unit_two,
            inverse_two,
            gain_two,
            output_all,
            ff_pieces,
            rows,
            n_seq,
        )
        result_sum = lax.psum_scatter(result_part, "seq", scatter_dimension=0, tiled=True)

        def own(array):
            return lax.dynamic_slice_in_dim(array, first_row, local, 0)

        ring = Scatter(lambda at: lax.dynamic_index_in_dim(through, at, 0, False), n_seq)
        ring.step()
        grad_down = weight_grad(down_grad, hidden, n_seq, n_batch)
        (grad_down,) = ring.tie(grad_down)
        ring.step()
        grad_down = grad_near(grad_down, n_batch)
        grad_both = weight_grad(second_input, middle_grads, n_seq, n_batch)
        grad_both, grad_down = ring.tie(grad_both, grad_down)
        ring.step()
        grad_both = grad_near(grad_both, n_batch)
        grad_down = grad_far_begin(grad_down, n_batch)
        grad_output = weight_grad(
            mixed_all, back, n_seq, n_batch, rest=cotangent.astype(bf16)
        )
        grad_both, grad_output, grad_down, result_sum = ring.tie(
            grad_both, grad_output, grad_down, result_sum
        )
        ring.step()
        grad_both = grad_far_begin(grad_both, n_batch)
        grad_output = grad_near(grad_output, n_batch)
        grad_down = exchange_begin(grad_far_end(grad_down), n_seq, 4)
        heads_weight = lax.dynamic_slice_in_dim(output_all, seq_at * columns, columns, 0)
        from_cot = dot(down_grad, heads_weight, ((1,), (1,)))
        from_cot, grad_output = ring.tie(from_cot, grad_output)
        context_grad = (ring.total() + from_cot).astype(bf16)
        joint_grad = attend_back(low, context_grad, context, lse, tables)
        joint_grad, grad_both, grad_down = tie(joint_grad, grad_both, grad_down)
        grad_output = grad_far_begin(grad_output, n_batch)
        grad_both = exchange_begin(grad_far_end(grad_both), n_seq, 4)
        grad_down = rest_of_exchange(exchange_end(grad_down, n_seq, 4), n_seq)
        grad_down = exchange_begin(grad_down, n_seq, 1)
        both, first_sums, bias_sums = first_back(joint_grad, center, gain_one, back, pieces, rows)

        ring = Scatter(lambda at: lax.dynamic_slice_in_dim(both, at * local, local, 0), n_seq)
        ring.step()
        bias_part = lax.dynamic_update_slice_in_dim(
            jnp.zeros((3, n_seq, columns), f32), bias_sums[:1].reshape(3, 1, columns), seq_at, 1
        )
        vectors = [first_sums[0], first_sums[1], second_sums[0], second_sums[1], bias_part]
        vectors = [v.reshape(n_seq, n_batch, 1, -1).astype(bf16) for v in vectors]
        vectors = jnp.concatenate(vectors, axis=3)
        vectors = jnp.pad(vectors, ((0, 0), (0, 0), (0, 15), (0, 3 * columns - 7 * piece)))
        grad_joint = weight_grad(first_input, joint_grad, n_seq, n_batch, below=vectors)
        grad_joint, grad_down, grad_both, grad_output = ring.tie(
            grad_joint, grad_down, grad_both, grad_output
        )
        grad_output = lax.psum_scatter(
            grad_far_end(grad_output), "seq", scatter_dimension=0, tiled=False
        )
        ring.step()
        grad_joint = grad_near(grad_joint, n_batch)
        grad_both = rest_of_exchange(exchange_end(grad_both, n_seq, 4), n_seq)
        grad_both = exchange_begin(grad_both, n_seq, 1)
        (grad_joint,) = ring.tie(grad_joint)
        ring.step()
        grad_joint = grad_far_begin(grad_joint, n_batch)
        grad_down = exchange_begin(exchange_end(grad_down, n_seq, 1), n_seq, 2)
        grad_joint, grad_both, grad_down, result_sum = ring.tie(
            grad_joint, grad_both, grad_down, result_sum
        )
        grad_down = exchange_end(grad_down, n_seq, 2)
        ring.step()
        grad_joint = exchange_begin(grad_far_end(grad_joint), n_seq, 1)
        grad_both = exchange_begin(exchange_end(grad_both, n_seq, 1), n_seq, 2)
        (grad_joint,) = ring.tie(grad_joint)
        grad_joint = exchange_end(grad_joint, n_seq, 1)
        if n_seq == 8:
            parts = exchange_parts(grad_joint)
        grad_both = exchange_end(grad_both, n_seq, 2)
        token_grad = cotangent + ring.total()
        mixed_own = after(own(mixed_all), grad_joint)
        result = values + dot(mixed_own, output_all, ((1,), (0,))) + result_sum.astype(f32)
        grad_output = grad_output.astype(f32)

        def unsplit(grad):
            grad = grad.reshape(n_seq, rows, tiles, 128).astype(f32)
            return jnp.transpose(grad, (1, 2, 0, 3)).reshape(rows, n_seq * ff_local)[:, :ff_width]

        grad_gate = unsplit(grad_both[:, :, :ff_local])
        grad_up = unsplit(grad_both[:, :, ff_local:])
        grad_down = unsplit(grad_down)
        if n_seq == 8:
            done = tie(*parts, grad_gate, grad_up, grad_down, token_grad, result)
            parts, (grad_gate, grad_up, grad_down, token_grad, result) = done[:3], done[3:]
            grad_joint, vectors = unpack_joint(grad_joint, parts, rows)
            vectors = vectors[0]
        else:
            grad_joint = exchange_far(grad_joint, n_seq).astype(f32)
            vectors = jnp.sum(grad_joint[:, rows], axis=0)
            grad_joint = grad_joint[:, :rows].reshape(n_seq, rows, 3, columns)
            grad_joint = jnp.transpose(grad_joint, (1, 2, 0, 3)).reshape(rows, 3 * width)
        return (
            result[None],
            token_grad[None],
            vectors[:piece],
            vectors[piece : 2 * piece],
            grad_joint,
            vectors[4 * piece : 7 * piece],
            grad_output,
            vectors[2 * piece : 3 * piece],
            vectors[3 * piece : 4 * piece],
            grad_gate,
            grad_up,
            grad_down,
        )

    return body


def solution(mesh):
    rows = P(("seq", "batch"))
    matrix = P(("seq", "batch"), None)
    data = P("batch", "seq", None)
    return jax.shard_map(
        make_body(mesh.shape["seq"], mesh.shape["batch"]),
        mesh=mesh,
        in_specs=(
            data,
            P("batch"),
            P(),
            data,
            rows,
            rows,
            matrix,
            rows,
            matrix,
            rows,
            rows,
            matrix,
            matrix,
            matrix,
        ),
        out_specs=(data, data, rows, rows, matrix, rows, matrix, rows, rows, matrix, matrix, matrix),
        check_vma=False,
    )
```
